256 devices in a mesh: ia: 16 (over z, y_lo), ja: 4 (over y_hi, core), ka: 4 (over x).
Axes of the slice: x: 4, y: 4 (y_hi: 2, y_lo: 2; y = y_hi * 2 + y_lo), z: 8, core: 2. Of those that a mesh axis runs over, the one named last changes fastest.
Arguments:
- tensor: float32 [96, 2048, 2048], P('ka', 'ia', 'ja'), may hold values from -6 to 6
- factor_b: float32 [2048, 256], P(('ja', 'ia', 'ka')), as said below
- factor_c: float32 [96, 256], P('ka'), as said below
Outputs:
- hat_a: float32 [2048, 256], P(('ia', 'ja', 'ka'))
- weight_a: float32 [256], replicated
- hat_b: float32 [2048, 256], P(('ja', 'ia', 'ka'))
- weight_b: float32 [256], replicated
The draws below stay inside these ranges and needn't reach their ends.
Inputs may be any that keep to these rules, and one draw needn't show every extreme that they name: `factor_b`: Real-valued factor entries; entries of one row may be correlated. `factor_c`: Real-valued factor entries; entries of one row may be correlated.
All inputs are finite; a program needn't handle non-finite values.
Results may differ from the reference program's by a relative error of at most 0.00018.
Values sent between devices are 32-bit elements; how exact they have to be, the bound alone decides.
A program may use at most 64 MiB of HBM per device.

```python
import math
import jax
import jax.numpy as jnp
from jax import lax

R = 256
I = 2048
J = 2048
K = 96


def factor_values(key, length, rank, scale):
    keys = jax.random.split(key, 5)
    rough = jax.random.normal(keys[0], (length, rank), jnp.float32)
    base = rough
    shared = jax.random.normal(keys[2], (length, 1), jnp.float32)
    mixing = jax.random.uniform(keys[3], (1, rank), jnp.float32, 0.4, 0.9)
    column = jnp.exp(jax.random.uniform(keys[4], (1, rank), jnp.float32, -math.log(2.0), math.log(2.0)))
    ramp = 0.5 + jnp.arange(length, dtype=jnp.float32) / length
    return (base + mixing * shared) * column * ramp[:, None] * scale


def draw_factor_b(key, part):
    key = jax.random.fold_in(key, 11)
    return factor_values(key, J, R, 1.0 / math.sqrt(J))


def draw_factor_c(key, part):
    key = jax.random.fold_in(key, 23)
    return factor_values(key, K, R, 0.3 / math.sqrt(K))


def block_scale(own_key, extent, cuts, low, high):
    def one(position, blocks):
        steps = jax.random.uniform(jax.random.fold_in(jax.random.fold_in(own_key, 6), position), (blocks,), jnp.float32, low / len(cuts), high / len(cuts))
        return jnp.repeat(jnp.exp(steps), extent[position] // blocks).reshape((-1,) + (1,) * (len(extent) - position - 1))

    gain = one(*cuts[0])
    for cut in cuts[1:]:
        gain = gain * one(*cut)
    return gain


def noise(own_key, extent, scale, bound, cuts=(), kind=jnp.bfloat16):
    values = scale * jax.random.normal(own_key, extent, jnp.float32)
    if cuts:
        values = values * block_scale(own_key, extent, cuts, -0.22, 0.18)
    return jnp.clip(values, -bound, bound).astype(kind)


def setup_inputs(seed: int = 0) -> dict:
    key_of = jax.random.split(jax.random.key(seed), 4)
    tensor = noise(key_of[0], (K, I, J), 1.0, 6.0, ((0, 4), (1, 16), (2, 4)), jnp.float32)
    factor_b = draw_factor_b(jax.random.fold_in(key_of[3], 71), 0)
    factor_c = draw_factor_c(jax.random.fold_in(key_of[3], 71), 0)
    return {"tensor": tensor, "factor_b": factor_b, "factor_c": factor_c}


ridge_term = 0.01
epsilon = 1e-06

def solve_rows(system, right):
    lower = jnp.linalg.cholesky(system)
    return jax.scipy.linalg.cho_solve((lower, True), right.T).T

def scaled(raw_factor):
    weight = jnp.sqrt(lax.optimization_barrier(jnp.mean(raw_factor * raw_factor, axis=0)) + epsilon)
    return (raw_factor / weight, weight)

def reference(tensor, factor_b, factor_c):
    high = lax.Precision.HIGHEST
    rank = factor_c.shape[1]
    identity = jnp.eye(rank, dtype=jnp.float32)
    gram_b = jnp.dot(factor_b.T.astype(jnp.float32), factor_b.astype(jnp.float32), precision=high, preferred_element_type=jnp.float32)
    gram_c = jnp.dot(factor_c.T.astype(jnp.float32), factor_c.astype(jnp.float32), precision=high, preferred_element_type=jnp.float32)
    along_j = jnp.einsum('kij,jr->kir', tensor, factor_b, precision=high)
    mttkrp_a = lax.optimization_barrier(jnp.sum(along_j * factor_c[:, None, :], axis=0))
    raw_a = solve_rows(gram_b * gram_c + ridge_term * identity, mttkrp_a)
    hat_a, weight_a = scaled(raw_a)
    gram_a = jnp.dot(hat_a.T.astype(jnp.float32), hat_a.astype(jnp.float32), precision=high, preferred_element_type=jnp.float32)
    along_i = jnp.einsum('kij,ir->kjr', tensor, hat_a, precision=high)
    mttkrp_b = lax.optimization_barrier(jnp.sum(along_i * factor_c[:, None, :], axis=0))
    raw_b = solve_rows(gram_a * gram_c + ridge_term * identity, mttkrp_b)
    hat_b, weight_b = scaled(raw_b)
    return (hat_a, weight_a, hat_b, weight_b)
```

```python
import functools

import jax
import jax.numpy as jnp
from jax import lax
from jax.experimental import pallas as pl
from jax.experimental.pallas import tpu as pltpu
from jax.sharding import PartitionSpec as P

ridge_term = 0.01
epsilon = 1e-06

MESH = pl.DeviceIdType.MESH
HIGH = lax.Precision.HIGHEST
F32 = jnp.float32
BF16 = jnp.bfloat16
NB = 16
TN = (((0,), (0,)), ((), ()))


def split2(x):
    hi = x.astype(BF16)
    return hi, (x - hi.astype(F32)).astype(BF16)


def split3(x):
    hi = x.astype(BF16)
    rest = x - hi.astype(F32)
    mid = rest.astype(BF16)
    return hi, mid, (rest - mid.astype(F32)).astype(BF16)


def sweep_panels(a_ref, first, last):
    rank = a_ref.shape[0]
    lane = lax.broadcasted_iota(jnp.int32, (NB, rank), 1)
    row = lax.broadcasted_iota(jnp.int32, (NB, rank), 0)
    row1 = lax.broadcasted_iota(jnp.int32, (NB, 128), 0)
    lane_all = lax.broadcasted_iota(jnp.int32, (rank, rank), 1)

    def wide(v):
        return jnp.concatenate([v] * (rank // 128), axis=1)

    def panel(b, carry):
        r0 = pl.multiple_of(b * NB, NB)
        r = a_ref[pl.ds(r0, NB), :]
        base = pl.multiple_of(lax.div(r0, 128) * 128, 128)
        half = a_ref[pl.ds(r0, NB), pl.ds(base, 128)]
        d = pltpu.roll(half, lax.rem(128 - (r0 - base), 128), 1)
        cols = [jnp.broadcast_to(d[:, j : j + 1], (NB, 128)) for j in range(NB)]
        inside = (lane >= r0) & (lane < r0 + NB)
        rz = jnp.where(inside, 0.0, r)
        q = jnp.where(inside, jnp.where(lane - r0 == row, -1.0, 0.0), r)
        for p in range(0, NB, 2):
            cp, cq = cols[p], cols[p + 1]
            a, b1, e = cp[p : p + 1], cp[p + 1 : p + 2], cq[p + 1 : p + 2]
            inv = 1.0 / (a * e - b1 * b1)
            fa, fb, fe = a * inv, b1 * inv, e * inv

            def apply(y, ma, mb, me, mp, mq, rows):
                yp, yq = y[p : p + 1], y[p + 1 : p + 2]
                np_ = me * yp - mb * yq
                nq_ = ma * yq - mb * yp
                new = y - mp * np_ - mq * nq_
                return jnp.where(rows == p, np_, jnp.where(rows == p + 1, nq_, new))

            for j in range(p + 2, NB):
                cols[j] = apply(cols[j], fa, fb, fe, cp, cq, row1)
            q = apply(q, wide(fa), wide(fb), wide(fe), wide(cp), wide(cq), row)
        r1, r2, r3 = split3(rz)
        q1, q2, q3 = split3(q)
        left = jnp.concatenate([r1, r1, r2, r2, r1, r3], axis=0)
        right = jnp.concatenate([q1, q2, q1, q2, q3, q1], axis=0)
        update = lax.dot_general(left, right, TN, preferred_element_type=F32)
        a_ref[...] = jnp.where((lane_all >= r0) & (lane_all < r0 + NB), 0.0, a_ref[...]) - update
        a_ref[pl.ds(r0, NB), :] = q
        return carry

    lax.fori_loop(first, last, panel, 0)


def diagonal(matrix):
    rank = matrix.shape[0]
    eye = lax.broadcasted_iota(jnp.int32, (rank, rank), 0) == lax.broadcasted_iota(jnp.int32, (rank, rank), 1)
    kept = jnp.where(eye, matrix, 0.0)
    return jnp.sum(kept, axis=0, keepdims=True), jnp.sum(kept, axis=1, keepdims=True)


def scale_system(a_ref, product):
    rank = product.shape[0]
    eye = lax.broadcasted_iota(jnp.int32, (rank, rank), 0) == lax.broadcasted_iota(jnp.int32, (rank, rank), 1)
    system = product + jnp.where(eye, ridge_term, 0.0)
    along, down = diagonal(system)
    along, down = lax.rsqrt(along), lax.rsqrt(down)
    a_ref[...] = system * down * along
    return along


def kernel(
    n_x, n_z, total_a, total_b,
    t_hbm, b_ref, c_ref,
    hat_a_ref, w_a_ref, hat_b_ref, w_b_ref,
    t_f32, t_hi, t_lo, bz, bfull, bst, call, pb, pbc, hs, pby, gb, gc, ma, ra, pa, pg, gz, gs, ga, sysm, scl, iw,
    mbt, mb, rb1, mb1, rb2, sq, sqp, sqs, sqz,
    t_sem, send_sem, recv_sem,
):
    depth, height, width = t_f32.shape
    rank = c_ref.shape[1]
    ia, ja, ka = lax.axis_index("ia"), lax.axis_index("ja"), lax.axis_index("ka")
    z, yl = lax.div(ia, 2), lax.rem(ia, 2)
    yh, core = lax.div(ja, 2), lax.rem(ja, 2)
    n_s = 4 * n_x
    n_q = 2 * n_s
    n_g = 2 * n_x
    s = ja * n_x + ka
    q = yl * n_s + s
    g = yl * n_x + ka

    def plane_peer(d):
        yl2 = lax.rem(yl + lax.div(d, n_s), 2)
        ja2 = lax.rem(ja + lax.rem(lax.div(d, n_x), 4), 4)
        ka2 = lax.rem(ka + lax.rem(d, n_x), n_x)
        return yl2 * n_s + ja2 * n_x + ka2, (z * 2 + yl2, ja2, ka2)

    def group_peer(d):
        yl2 = lax.rem(yl + lax.div(d, n_x), 2)
        ka2 = lax.rem(ka + lax.rem(d, n_x), n_x)
        return yl2 * n_x + ka2, (z * 2 + yl2, ja, ka2)

    def share_peer(d):
        ja2 = lax.rem(ja + lax.div(d, n_x), 4)
        ka2 = lax.rem(ka + lax.rem(d, n_x), n_x)
        return ja2 * n_x + ka2, (ia, ja2, ka2)

    def z_peer(d):
        z2 = lax.rem(z + d, n_z)
        return z2, (z2 * 2 + yl, ja, ka)

    def x_peer(d):
        ka2 = lax.rem(ka + d, n_x)
        return ka2, (ia, ja, ka2)

    def send(stage, src, dst, device):
        pltpu.make_async_remote_copy(
            src_ref=src, dst_ref=dst, send_sem=send_sem.at[stage], recv_sem=recv_sem.at[stage],
            device_id=device, device_id_type=MESH,
        ).start()

    def fan(stage, count, peer, src, dst):
        def body(d, carry):
            where, device = peer(d)
            send(stage, src(where), dst, device)
            return carry

        lax.fori_loop(1, count, body, 0)

    def arrived(stage, ref):
        pltpu.make_async_copy(ref, ref, recv_sem.at[stage]).wait()

    def sent(stage, ref):
        pltpu.make_async_copy(ref, ref, send_sem.at[stage]).wait()

    n_chunk = t_sem.shape[0]
    per = depth // n_chunk
    loads = [
        pltpu.make_async_copy(t_hbm.at[pl.ds(i * per, per)], t_f32.at[pl.ds(i * per, per)], t_sem.at[i])
        for i in range(n_chunk)
    ]
    for load in loads:
        load.start()

    barrier = pltpu.get_barrier_semaphore()

    def greet(peer):
        def body(d, carry):
            pl.semaphore_signal(barrier, inc=1, device_id=peer(d)[1], device_id_type=MESH)
            return carry

        return body

    lax.fori_loop(1, n_z, greet(z_peer), 0)
    lax.fori_loop(1, n_q, greet(plane_peer), 0)
    pl.semaphore_wait(barrier, n_q + n_z - 2)

    fan(0, n_z, z_peer, lambda _: b_ref, bz.at[z])
    fan(1, n_x, x_peer, lambda _: c_ref, call.at[ka])
    bz[z] = b_ref[...]
    call[ka] = c_ref[...]

    def cut(first, last):
        def body(k, carry):
            hi, lo = split2(t_f32[k])
            t_hi[k] = hi
            t_lo[k] = lo
            return carry

        lax.fori_loop(first, last, body, 0)

    early = n_chunk // 2
    for i in range(early):
        loads[i].wait()
        cut(i * per, (i + 1) * per)
    arrived(0, bz.at[pl.ds(0, n_z - 1)])
    fan(2, n_g, group_peer, lambda _: bz, bfull.at[:, g])
    bfull[:, g] = bz[...]
    for i in range(early, n_chunk):
        loads[i].wait()
        cut(i * per, (i + 1) * per)
    if n_x > 1:
        arrived(1, call.at[pl.ds(0, n_x - 1)])
    call_rows = call[...].reshape(n_x * depth, rank)
    gc[...] = lax.dot_general(call_rows, call_rows, TN, precision=HIGH, preferred_element_type=F32)

    arrived(2, bfull.at[:, pl.ds(0, n_g - 1)])
    rows_b = bfull[...].reshape(width, rank)
    pb[...] = lax.dot_general(rows_b, rows_b, TN, precision=HIGH, preferred_element_type=F32).reshape(pb.shape)
    sibling = (ia, ja + 1 - 2 * core, ka)
    across = (z * 2 + 1 - yl, ja + 2 - 4 * yh, ka)
    send(3, pb.at[1 - core], pbc, sibling)
    hi, lo = split2(rows_b)
    bst[...] = jnp.concatenate([hi, lo, hi], axis=0)
    ma[...] = jnp.zeros_like(ma)

    def first_mode(i, carry):
        k0 = i * per
        th = t_hi[pl.ds(k0, per)].reshape(per * height, width)
        tl = t_lo[pl.ds(k0, per)].reshape(per * height, width)
        along = jnp.dot(jnp.concatenate([th, th, tl], axis=1), bst[...], preferred_element_type=F32)
        total = ma[...].reshape(height, rank)
        for j in range(per):
            total = total + along[j * height : (j + 1) * height] * c_ref[pl.ds(k0 + j, 1), :]
        ma[...] = total.reshape(ma.shape)
        return carry

    lax.fori_loop(0, early, first_mode, 0)
    arrived(3, pbc)
    hs[...] = pb[core] + pbc[...]
    send(4, hs, pby, across)
    lax.fori_loop(early, n_chunk, first_mode, 0)
    fan(5, n_s, share_peer, lambda where: ma.at[where], ra.at[s])
    ra[s] = ma[s]
    arrived(4, pby)
    gb[core] = hs[...] + pby[...]
    send(6, gb.at[core], gb.at[core], sibling)
    arrived(6, gb.at[0])

    scl[...] = scale_system(sysm, gb[...].reshape(rank, rank) * gc[...])
    sweep_panels(sysm, 0, rank // NB)
    arrived(5, ra.at[pl.ds(0, n_s - 1)])
    share_a = jnp.sum(ra[...], axis=0)
    raw_a = -jnp.dot(share_a * scl[...], sysm[...], precision=HIGH, preferred_element_type=F32) * scl[...]

    pa[q] = raw_a
    fan(7, n_q, plane_peer, lambda _: pa.at[q], pa.at[q])
    arrived(7, pa.at[pl.ds(0, n_q - 1)])
    rows_a = pa[...].reshape(n_q * 8, rank)
    pg[...] = lax.dot_general(rows_a, rows_a, TN, precision=HIGH, preferred_element_type=F32).reshape(pg.shape)
    fan(8, n_z, z_peer, lambda _: pg.at[q], gz.at[z])
    gz[z] = pg[q]
    mbt[...] = jnp.zeros_like(mbt)

    def second_mode(i, carry):
        k0 = i * per
        rows = pa[pl.ds(yl * n_s, n_s)].reshape(height, rank)
        both = jnp.concatenate([rows * c_ref[pl.ds(k0 + j, 1), :] for j in range(per)], axis=0)
        hi, lo = split2(both)
        th = t_hi[pl.ds(k0, per)].reshape(per * height, width)
        tl = t_lo[pl.ds(k0, per)].reshape(per * height, width)
        mbt[...] += lax.dot_general(
            jnp.concatenate([hi, lo, hi], axis=0), jnp.concatenate([th, th, tl], axis=0), TN,
            preferred_element_type=F32,
        )
        return carry

    lax.fori_loop(0, early, second_mode, 0)
    arrived(8, gz.at[pl.ds(0, n_z - 1)])
    gs[...] = jnp.sum(gz[...], axis=0)
    fan(9, n_q, plane_peer, lambda _: gs, ga.at[q])
    ga[q] = gs[...]
    lax.fori_loop(early, n_chunk, second_mode, 0)
    mb[...] = mbt[...].T.reshape(mb.shape)
    fan(10, n_g, group_peer, lambda where: mb.at[:, where], rb1.at[g])
    rb1[g] = mb[:, g]

    arrived(9, ga.at[pl.ds(0, n_q - 1)])
    gram = ga[...].reshape(rank, rank)
    along, down = diagonal(gram)
    weight_a = jnp.sqrt(along * (1.0 / total_a) + epsilon)
    iw[...] = 1.0 / weight_a
    w_a_ref[...] = weight_a
    hat_a_ref[...] = pa[q] / weight_a
    down = 1.0 / jnp.sqrt(down * (1.0 / total_a) + epsilon)
    scl[...] = scale_system(sysm, gram * down * iw[...] * gc[...])
    middle = rank // NB // 2
    sweep_panels(sysm, 0, middle)
    arrived(10, rb1.at[pl.ds(0, n_g - 1)])
    mb1[...] = jnp.sum(rb1[...], axis=0)
    fan(11, n_z, z_peer, lambda where: mb1.at[where], rb2.at[z])
    rb2[z] = mb1[z]
    sweep_panels(sysm, middle, rank // NB)
    arrived(11, rb2.at[pl.ds(0, n_z - 1)])
    share_b = jnp.sum(rb2[...], axis=0)
    raw_b = -jnp.dot(share_b * iw[...] * scl[...], sysm[...], precision=HIGH, preferred_element_type=F32) * scl[...]

    sq[...] = jnp.sum(raw_b * raw_b, axis=0, keepdims=True)
    fan(12, n_q, plane_peer, lambda _: sq, sqp.at[q])
    sqp[q] = sq[...]
    arrived(12, sqp.at[pl.ds(0, n_q - 1)])
    sqs[...] = jnp.sum(sqp[...], axis=0)
    fan(13, n_z, z_peer, lambda _: sqs, sqz.at[z])
    sqz[z] = sqs[...]
    arrived(13, sqz.at[pl.ds(0, n_z - 1)])
    weight_b = jnp.sqrt(jnp.sum(sqz[...], axis=0) * (1.0 / total_b) + epsilon)
    w_b_ref[...] = weight_b
    hat_b_ref[...] = raw_b / weight_b

    sent(0, bz.at[pl.ds(0, n_z - 1)])
    if n_x > 1:
        sent(1, call.at[pl.ds(0, n_x - 1)])
    sent(2, bfull.at[:, pl.ds(0, n_g - 1)])
    sent(3, pbc)
    sent(4, pby)
    sent(5, ra.at[pl.ds(0, n_s - 1)])
    sent(6, gb.at[0])
    sent(7, pa.at[pl.ds(0, n_q - 1)])
    sent(8, gz.at[pl.ds(0, n_z - 1)])
    sent(9, ga.at[pl.ds(0, n_q - 1)])
    sent(10, rb1.at[pl.ds(0, n_g - 1)])
    sent(11, rb2.at[pl.ds(0, n_z - 1)])
    sent(12, sqp.at[pl.ds(0, n_q - 1)])
    sent(13, sqz.at[pl.ds(0, n_z - 1)])


def local(tensor, factor_b, factor_c):
    depth, height, width = tensor.shape
    rank = factor_c.shape[1]
    n_x, n_z = lax.axis_size("ka"), lax.axis_size("ia") // 2
    n_s, n_q, n_g = 4 * n_x, 8 * n_x, 2 * n_x
    part = rank // n_q
    n_chunk = 6
    v = pltpu.VMEM
    out = jax.ShapeDtypeStruct
    vmem = pl.BlockSpec(memory_space=pltpu.VMEM)
    hat_a, weight_a, hat_b, weight_b = pl.pallas_call(
        functools.partial(kernel, n_x, n_z, height * lax.axis_size("ia"), width * lax.axis_size("ja")),
        out_shape=[out((8, rank), F32), out((1, rank), F32), out((8, rank), F32), out((1, rank), F32)],
        in_specs=[pl.BlockSpec(memory_space=pl.ANY), vmem, vmem],
        out_specs=[vmem] * 4,
        scratch_shapes=[
            v((depth, height, width), F32),
            v((depth, height, width), BF16),
            v((depth, height, width), BF16),
            v((n_z, 8, rank), F32),
            v((n_z, n_g, 8, rank), F32),
            v((3 * width, rank), BF16),
            v((n_x, depth, rank), F32),
            v((2, rank // 2, rank), F32),
            v((rank // 2, rank), F32),
            v((rank // 2, rank), F32),
            v((rank // 2, rank), F32),
            v((2, rank // 2, rank), F32),
            v((rank, rank), F32),
            v((n_s, 8, rank), F32),
            v((n_s, 8, rank), F32),
            v((n_q, 8, rank), F32),
            v((n_q, part, rank), F32),
            v((n_z, part, rank), F32),
            v((part, rank), F32),
            v((n_q, part, rank), F32),
            v((rank, rank), F32),
            v((1, rank), F32),
            v((1, rank), F32),
            v((rank, width), F32),
            v((n_z, n_g, 8, rank), F32),
            v((n_g, n_z, 8, rank), F32),
            v((n_z, 8, rank), F32),
            v((n_z, 8, rank), F32),
            v((1, rank), F32),
            v((n_q, 1, rank), F32),
            v((1, rank), F32),
            v((n_z, 1, rank), F32),
            pltpu.SemaphoreType.DMA((n_chunk,)),
            pltpu.SemaphoreType.DMA((14,)),
            pltpu.SemaphoreType.DMA((14,)),
        ],
        compiler_params=pltpu.CompilerParams(
            collective_id=0, has_side_effects=True, vmem_limit_bytes=40 * 1024 * 1024
        ),
    )(tensor, factor_b, factor_c)
    return hat_a, weight_a.reshape(rank), hat_b, weight_b.reshape(rank)


def solution(mesh):
    return jax.shard_map(
        local,
        mesh=mesh,
        in_specs=(P("ka", "ia", "ja"), P(("ja", "ia", "ka"), None), P("ka", None)),
        out_specs=(P(("ia", "ja", "ka"), None), P(), P(("ja", "ia", "ka"), None), P()),
        check_vma=False,
    )
```

```python
import functools

import jax
import jax.numpy as jnp
from jax import lax
from jax.experimental import pallas as pl
from jax.experimental.pallas import tpu as pltpu
from jax.sharding import PartitionSpec as P

ridge_term = 0.01
epsilon = 1e-06

MESH = pl.DeviceIdType.MESH
HIGH = lax.Precision.HIGHEST
F32 = jnp.float32
BF16 = jnp.bfloat16
VMEM_LIMIT = 65000000
NB = 32
TN = (((0,), (0,)), ((), ()))


def split2(x):
    hi = x.astype(BF16)
    return hi, (x - hi.astype(F32)).astype(BF16)


def split3(x):
    hi = x.astype(BF16)
    rest = x - hi.astype(F32)
    mid = rest.astype(BF16)
    return hi, mid, (rest - mid.astype(F32)).astype(BF16)


def every(v):
    return jnp.broadcast_to(v, (8, 128))


def inverse8(e):
    get = lambda i, j: e[min(i, j)][max(i, j)]
    for p in range(0, 8, 2):
        a, b, c = e[p][p], e[p][p + 1], e[p + 1][p + 1]
        det = a * c - b * b
        inv = pl.reciprocal(det, approx=True)
        inv = inv * (2.0 - det * inv)
        inv = inv * (2.0 - det * inv)
        fa, fb, fc = a * inv, b * inv, c * inv
        others = [i for i in range(8) if i not in (p, p + 1)]
        old = {i: (get(i, p), get(i, p + 1)) for i in others}
        new = {i: (fc * old[i][0] - fb * old[i][1], fa * old[i][1] - fb * old[i][0]) for i in others}
        for i in others:
            for j in others:
                if i <= j:
                    e[i][j] = e[i][j] - new[i][0] * old[j][0] - new[i][1] * old[j][1]
        for i in others:
            e[min(i, p)][max(i, p)], e[min(i, p + 1)][max(i, p + 1)] = new[i]
        e[p][p], e[p][p + 1], e[p + 1][p + 1] = -fc, fb, -fa
    return e


def sum_of(terms):
    while len(terms) > 1:
        terms = [sum(terms[i : i + 2][1:], terms[i]) for i in range(0, len(terms), 2)]
    return terms[0]


def sweep_panels(a_ref, first, last):
    rank = a_ref.shape[0]
    parts = rank // 128
    lane = lax.broadcasted_iota(jnp.int32, (NB, rank), 1)
    row = lax.broadcasted_iota(jnp.int32, (NB, rank), 0)
    row8 = lax.broadcasted_iota(jnp.int32, (8, 128), 0)
    lane_all = lax.broadcasted_iota(jnp.int32, (rank, rank), 1)
    groups = NB // 8

    def panel(b, carry):
        r0 = pl.multiple_of(b * NB, NB)
        r = a_ref[pl.ds(r0, NB), :]
        base = pl.multiple_of(lax.div(r0, 128) * 128, 128)
        half = a_ref[pl.ds(r0, NB), pl.ds(base, 128)]
        d = pltpu.roll(half, lax.rem(128 - (r0 - base), 128), 1)
        inside = (lane >= r0) & (lane < r0 + NB)
        rz = jnp.where(inside, 0.0, r)
        start = jnp.where(inside, jnp.where(lane - r0 == row, -1.0, 0.0), r)
        x = [
            [d[8 * m : 8 * m + 8]] + [start[8 * m : 8 * m + 8, 128 * h : 128 * h + 128] for h in range(parts)]
            for m in range(groups)
        ]
        for i in range(groups):
            cols = [every(x[i][0][:, 8 * i + j : 8 * i + j + 1]) for j in range(8)]
            e = [[every(cols[j][k : k + 1]) if k <= j else None for j in range(8)] for k in range(8)]
            e = inverse8(e)
            weights = []
            for j in range(8):
                w = e[0][j]
                for k in range(1, 8):
                    w = jnp.where(row8 == k, e[min(k, j)][max(k, j)], w)
                weights.append(w)
            x[i] = [-sum_of([weights[j] * every(y[j : j + 1]) for j in range(8)]) for y in x[i]]
            spread = [[every(y[j : j + 1]) for j in range(8)] for y in x[i]]
            for m in range(groups):
                if m != i:
                    left = [every(x[m][0][:, 8 * i + j : 8 * i + j + 1]) for j in range(8)]
                    x[m] = [y - sum_of([left[j] * s[j] for j in range(8)]) for y, s in zip(x[m], spread)]
        q = jnp.concatenate([jnp.concatenate(x[m][1:], axis=1) for m in range(groups)], axis=0)
        r1, r2, r3 = split3(rz)
        q1, q2, q3 = split3(q)
        left = jnp.concatenate([r1, r1, r2, r2, r1, r3], axis=0)
        right = jnp.concatenate([q1, q2, q1, q2, q3, q1], axis=0)
        update = lax.dot_general(left, right, TN, preferred_element_type=F32)
        a_ref[...] = jnp.where((lane_all >= r0) & (lane_all < r0 + NB), 0.0, a_ref[...]) - update
        a_ref[pl.ds(r0, NB), :] = q
        return carry

    lax.fori_loop(first, last, panel, 0)


def diagonal(matrix):
    rank = matrix.shape[0]
    eye = lax.broadcasted_iota(jnp.int32, (rank, rank), 0) == lax.broadcasted_iota(jnp.int32, (rank, rank), 1)
    kept = jnp.where(eye, matrix, 0.0)
    return jnp.sum(kept, axis=0, keepdims=True), jnp.sum(kept, axis=1, keepdims=True)


def scale_system(a_ref, product):
    rank = product.shape[0]
    eye = lax.broadcasted_iota(jnp.int32, (rank, rank), 0) == lax.broadcasted_iota(jnp.int32, (rank, rank), 1)
    system = product + jnp.where(eye, ridge_term, 0.0)
    along, down = diagonal(system)
    along, down = lax.rsqrt(along), lax.rsqrt(down)
    a_ref[...] = system * down * along
    return along


def kernel(
    n_x, n_z, total_a, total_b,
    t_hbm, b_hbm, c_hbm,
    hat_a_hbm, w_a_hbm, hat_b_hbm, w_b_hbm,
    hat_a_ref, w_a_ref, hat_b_ref, w_b_ref, b_ref, c_ref, t_f32, t_hi, t_lo, bz, bfull, bst, call, pb, pbc, hs, pby, gb, gc, ma, ra, pa, pg, gz, gs, ga, sysm, scl, iw,
    mbt, mb, rb1, mb1, rb2, sq, sqp, sqs, sqz,
    t_sem, out_sem, send_sem, recv_sem,
):
    depth, height, width = t_f32.shape
    rank = c_ref.shape[1]
    ia, ja, ka = lax.axis_index("ia"), lax.axis_index("ja"), lax.axis_index("ka")
    z, yl = lax.div(ia, 2), lax.rem(ia, 2)
    yh, core = lax.div(ja, 2), lax.rem(ja, 2)
    n_s = 4 * n_x
    n_q = 2 * n_s
    n_g = 2 * n_x
    s = ja * n_x + ka
    q = yl * n_s + s
    g = yl * n_x + ka

    def plane_peer(d):
        yl2 = lax.rem(yl + lax.div(d, n_s), 2)
        ja2 = lax.rem(ja + lax.rem(lax.div(d, n_x), 4), 4)
        ka2 = lax.rem(ka + lax.rem(d, n_x), n_x)
        return yl2 * n_s + ja2 * n_x + ka2, (z * 2 + yl2, ja2, ka2)

    def group_peer(d):
        yl2 = lax.rem(yl + lax.div(d, n_x), 2)
        ka2 = lax.rem(ka + lax.rem(d, n_x), n_x)
        return yl2 * n_x + ka2, (z * 2 + yl2, ja, ka2)

    def share_peer(d):
        ja2 = lax.rem(ja + lax.div(d, n_x), 4)
        ka2 = lax.rem(ka + lax.rem(d, n_x), n_x)
        return ja2 * n_x + ka2, (ia, ja2, ka2)

    def z_peer(d):
        z2 = lax.rem(z + d, n_z)
        return z2, (z2 * 2 + yl, ja, ka)

    def x_peer(d):
        ka2 = lax.rem(ka + d, n_x)
        return ka2, (ia, ja, ka2)

    def send(stage, src, dst, device):
        pltpu.make_async_remote_copy(
            src_ref=src, dst_ref=dst, send_sem=send_sem.at[stage], recv_sem=recv_sem.at[stage],
            device_id=device, device_id_type=MESH,
        ).start()

    def fan(stage, count, peer, src, dst):
        def body(d, carry):
            where, device = peer(d)
            send(stage, src(where), dst, device)
            return carry

        lax.fori_loop(1, count, body, 0)

    def arrived(stage, ref):
        pltpu.make_async_copy(ref, ref, recv_sem.at[stage]).wait()

    def sent(stage, ref):
        pltpu.make_async_copy(ref, ref, send_sem.at[stage]).wait()

    n_chunk = t_sem.shape[0] - 2
    per = depth // n_chunk
    loads = [
        pltpu.make_async_copy(t_hbm.at[pl.ds(i * per, per)], t_f32.at[pl.ds(i * per, per)], t_sem.at[i])
        for i in range(n_chunk)
    ]
    small = [pltpu.make_async_copy(b_hbm, b_ref, t_sem.at[n_chunk]), pltpu.make_async_copy(c_hbm, c_ref, t_sem.at[n_chunk + 1])]
    for load in small + loads:
        load.start()

    barrier = pltpu.get_barrier_semaphore()

    def greet(peer):
        def body(d, carry):
            pl.semaphore_signal(barrier, inc=1, device_id=peer(d)[1], device_id_type=MESH)
            return carry

        return body

    lax.fori_loop(1, n_z, greet(z_peer), 0)
    lax.fori_loop(1, n_q, greet(plane_peer), 0)
    pl.semaphore_wait(barrier, n_q + n_z - 2)

    for load in small:
        load.wait()
    fan(0, n_z, z_peer, lambda _: b_ref, bz.at[z])
    fan(1, n_x, x_peer, lambda _: c_ref, call.at[ka])
    bz[z] = b_ref[...]
    call[ka] = c_ref[...]

    def cut(first, last):
        def body(k, carry):
            hi, lo = split2(t_f32[k])
            t_hi[k] = hi
            t_lo[k] = lo
            return carry

        lax.fori_loop(first, last, body, 0)

    early = n_chunk // 2
    for i in range(early):
        loads[i].wait()
        cut(i * per, (i + 1) * per)
    arrived(0, bz.at[pl.ds(0, n_z - 1)])
    fan(2, n_g, group_peer, lambda _: bz, bfull.at[:, g])
    bfull[:, g] = bz[...]
    for i in range(early, n_chunk):
        loads[i].wait()
        cut(i * per, (i + 1) * per)
    if n_x > 1:
        arrived(1, call.at[pl.ds(0, n_x - 1)])
    call_rows = call[...].reshape(n_x * depth, rank)
    gc[...] = lax.dot_general(call_rows, call_rows, TN, precision=HIGH, preferred_element_type=F32)

    arrived(2, bfull.at[:, pl.ds(0, n_g - 1)])
    rows_b = bfull[...].reshape(width, rank)
    pb[...] = lax.dot_general(rows_b, rows_b, TN, precision=HIGH, preferred_element_type=F32).reshape(pb.shape)
    sibling = (ia, ja + 1 - 2 * core, ka)
    across = (z * 2 + 1 - yl, ja + 2 - 4 * yh, ka)
    send(3, pb.at[1 - core], pbc, sibling)
    hi, lo = split2(rows_b)
    bst[...] = jnp.concatenate([hi, lo, hi], axis=0)
    ma[...] = jnp.zeros_like(ma)

    def first_mode(i, carry):
        k0 = i * per
        th = t_hi[pl.ds(k0, per)].reshape(per * height, width)
        tl = t_lo[pl.ds(k0, per)].reshape(per * height, width)
        along = jnp.dot(jnp.concatenate([th, th, tl], axis=1), bst[...], preferred_element_type=F32)
        total = ma[...].reshape(height, rank)
        for j in range(per):
            total = total + along[j * height : (j + 1) * height] * c_ref[pl.ds(k0 + j, 1), :]
        ma[...] = total.reshape(ma.shape)
        return carry

    lax.fori_loop(0, early, first_mode, 0)
    arrived(3, pbc)
    hs[...] = pb[core] + pbc[...]
    send(4, hs, pby, across)
    lax.fori_loop(early, n_chunk, first_mode, 0)
    fan(5, n_s, share_peer, lambda where: ma.at[where], ra.at[s])
    ra[s] = ma[s]
    arrived(4, pby)
    gb[core] = hs[...] + pby[...]
    send(6, gb.at[core], gb.at[core], sibling)
    arrived(6, gb.at[0])

    scl[...] = scale_system(sysm, gb[...].reshape(rank, rank) * gc[...])
    sweep_panels(sysm, 0, rank // NB)
    arrived(5, ra.at[pl.ds(0, n_s - 1)])
    share_a = jnp.sum(ra[...], axis=0)
    raw_a = -jnp.dot(share_a * scl[...], sysm[...], precision=HIGH, preferred_element_type=F32) * scl[...]

    pa[q] = raw_a
    fan(7, n_q, plane_peer, lambda _: pa.at[q], pa.at[q])
    arrived(7, pa.at[pl.ds(0, n_q - 1)])
    rows_a = pa[...].reshape(n_q * 8, rank)
    pg[...] = lax.dot_general(rows_a, rows_a, TN, precision=HIGH, preferred_element_type=F32).reshape(pg.shape)
    fan(8, n_z, z_peer, lambda _: pg.at[q], gz.at[z])
    gz[z] = pg[q]
    mbt[...] = jnp.zeros_like(mbt)

    def second_mode(i, carry):
        k0 = i * per
        rows = pa[pl.ds(yl * n_s, n_s)].reshape(height, rank)
        both = jnp.concatenate([rows * c_ref[pl.ds(k0 + j, 1), :] for j in range(per)], axis=0)
        hi, lo = split2(both)
        th = t_hi[pl.ds(k0, per)].reshape(per * height, width)
        tl = t_lo[pl.ds(k0, per)].reshape(per * height, width)
        mbt[...] += lax.dot_general(
            jnp.concatenate([hi, lo, hi], axis=0), jnp.concatenate([th, th, tl], axis=0), TN,
            preferred_element_type=F32,
        )
        return carry

    lax.fori_loop(0, early, second_mode, 0)
    arrived(8, gz.at[pl.ds(0, n_z - 1)])
    gs[...] = jnp.sum(gz[...], axis=0)
    fan(9, n_q, plane_peer, lambda _: gs, ga.at[q])
    ga[q] = gs[...]
    lax.fori_loop(early, n_chunk, second_mode, 0)
    mb[...] = mbt[...].T.reshape(mb.shape)
    fan(10, n_g, group_peer, lambda where: mb.at[:, where], rb1.at[g])
    rb1[g] = mb[:, g]

    arrived(9, ga.at[pl.ds(0, n_q - 1)])
    gram = ga[...].reshape(rank, rank)
    along, down = diagonal(gram)
    weight_a = jnp.sqrt(along * (1.0 / total_a) + epsilon)
    iw[...] = 1.0 / weight_a
    w_a_ref[...] = weight_a
    hat_a_ref[...] = pa[q] / weight_a
    results = [
        pltpu.make_async_copy(have, want, out_sem.at[i])
        for i, (have, want) in enumerate(
            [(hat_a_ref, hat_a_hbm), (w_a_ref, w_a_hbm), (hat_b_ref, hat_b_hbm), (w_b_ref, w_b_hbm)]
        )
    ]
    for result in results[:2]:
        result.start()
    down = 1.0 / jnp.sqrt(down * (1.0 / total_a) + epsilon)
    scl[...] = scale_system(sysm, gram * down * iw[...] * gc[...])
    middle = rank // NB // 2
    sweep_panels(sysm, 0, middle)
    arrived(10, rb1.at[pl.ds(0, n_g - 1)])
    mb1[...] = jnp.sum(rb1[...], axis=0)
    fan(11, n_z, z_peer, lambda where: mb1.at[where], rb2.at[z])
    rb2[z] = mb1[z]
    sweep_panels(sysm, middle, rank // NB)
    arrived(11, rb2.at[pl.ds(0, n_z - 1)])
    share_b = jnp.sum(rb2[...], axis=0)
    raw_b = -jnp.dot(share_b * iw[...] * scl[...], sysm[...], precision=HIGH, preferred_element_type=F32) * scl[...]

    sq[...] = jnp.sum(raw_b * raw_b, axis=0, keepdims=True)
    fan(12, n_q, plane_peer, lambda _: sq, sqp.at[q])
    sqp[q] = sq[...]
    arrived(12, sqp.at[pl.ds(0, n_q - 1)])
    sqs[...] = jnp.sum(sqp[...], axis=0)
    fan(13, n_z, z_peer, lambda _: sqs, sqz.at[z])
    sqz[z] = sqs[...]
    arrived(13, sqz.at[pl.ds(0, n_z - 1)])
    weight_b = jnp.sqrt(jnp.sum(sqz[...], axis=0) * (1.0 / total_b) + epsilon)
    w_b_ref[...] = weight_b
    hat_b_ref[...] = raw_b / weight_b
    for result in results[2:]:
        result.start()

    sent(0, bz.at[pl.ds(0, n_z - 1)])
    if n_x > 1:
        sent(1, call.at[pl.ds(0, n_x - 1)])
    sent(2, bfull.at[:, pl.ds(0, n_g - 1)])
    sent(3, pbc)
    sent(4, pby)
    sent(5, ra.at[pl.ds(0, n_s - 1)])
    sent(6, gb.at[0])
    sent(7, pa.at[pl.ds(0, n_q - 1)])
    sent(8, gz.at[pl.ds(0, n_z - 1)])
    sent(9, ga.at[pl.ds(0, n_q - 1)])
    sent(10, rb1.at[pl.ds(0, n_g - 1)])
    sent(11, rb2.at[pl.ds(0, n_z - 1)])
    sent(12, sqp.at[pl.ds(0, n_q - 1)])
    sent(13, sqz.at[pl.ds(0, n_z - 1)])
    for result in results:
        result.wait()


def finish(*refs):
    copies = [pltpu.make_async_copy(refs[i], refs[4 + i], refs[8].at[i]) for i in range(4)]
    for copy in copies:
        copy.start()
    for copy in copies:
        copy.wait()


def local(tensor, factor_b, factor_c):
    depth, height, width = tensor.shape
    rank = factor_c.shape[1]
    n_x, n_z = lax.axis_size("ka"), lax.axis_size("ia") // 2
    n_s, n_q, n_g = 4 * n_x, 8 * n_x, 2 * n_x
    part = rank // n_q
    n_chunk = 6
    v = pltpu.VMEM
    out = jax.ShapeDtypeStruct
    hbm = pl.BlockSpec(memory_space=pltpu.HBM)
    results = [out((8, rank), F32), out((1, rank), F32), out((8, rank), F32), out((1, rank), F32)]
    found = pl.pallas_call(
        functools.partial(kernel, n_x, n_z, height * lax.axis_size("ia"), width * lax.axis_size("ja")),
        out_shape=results,
        in_specs=[hbm] * 3,
        out_specs=[hbm] * 4,
        scratch_shapes=[
            v((8, rank), F32),
            v((1, rank), F32),
            v((8, rank), F32),
            v((1, rank), F32),
            v((8, rank), F32),
            v((depth, rank), F32),
            v((depth, height, width), F32),
            v((depth, height, width), BF16),
            v((depth, height, width), BF16),
            v((n_z, 8, rank), F32),
            v((n_z, n_g, 8, rank), F32),
            v((3 * width, rank), BF16),
            v((n_x, depth, rank), F32),
            v((2, rank // 2, rank), F32),
            v((rank // 2, rank), F32),
            v((rank // 2, rank), F32),
            v((rank // 2, rank), F32),
            v((2, rank // 2, rank), F32),
            v((rank, rank), F32),
            v((n_s, 8, rank), F32),
            v((n_s, 8, rank), F32),
            v((n_q, 8, rank), F32),
            v((n_q, part, rank), F32),
            v((n_z, part, rank), F32),
            v((part, rank), F32),
            v((n_q, part, rank), F32),
            v((rank, rank), F32),
            v((1, rank), F32),
            v((1, rank), F32),
            v((rank, width), F32),
            v((n_z, n_g, 8, rank), F32),
            v((n_g, n_z, 8, rank), F32),
            v((n_z, 8, rank), F32),
            v((n_z, 8, rank), F32),
            v((1, rank), F32),
            v((n_q, 1, rank), F32),
            v((1, rank), F32),
            v((n_z, 1, rank), F32),
            pltpu.SemaphoreType.DMA((n_chunk + 2,)),
            pltpu.SemaphoreType.DMA((4,)),
            pltpu.SemaphoreType.DMA((14,)),
            pltpu.SemaphoreType.DMA((14,)),
        ],
        compiler_params=pltpu.CompilerParams(
            collective_id=0, has_side_effects=True, vmem_limit_bytes=VMEM_LIMIT
        ),
    )(tensor, factor_b, factor_c)
    hat_a, weight_a, hat_b, weight_b = pl.pallas_call(
        finish,
        out_shape=results,
        in_specs=[hbm] * 4,
        out_specs=[hbm] * 4,
        scratch_shapes=[pltpu.SemaphoreType.DMA((4,))],
        compiler_params=pltpu.CompilerParams(vmem_limit_bytes=VMEM_LIMIT),
    )(*found)
    return hat_a, weight_a.reshape(rank), hat_b, weight_b.reshape(rank)


def solution(mesh):
    return jax.shard_map(
        local,
        mesh=mesh,
        in_specs=(P("ka", "ia", "ja"), P(("ja", "ia", "ka"), None), P("ka", None)),
        out_specs=(P(("ia", "ja", "ka"), None), P(), P(("ja", "ia", "ka"), None), P()),
        check_vma=False,
    )
```

```python
import functools

import jax
import jax.numpy as jnp
from jax import lax
from jax.experimental import pallas as pl
from jax.experimental.pallas import tpu as pltpu
from jax.sharding import PartitionSpec as P

ridge_term = 0.01
epsilon = 1e-06

MESH = pl.DeviceIdType.MESH
HIGH = lax.Precision.HIGHEST
F32 = jnp.float32
BF16 = jnp.bfloat16
VMEM_LIMIT = 65000000
NB = 32
TN = (((0,), (0,)), ((), ()))


def split2(x):
    hi = x.astype(BF16)
    return hi, (x - hi.astype(F32)).astype(BF16)


def split3(x):
    hi = x.astype(BF16)
    rest = x - hi.astype(F32)
    mid = rest.astype(BF16)
    return hi, mid, (rest - mid.astype(F32)).astype(BF16)


def every(v):
    return jnp.broadcast_to(v, (8, 128))


def sweep_panels(a_ref, lt_ref, rt_ref, q_ref, first, last):
    rank = a_ref.shape[0]
    parts = rank // 128
    groups = NB // 8
    lane = lax.broadcasted_iota(jnp.int32, (NB, rank), 1)
    row = lax.broadcasted_iota(jnp.int32, (NB, rank), 0)
    row8 = lax.broadcasted_iota(jnp.int32, (8, 128), 0)

    def panel(b, carry):
        r0 = pl.multiple_of(b * NB, NB)
        before = (lane >= r0 - NB) & (lane < r0)
        r = jnp.where(before, 0.0, a_ref[pl.ds(r0, NB), :]) - jnp.dot(
            lt_ref[pl.ds(r0, NB), :], rt_ref[...], preferred_element_type=F32
        )
        base = lax.div(r0, 128)
        half = r[:, :128]
        for h in range(1, parts):
            half = jnp.where(base == h, r[:, 128 * h : 128 * h + 128], half)
        d = pltpu.roll(half, lax.rem(128 - (r0 - base * 128), 128), 1)
        catch_up(a_ref, lt_ref, rt_ref, q_ref, b)

        inside = (lane >= r0) & (lane < r0 + NB)
        rz = jnp.where(inside, 0.0, r)
        start = jnp.where(inside, jnp.where(lane - r0 == row, -1.0, 0.0), r)
        x = [
            [d[8 * m : 8 * m + 8]] + [start[8 * m : 8 * m + 8, 128 * h : 128 * h + 128] for h in range(parts)]
            for m in range(groups)
        ]
        for p in range(0, NB, 2):
            i, s = p // 8, p % 8
            left = [every(x[m][0][:, p : p + 1]) for m in range(groups)]
            right = [every(x[m][0][:, p + 1 : p + 2]) for m in range(groups)]
            a, c, e = every(left[i][s : s + 1]), every(right[i][s : s + 1]), every(right[i][s + 1 : s + 2])
            det = a * e - c * c
            inv = pl.reciprocal(det, approx=True)
            inv = inv * (2.0 - det * inv)
            inv = inv * (2.0 - det * inv)
            fa, fc, fe = a * inv, c * inv, e * inv
            for v in range(parts + 1):
                yp, yq = every(x[i][v][s : s + 1]), every(x[i][v][s + 1 : s + 2])
                wp = fe * yp - fc * yq
                wq = fa * yq - fc * yp
                for m in range(groups):
                    x[m][v] = x[m][v] - left[m] * wp - right[m] * wq
                x[i][v] = jnp.where(row8 == s, wp, jnp.where(row8 == s + 1, wq, x[i][v]))
        q = jnp.concatenate([jnp.concatenate(x[m][1:], axis=1) for m in range(groups)], axis=0)
        r1, r2, r3 = split3(rz)
        q1, q2, q3 = split3(q)
        lt_ref[...] = jnp.concatenate([r1, r1, r2, r2, r1, r3], axis=0).T
        rt_ref[...] = jnp.concatenate([q1, q2, q1, q2, q3, q1], axis=0)
        q_ref[...] = q
        return carry

    lax.fori_loop(first, last, panel, 0)


def catch_up(a_ref, lt_ref, rt_ref, q_ref, b):
    rank = a_ref.shape[0]
    r0 = b * NB
    lane = lax.broadcasted_iota(jnp.int32, (rank, rank), 1)
    update = jnp.dot(lt_ref[...], rt_ref[...], preferred_element_type=F32)
    a_ref[...] = jnp.where((lane >= r0 - NB) & (lane < r0), 0.0, a_ref[...]) - update
    a_ref[pl.ds(pl.multiple_of(jnp.maximum(r0 - NB, 0), NB), NB), :] = q_ref[...]


def sweep_begin(a_ref, lt_ref, rt_ref, q_ref):
    lt_ref[...] = jnp.zeros_like(lt_ref)
    rt_ref[...] = jnp.zeros_like(rt_ref)
    q_ref[...] = a_ref[:NB, :]


def sweep_end(a_ref, lt_ref, rt_ref, q_ref):
    catch_up(a_ref, lt_ref, rt_ref, q_ref, a_ref.shape[0] // NB)


def diagonal(matrix):
    rank = matrix.shape[0]
    eye = lax.broadcasted_iota(jnp.int32, (rank, rank), 0) == lax.broadcasted_iota(jnp.int32, (rank, rank), 1)
    kept = jnp.where(eye, matrix, 0.0)
    return jnp.sum(kept, axis=0, keepdims=True), jnp.sum(kept, axis=1, keepdims=True)


def scale_system(a_ref, product):
    rank = product.shape[0]
    eye = lax.broadcasted_iota(jnp.int32, (rank, rank), 0) == lax.broadcasted_iota(jnp.int32, (rank, rank), 1)
    system = product + jnp.where(eye, ridge_term, 0.0)
    along, down = diagonal(system)
    along, down = lax.rsqrt(along), lax.rsqrt(down)
    a_ref[...] = system * down * along
    return along


def kernel(
    n_x, n_z, total_a, total_b,
    t_hbm, b_hbm, c_hbm,
    hat_a_hbm, w_a_hbm, hat_b_hbm, w_b_hbm,
    hat_a_ref, w_a_ref, hat_b_ref, w_b_ref, b_ref, c_ref, t_f32, t_hi, t_lo, bz, bfull, bst, call, pb, pbc, hs, pby, gb, gc, ma, ra, pa, pg, gz, gs, ga, sysm, lt, rt, qp, scl, iw,
    mbt, mb, rb1, mb1, rb2, sq, sqp, sqs, sqz,
    t_sem, out_sem, send_sem, recv_sem,
):
    depth, height, width = t_f32.shape
    rank = c_ref.shape[1]
    ia, ja, ka = lax.axis_index("ia"), lax.axis_index("ja"), lax.axis_index("ka")
    z, yl = lax.div(ia, 2), lax.rem(ia, 2)
    yh, core = lax.div(ja, 2), lax.rem(ja, 2)
    n_s = 4 * n_x
    n_q = 2 * n_s
    n_g = 2 * n_x
    s = ja * n_x + ka
    q = yl * n_s + s
    g = yl * n_x + ka

    yls = [lax.rem(yl + d, 2) for d in range(2)]
    jas = [lax.rem(ja + d, 4) for d in range(4)]
    kas = [lax.rem(ka + d, n_x) for d in range(n_x)]
    zs = [lax.rem(z + d, n_z) for d in range(n_z)]
    ias = [z * 2 + yl2 for yl2 in yls]

    def plane_peer(d):
        y, j, k = d // n_s, d // n_x % 4, d % n_x
        return yls[y] * n_s + jas[j] * n_x + kas[k], (ias[y], jas[j], kas[k])

    def group_peer(d):
        y, k = d // n_x, d % n_x
        return yls[y] * n_x + kas[k], (ias[y], ja, kas[k])

    def share_peer(d):
        j, k = d // n_x, d % n_x
        return jas[j] * n_x + kas[k], (ia, jas[j], kas[k])

    def z_peer(d):
        return zs[d], (zs[d] * 2 + yl, ja, ka)

    def x_peer(d):
        return kas[d], (ia, ja, kas[d])

    def send(stage, src, dst, device):
        pltpu.make_async_remote_copy(
            src_ref=src, dst_ref=dst, send_sem=send_sem.at[stage], recv_sem=recv_sem.at[stage],
            device_id=device, device_id_type=MESH,
        ).start()

    def fan(stage, count, peer, src, dst):
        for d in range(1, count):
            where, device = peer(d)
            send(stage, src(where), dst, device)

    def arrived(stage, ref):
        pltpu.make_async_copy(ref, ref, recv_sem.at[stage]).wait()

    def sent(stage, ref):
        pltpu.make_async_copy(ref, ref, send_sem.at[stage]).wait()

    n_chunk = t_sem.shape[0] - 2
    per = depth // n_chunk
    loads = [
        pltpu.make_async_copy(t_hbm.at[pl.ds(i * per, per)], t_f32.at[pl.ds(i * per, per)], t_sem.at[i])
        for i in range(n_chunk)
    ]
    small = [pltpu.make_async_copy(b_hbm, b_ref, t_sem.at[n_chunk]), pltpu.make_async_copy(c_hbm, c_ref, t_sem.at[n_chunk + 1])]
    for load in small + loads:
        load.start()

    barrier = pltpu.get_barrier_semaphore()

    for count, peer in ((n_z, z_peer), (n_q, plane_peer)):
        for d in range(1, count):
            pl.semaphore_signal(barrier, inc=1, device_id=peer(d)[1], device_id_type=MESH)
    pl.semaphore_wait(barrier, n_q + n_z - 2)

    for load in small:
        load.wait()
    fan(0, n_z, z_peer, lambda _: b_ref, bz.at[z])
    fan(1, n_x, x_peer, lambda _: c_ref, call.at[ka])
    bz[z] = b_ref[...]
    call[ka] = c_ref[...]

    def cut(first, last):
        def body(k, carry):
            hi, lo = split2(t_f32[k])
            t_hi[k] = hi
            t_lo[k] = lo
            return carry

        lax.fori_loop(first, last, body, 0)

    early = n_chunk // 2
    arrived(0, bz.at[pl.ds(0, n_z - 1)])
    fan(2, n_g, group_peer, lambda _: bz, bfull.at[:, g])
    bfull[:, g] = bz[...]
    for i in range(n_chunk):
        loads[i].wait()
        cut(i * per, (i + 1) * per)
    if n_x > 1:
        arrived(1, call.at[pl.ds(0, n_x - 1)])
    call_rows = call[...].reshape(n_x * depth, rank)
    gc[...] = lax.dot_general(call_rows, call_rows, TN, precision=HIGH, preferred_element_type=F32)

    arrived(2, bfull.at[:, pl.ds(0, n_g - 1)])
    rows_b = bfull[...].reshape(width, rank)
    pb[...] = lax.dot_general(rows_b, rows_b, TN, precision=HIGH, preferred_element_type=F32).reshape(pb.shape)
    sibling = (ia, ja + 1 - 2 * core, ka)
    across = (z * 2 + 1 - yl, ja + 2 - 4 * yh, ka)
    send(3, pb.at[1 - core], pbc, sibling)
    hi, lo = split2(rows_b)
    bst[...] = jnp.concatenate([hi, lo, hi], axis=0)
    ma[...] = jnp.zeros_like(ma)

    def first_mode(i, carry):
        k0 = i * per
        th = t_hi[pl.ds(k0, per)].reshape(per * height, width)
        tl = t_lo[pl.ds(k0, per)].reshape(per * height, width)
        along = jnp.dot(jnp.concatenate([th, th, tl], axis=1), bst[...], preferred_element_type=F32)
        total = ma[...].reshape(height, rank)
        for j in range(per):
            total = total + along[j * height : (j + 1) * height] * c_ref[pl.ds(k0 + j, 1), :]
        ma[...] = total.reshape(ma.shape)
        return carry

    lax.fori_loop(0, early, first_mode, 0)
    arrived(3, pbc)
    hs[...] = pb[core] + pbc[...]
    send(4, hs, pby, across)
    lax.fori_loop(early, n_chunk, first_mode, 0)
    fan(5, n_s, share_peer, lambda where: ma.at[where], ra.at[s])
    ra[s] = ma[s]
    arrived(4, pby)
    gb[core] = hs[...] + pby[...]
    send(6, gb.at[core], gb.at[core], sibling)
    arrived(6, gb.at[0])

    scl[...] = scale_system(sysm, gb[...].reshape(rank, rank) * gc[...])
    sweep = (sysm, lt, rt, qp)
    sweep_begin(*sweep)
    sweep_panels(*sweep, 0, rank // NB)
    sweep_end(*sweep)
    arrived(5, ra.at[pl.ds(0, n_s - 1)])
    share_a = jnp.sum(ra[...], axis=0)
    raw_a = -jnp.dot(share_a * scl[...], sysm[...], precision=HIGH, preferred_element_type=F32) * scl[...]

    pa[q] = raw_a
    fan(7, n_q, plane_peer, lambda _: pa.at[q], pa.at[q])
    arrived(7, pa.at[pl.ds(0, n_q - 1)])
    rows_a = pa[...].reshape(n_q * 8, rank)
    pg[...] = lax.dot_general(rows_a, rows_a, TN, precision=HIGH, preferred_element_type=F32).reshape(pg.shape)
    fan(8, n_z, z_peer, lambda _: pg.at[q], gz.at[z])
    gz[z] = pg[q]
    mbt[...] = jnp.zeros_like(mbt)

    def second_mode(i, carry):
        k0 = i * per
        rows = pa[pl.ds(yl * n_s, n_s)].reshape(height, rank)
        both = jnp.concatenate([rows * c_ref[pl.ds(k0 + j, 1), :] for j in range(per)], axis=0)
        hi, lo = split2(both)
        th = t_hi[pl.ds(k0, per)].reshape(per * height, width)
        tl = t_lo[pl.ds(k0, per)].reshape(per * height, width)
        mbt[...] += lax.dot_general(
            jnp.concatenate([hi, lo, hi], axis=0), jnp.concatenate([th, th, tl], axis=0), TN,
            preferred_element_type=F32,
        )
        return carry

    lax.fori_loop(0, early, second_mode, 0)
    arrived(8, gz.at[pl.ds(0, n_z - 1)])
    gs[...] = jnp.sum(gz[...], axis=0)
    fan(9, n_q, plane_peer, lambda _: gs, ga.at[q])
    ga[q] = gs[...]
    lax.fori_loop(early, n_chunk, second_mode, 0)
    mb[...] = mbt[...].T.reshape(mb.shape)
    fan(10, n_g, group_peer, lambda where: mb.at[:, where], rb1.at[g])
    rb1[g] = mb[:, g]

    arrived(9, ga.at[pl.ds(0, n_q - 1)])
    gram = ga[...].reshape(rank, rank)
    along, down = diagonal(gram)
    weight_a = jnp.sqrt(along * (1.0 / total_a) + epsilon)
    iw[...] = 1.0 / weight_a
    w_a_ref[...] = weight_a
    hat_a_ref[...] = pa[q] / weight_a
    results = [
        pltpu.make_async_copy(have, want, out_sem.at[i])
        for i, (have, want) in enumerate(
            [(hat_a_ref, hat_a_hbm), (w_a_ref, w_a_hbm), (hat_b_ref, hat_b_hbm), (w_b_ref, w_b_hbm)]
        )
    ]
    for result in results[:2]:
        result.start()
    down = 1.0 / jnp.sqrt(down * (1.0 / total_a) + epsilon)
    scl[...] = scale_system(sysm, gram * down * iw[...] * gc[...])
    middle = rank // NB // 2
    sweep_begin(*sweep)
    sweep_panels(*sweep, 0, middle)
    arrived(10, rb1.at[pl.ds(0, n_g - 1)])
    mb1[...] = jnp.sum(rb1[...], axis=0)
    fan(11, n_z, z_peer, lambda where: mb1.at[where], rb2.at[z])
    rb2[z] = mb1[z]
    sweep_panels(*sweep, middle, rank // NB)
    sweep_end(*sweep)
    arrived(11, rb2.at[pl.ds(0, n_z - 1)])
    share_b = jnp.sum(rb2[...], axis=0)
    raw_b = -jnp.dot(share_b * iw[...] * scl[...], sysm[...], precision=HIGH, preferred_element_type=F32) * scl[...]

    sq[...] = jnp.sum(raw_b * raw_b, axis=0, keepdims=True)
    fan(12, n_q, plane_peer, lambda _: sq, sqp.at[q])
    sqp[q] = sq[...]
    arrived(12, sqp.at[pl.ds(0, n_q - 1)])
    sqs[...] = jnp.sum(sqp[...], axis=0)
    fan(13, n_z, z_peer, lambda _: sqs, sqz.at[z])
    sqz[z] = sqs[...]
    arrived(13, sqz.at[pl.ds(0, n_z - 1)])
    weight_b = jnp.sqrt(jnp.sum(sqz[...], axis=0) * (1.0 / total_b) + epsilon)
    w_b_ref[...] = weight_b
    hat_b_ref[...] = raw_b / weight_b
    for result in results[2:]:
        result.start()

    sent(0, bz.at[pl.ds(0, n_z - 1)])
    if n_x > 1:
        sent(1, call.at[pl.ds(0, n_x - 1)])
    sent(2, bfull.at[:, pl.ds(0, n_g - 1)])
    sent(3, pbc)
    sent(4, pby)
    sent(5, ra.at[pl.ds(0, n_s - 1)])
    sent(6, gb.at[0])
    sent(7, pa.at[pl.ds(0, n_q - 1)])
    sent(8, gz.at[pl.ds(0, n_z - 1)])
    sent(9, ga.at[pl.ds(0, n_q - 1)])
    sent(10, rb1.at[pl.ds(0, n_g - 1)])
    sent(11, rb2.at[pl.ds(0, n_z - 1)])
    sent(12, sqp.at[pl.ds(0, n_q - 1)])
    sent(13, sqz.at[pl.ds(0, n_z - 1)])
    for result in results:
        result.wait()


def finish(*refs):
    copies = [pltpu.make_async_copy(refs[i], refs[4 + i], refs[8].at[i]) for i in range(4)]
    for copy in copies:
        copy.start()
    for copy in copies:
        copy.wait()


def local(tensor, factor_b, factor_c):
    depth, height, width = tensor.shape
    rank = factor_c.shape[1]
    n_x, n_z = lax.axis_size("ka"), lax.axis_size("ia") // 2
    n_s, n_q, n_g = 4 * n_x, 8 * n_x, 2 * n_x
    part = rank // n_q
    n_chunk = 6
    v = pltpu.VMEM
    out = jax.ShapeDtypeStruct
    hbm = pl.BlockSpec(memory_space=pltpu.HBM)
    results = [out((8, rank), F32), out((1, rank), F32), out((8, rank), F32), out((1, rank), F32)]
    found = pl.pallas_call(
        functools.partial(kernel, n_x, n_z, height * lax.axis_size("ia"), width * lax.axis_size("ja")),
        out_shape=results,
        in_specs=[hbm] * 3,
        out_specs=[hbm] * 4,
        scratch_shapes=[
            v((8, rank), F32),
            v((1, rank), F32),
            v((8, rank), F32),
            v((1, rank), F32),
            v((8, rank), F32),
            v((depth, rank), F32),
            v((depth, height, width), F32),
            v((depth, height, width), BF16),
            v((depth, height, width), BF16),
            v((n_z, 8, rank), F32),
            v((n_z, n_g, 8, rank), F32),
            v((3 * width, rank), BF16),
            v((n_x, depth, rank), F32),
            v((2, rank // 2, rank), F32),
            v((rank // 2, rank), F32),
            v((rank // 2, rank), F32),
            v((rank // 2, rank), F32),
            v((2, rank // 2, rank), F32),
            v((rank, rank), F32),
            v((n_s, 8, rank), F32),
            v((n_s, 8, rank), F32),
            v((n_q, 8, rank), F32),
            v((n_q, part, rank), F32),
            v((n_z, part, rank), F32),
            v((part, rank), F32),
            v((n_q, part, rank), F32),
            v((rank, rank), F32),
            v((rank, 6 * NB), BF16),
            v((6 * NB, rank), BF16),
            v((NB, rank), F32),
            v((1, rank), F32),
            v((1, rank), F32),
            v((rank, width), F32),
            v((n_z, n_g, 8, rank), F32),
            v((n_g, n_z, 8, rank), F32),
            v((n_z, 8, rank), F32),
            v((n_z, 8, rank), F32),
            v((1, rank), F32),
            v((n_q, 1, rank), F32),
            v((1, rank), F32),
            v((n_z, 1, rank), F32),
            pltpu.SemaphoreType.DMA((n_chunk + 2,)),
            pltpu.SemaphoreType.DMA((4,)),
            pltpu.SemaphoreType.DMA((14,)),
            pltpu.SemaphoreType.DMA((14,)),
        ],
        compiler_params=pltpu.CompilerParams(
            collective_id=0, has_side_effects=True, vmem_limit_bytes=VMEM_LIMIT
        ),
    )(tensor, factor_b, factor_c)
    hat_a, weight_a, hat_b, weight_b = pl.pallas_call(
        finish,
        out_shape=results,
        in_specs=[hbm] * 4,
        out_specs=[hbm] * 4,
        scratch_shapes=[pltpu.SemaphoreType.DMA((4,))],
        compiler_params=pltpu.CompilerParams(vmem_limit_bytes=VMEM_LIMIT),
    )(*found)
    return hat_a, weight_a.reshape(rank), hat_b, weight_b.reshape(rank)


def solution(mesh):
    return jax.shard_map(
        local,
        mesh=mesh,
        in_specs=(P("ka", "ia", "ja"), P(("ja", "ia", "ka"), None), P("ka", None)),
        out_specs=(P(("ia", "ja", "ka"), None), P(), P(("ja", "ia", "ka"), None), P()),
        check_vma=False,
    )
```

```python
import functools

import jax
import jax.numpy as jnp
from jax import lax
from jax.experimental import pallas as pl
from jax.experimental.pallas import tpu as pltpu
from jax.sharding import PartitionSpec as P

ridge_term = 0.01
epsilon = 1e-06

MESH = pl.DeviceIdType.MESH
HIGH = lax.Precision.HIGHEST
F32 = jnp.float32
BF16 = jnp.bfloat16
VMEM_LIMIT = 65000000
NB = 32
SUB = 16
TN = (((0,), (0,)), ((), ()))


def split2(x):
    hi = x.astype(BF16)
    return hi, (x - hi.astype(F32)).astype(BF16)


def split3(x):
    hi = x.astype(BF16)
    rest = x - hi.astype(F32)
    mid = rest.astype(BF16)
    return hi, mid, (rest - mid.astype(F32)).astype(BF16)


def sweep_half(a_ref, lt_ref, rt_ref, q_ref, tmp_ref, h):
    rank = a_ref.shape[0]
    parts = rank // 128
    row8 = lax.broadcasted_iota(jnp.int32, (8, 128), 0)
    lane8 = lax.broadcasted_iota(jnp.int32, (8, 128), 1)
    lane = lax.broadcasted_iota(jnp.int32, (NB, rank), 1)
    groups = NB // 8
    wide = SUB // 8
    for t in range(128 // NB):
        l0 = t * NB
        r0 = pl.multiple_of(h * 128 + l0, NB)
        before = (lane >= r0 - NB) & (lane < r0)
        r = jnp.where(before, 0.0, a_ref[pl.ds(r0, NB), :]) - jnp.dot(
            lt_ref[pl.ds(r0, NB), :], rt_ref[...], preferred_element_type=F32
        )
        catch_up(a_ref, lt_ref, rt_ref, q_ref, r0)
        r1, r2, r3 = split3(jnp.where((lane >= r0) & (lane < r0 + NB), 0.0, r))
        lt_ref[...] = jnp.concatenate([r1, r1, r2, r2, r1, r3], axis=0).T
        half = [r[:, 128 * v : 128 * v + 128] for v in range(parts)]
        own = half[0]
        for v in range(1, parts):
            own = jnp.where(h == v, half[v], own)
        half = [own] + [jnp.where(h == v, half[0], half[v]) for v in range(1, parts)]
        x = [[y[8 * m : 8 * m + 8] for y in half] for m in range(groups)]
        for u in range(NB // SUB):
            mine = range(u * wide, (u + 1) * wide)
            rest = [m for m in range(groups) if m not in mine]
            first = l0 + u * SUB
            spread = lambda m, j: jnp.broadcast_to(x[m][0][:, first + j : first + j + 1], (8, 128))
            cols = [{m: spread(m, j) for m in mine} for j in range(SUB)]
            left = {m: [spread(m, j) for j in range(SUB)] for m in rest}
            slot = 0

            def rows_of(y, s):
                nonlocal slot
                tmp_ref[slot] = y
                found = [jnp.broadcast_to(tmp_ref[slot, i : i + 1, :], (8, 128)) for i in (s, s + 1)]
                slot += 1
                return found

            for p in range(0, SUB, 2):
                i, s = u * wide + p // 8, p % 8
                a, c = rows_of(cols[p][i], s)
                _, e = rows_of(cols[p + 1][i], s)
                det = a * e - c * c
                inv = pl.reciprocal(det, approx=True)
                inv = inv * (2.0 - det * inv)
                inv = inv * (2.0 - det * inv)

                def apply(y):
                    yp, yq = rows_of(y[i], s)
                    np_ = e * yp - c * yq
                    nq_ = a * yq - c * yp
                    done = {m: y[m] - (cols[p][m] * np_ + cols[p + 1][m] * nq_) * inv for m in mine}
                    done[i] = jnp.where(row8 == s, np_ * inv, jnp.where(row8 == s + 1, nq_ * inv, done[i]))
                    return done

                for j in range(p + 2, SUB):
                    cols[j] = apply(cols[j])
                here = (lane8 == first + p) | (lane8 == first + p + 1)
                unit = jnp.where(lane8 - first - p == row8 - s, -1.0, 0.0)
                for m in mine:
                    x[m][0] = jnp.where(here, unit if m == i else 0.0, x[m][0])
                for v in range(parts):
                    done = apply({m: x[m][v] for m in mine})
                    for m in mine:
                        x[m][v] = done[m]
            ours = (lane8 >= first) & (lane8 < first + SUB)
            base = slot
            for m in mine:
                for v in range(parts):
                    tmp_ref[slot] = x[m][v]
                    slot += 1
            for m in rest:
                x[m][0] = jnp.where(ours, 0.0, x[m][0])
                for v in range(parts):
                    terms = [
                        left[m][j] * jnp.broadcast_to(tmp_ref[base + j // 8 * parts + v, j % 8 : j % 8 + 1, :], (8, 128))
                        for j in range(SUB)
                    ]
                    while len(terms) > 1:
                        terms = [terms[k] + terms[k + 1] for k in range(0, len(terms), 2)]
                    x[m][v] = x[m][v] - terms[0]
        half = [jnp.concatenate([x[m][v] for m in range(groups)], axis=0) for v in range(parts)]
        half = [jnp.where(h == 0, half[0], half[1]), jnp.where(h == 0, half[1], half[0])]
        q = jnp.concatenate(half, axis=1)
        q1, q2, q3 = split3(q)
        rt_ref[...] = jnp.concatenate([q1, q2, q1, q2, q3, q1], axis=0)
        q_ref[...] = q


def catch_up(a_ref, lt_ref, rt_ref, q_ref, r0):
    rank = a_ref.shape[0]
    lane = lax.broadcasted_iota(jnp.int32, (rank, rank), 1)
    update = jnp.dot(lt_ref[...], rt_ref[...], preferred_element_type=F32)
    a_ref[...] = jnp.where((lane >= r0 - NB) & (lane < r0), 0.0, a_ref[...]) - update
    a_ref[pl.ds(pl.multiple_of(jnp.maximum(r0 - NB, 0), NB), NB), :] = q_ref[...]


def sweep_begin(a_ref, lt_ref, rt_ref, q_ref, tmp_ref):
    lt_ref[...] = jnp.zeros_like(lt_ref)
    rt_ref[...] = jnp.zeros_like(rt_ref)
    q_ref[...] = a_ref[:NB, :]


def sweep_end(a_ref, lt_ref, rt_ref, q_ref, tmp_ref):
    catch_up(a_ref, lt_ref, rt_ref, q_ref, a_ref.shape[0])


def diagonal(matrix):
    rank = matrix.shape[0]
    eye = lax.broadcasted_iota(jnp.int32, (rank, rank), 0) == lax.broadcasted_iota(jnp.int32, (rank, rank), 1)
    kept = jnp.where(eye, matrix, 0.0)
    return jnp.sum(kept, axis=0, keepdims=True), jnp.sum(kept, axis=1, keepdims=True)


def scale_system(a_ref, product):
    rank = product.shape[0]
    eye = lax.broadcasted_iota(jnp.int32, (rank, rank), 0) == lax.broadcasted_iota(jnp.int32, (rank, rank), 1)
    system = product + jnp.where(eye, ridge_term, 0.0)
    along, down = diagonal(system)
    along, down = lax.rsqrt(along), lax.rsqrt(down)
    a_ref[...] = system * down * along
    return along


def kernel(
    n_x, n_z, total_a, total_b,
    t_hbm, b_hbm, c_hbm,
    hat_a_hbm, w_a_hbm, hat_b_hbm, w_b_hbm,
    hat_a_ref, w_a_ref, hat_b_ref, w_b_ref, b_ref, c_ref, t_f32, t_hi, t_lo, bz, bfull, bst, call, pb, pbc, hs, pby, gb, gc, ma, ra, pa, pg, gz, gs, ga, sysm, lt, rt, qp, tmp, scl, iw,
    mbt, mb, rb1, mb1, rb2, sq, sqp, sqs, sqz,
    t_sem, out_sem, send_sem, recv_sem,
):
    depth, height, width = t_f32.shape
    rank = c_ref.shape[1]
    ia, ja, ka = lax.axis_index("ia"), lax.axis_index("ja"), lax.axis_index("ka")
    z, yl = lax.div(ia, 2), lax.rem(ia, 2)
    yh, core = lax.div(ja, 2), lax.rem(ja, 2)
    n_s = 4 * n_x
    n_q = 2 * n_s
    n_g = 2 * n_x
    s = ja * n_x + ka
    q = yl * n_s + s
    g = yl * n_x + ka

    yls = [lax.rem(yl + d, 2) for d in range(2)]
    jas = [lax.rem(ja + d, 4) for d in range(4)]
    kas = [lax.rem(ka + d, n_x) for d in range(n_x)]
    zs = [lax.rem(z + d, n_z) for d in range(n_z)]
    ias = [z * 2 + yl2 for yl2 in yls]

    def plane_peer(d):
        y, j, k = d // n_s, d // n_x % 4, d % n_x
        return yls[y] * n_s + jas[j] * n_x + kas[k], (ias[y], jas[j], kas[k])

    def group_peer(d):
        y, k = d // n_x, d % n_x
        return yls[y] * n_x + kas[k], (ias[y], ja, kas[k])

    def share_peer(d):
        j, k = d // n_x, d % n_x
        return jas[j] * n_x + kas[k], (ia, jas[j], kas[k])

    def z_peer(d):
        return zs[d], (zs[d] * 2 + yl, ja, ka)

    def x_peer(d):
        return kas[d], (ia, ja, kas[d])

    def send(stage, src, dst, device):
        pltpu.make_async_remote_copy(
            src_ref=src, dst_ref=dst, send_sem=send_sem.at[stage], recv_sem=recv_sem.at[stage],
            device_id=device, device_id_type=MESH,
        ).start()

    def fan(stage, count, peer, src, dst):
        for d in range(1, count):
            where, device = peer(d)
            send(stage, src(where), dst, device)

    def arrived(stage, ref):
        pltpu.make_async_copy(ref, ref, recv_sem.at[stage]).wait()

    def sent(stage, ref):
        pltpu.make_async_copy(ref, ref, send_sem.at[stage]).wait()

    n_chunk = t_sem.shape[0] - 2
    per = depth // n_chunk
    loads = [
        pltpu.make_async_copy(t_hbm.at[pl.ds(i * per, per)], t_f32.at[pl.ds(i * per, per)], t_sem.at[i])
        for i in range(n_chunk)
    ]
    small = [pltpu.make_async_copy(b_hbm, b_ref, t_sem.at[n_chunk]), pltpu.make_async_copy(c_hbm, c_ref, t_sem.at[n_chunk + 1])]
    for load in small + loads:
        load.start()

    barrier = pltpu.get_barrier_semaphore()

    for count, peer in ((n_z, z_peer), (n_q, plane_peer)):
        for d in range(1, count):
            pl.semaphore_signal(barrier, inc=1, device_id=peer(d)[1], device_id_type=MESH)
    pl.semaphore_wait(barrier, n_q + n_z - 2)

    for load in small:
        load.wait()
    fan(0, n_z, z_peer, lambda _: b_ref, bz.at[z])
    fan(1, n_x, x_peer, lambda _: c_ref, call.at[ka])
    bz[z] = b_ref[...]
    call[ka] = c_ref[...]

    def cut(first, last):
        def body(k, carry):
            hi, lo = split2(t_f32[k])
            t_hi[k] = hi
            t_lo[k] = lo
            return carry

        lax.fori_loop(first, last, body, 0)

    early = n_chunk // 2
    arrived(0, bz.at[pl.ds(0, n_z - 1)])
    fan(2, n_g, group_peer, lambda _: bz, bfull.at[:, g])
    bfull[:, g] = bz[...]
    for i in range(n_chunk):
        loads[i].wait()
        cut(i * per, (i + 1) * per)
    if n_x > 1:
        arrived(1, call.at[pl.ds(0, n_x - 1)])
    call_rows = call[...].reshape(n_x * depth, rank)
    gc[...] = lax.dot_general(call_rows, call_rows, TN, precision=HIGH, preferred_element_type=F32)

    arrived(2, bfull.at[:, pl.ds(0, n_g - 1)])
    rows_b = bfull[...].reshape(width, rank)
    pb[...] = lax.dot_general(rows_b, rows_b, TN, precision=HIGH, preferred_element_type=F32).reshape(pb.shape)
    sibling = (ia, ja + 1 - 2 * core, ka)
    across = (z * 2 + 1 - yl, ja + 2 - 4 * yh, ka)
    send(3, pb.at[1 - core], pbc, sibling)
    hi, lo = split2(rows_b)
    bst[...] = jnp.concatenate([hi, lo, hi], axis=0)
    ma[...] = jnp.zeros_like(ma)

    def first_mode(i, carry):
        k0 = i * per
        th = t_hi[pl.ds(k0, per)].reshape(per * height, width)
        tl = t_lo[pl.ds(k0, per)].reshape(per * height, width)
        along = jnp.dot(jnp.concatenate([th, th, tl], axis=1), bst[...], preferred_element_type=F32)
        total = ma[...].reshape(height, rank)
        for j in range(per):
            total = total + along[j * height : (j + 1) * height] * c_ref[pl.ds(k0 + j, 1), :]
        ma[...] = total.reshape(ma.shape)
        return carry

    lax.fori_loop(0, early, first_mode, 0)
    arrived(3, pbc)
    hs[...] = pb[core] + pbc[...]
    send(4, hs, pby, across)
    lax.fori_loop(early, n_chunk, first_mode, 0)
    fan(5, n_s, share_peer, lambda where: ma.at[where], ra.at[s])
    ra[s] = ma[s]
    arrived(4, pby)
    gb[core] = hs[...] + pby[...]
    send(6, gb.at[core], gb.at[core], sibling)
    arrived(6, gb.at[0])

    scl[...] = scale_system(sysm, gb[...].reshape(rank, rank) * gc[...])
    sweep = (sysm, lt, rt, qp, tmp)

    def half_of(h, carry):
        sweep_half(*sweep, h)
        return carry

    sweep_begin(*sweep)
    lax.fori_loop(0, rank // 128, half_of, 0)
    sweep_end(*sweep)
    arrived(5, ra.at[pl.ds(0, n_s - 1)])
    share_a = jnp.sum(ra[...], axis=0)
    raw_a = -jnp.dot(share_a * scl[...], sysm[...], precision=HIGH, preferred_element_type=F32) * scl[...]

    pa[q] = raw_a
    fan(7, n_q, plane_peer, lambda _: pa.at[q], pa.at[q])
    arrived(7, pa.at[pl.ds(0, n_q - 1)])
    rows_a = pa[...].reshape(n_q * 8, rank)
    pg[...] = lax.dot_general(rows_a, rows_a, TN, precision=HIGH, preferred_element_type=F32).reshape(pg.shape)
    fan(8, n_z, z_peer, lambda _: pg.at[q], gz.at[z])
    gz[z] = pg[q]
    mbt[...] = jnp.zeros_like(mbt)

    def second_mode(i, carry):
        k0 = i * per
        rows = pa[pl.ds(yl * n_s, n_s)].reshape(height, rank)
        both = jnp.concatenate([rows * c_ref[pl.ds(k0 + j, 1), :] for j in range(per)], axis=0)
        hi, lo = split2(both)
        th = t_hi[pl.ds(k0, per)].reshape(per * height, width)
        tl = t_lo[pl.ds(k0, per)].reshape(per * height, width)
        mbt[...] += lax.dot_general(
            jnp.concatenate([hi, lo, hi], axis=0), jnp.concatenate([th, th, tl], axis=0), TN,
            preferred_element_type=F32,
        )
        return carry

    lax.fori_loop(0, early, second_mode, 0)
    arrived(8, gz.at[pl.ds(0, n_z - 1)])
    gs[...] = jnp.sum(gz[...], axis=0)
    fan(9, n_q, plane_peer, lambda _: gs, ga.at[q])
    ga[q] = gs[...]
    lax.fori_loop(early, n_chunk, second_mode, 0)
    mb[...] = mbt[...].T.reshape(mb.shape)
    fan(10, n_g, group_peer, lambda where: mb.at[:, where], rb1.at[g])
    rb1[g] = mb[:, g]

    arrived(9, ga.at[pl.ds(0, n_q - 1)])
    gram = ga[...].reshape(rank, rank)
    along, down = diagonal(gram)
    weight_a = jnp.sqrt(along * (1.0 / total_a) + epsilon)
    iw[...] = 1.0 / weight_a
    w_a_ref[...] = weight_a
    hat_a_ref[...] = pa[q] / weight_a
    results = [
        pltpu.make_async_copy(have, want, out_sem.at[i])
        for i, (have, want) in enumerate(
            [(hat_a_ref, hat_a_hbm), (w_a_ref, w_a_hbm), (hat_b_ref, hat_b_hbm), (w_b_ref, w_b_hbm)]
        )
    ]
    for result in results[:2]:
        result.start()
    down = 1.0 / jnp.sqrt(down * (1.0 / total_a) + epsilon)
    scl[...] = scale_system(sysm, gram * down * iw[...] * gc[...])
    sweep_begin(*sweep)

    def half_with_sums(h, carry):
        sweep_half(*sweep, h)

        @pl.when(h == 0)
        def _():
            arrived(10, rb1.at[pl.ds(0, n_g - 1)])
            mb1[...] = jnp.sum(rb1[...], axis=0)
            fan(11, n_z, z_peer, lambda where: mb1.at[where], rb2.at[z])
            rb2[z] = mb1[z]

        return carry

    lax.fori_loop(0, rank // 128, half_with_sums, 0)
    sweep_end(*sweep)
    arrived(11, rb2.at[pl.ds(0, n_z - 1)])
    share_b = jnp.sum(rb2[...], axis=0)
    raw_b = -jnp.dot(share_b * iw[...] * scl[...], sysm[...], precision=HIGH, preferred_element_type=F32) * scl[...]

    sq[...] = jnp.sum(raw_b * raw_b, axis=0, keepdims=True)
    fan(12, n_q, plane_peer, lambda _: sq, sqp.at[q])
    sqp[q] = sq[...]
    arrived(12, sqp.at[pl.ds(0, n_q - 1)])
    sqs[...] = jnp.sum(sqp[...], axis=0)
    fan(13, n_z, z_peer, lambda _: sqs, sqz.at[z])
    sqz[z] = sqs[...]
    arrived(13, sqz.at[pl.ds(0, n_z - 1)])
    weight_b = jnp.sqrt(jnp.sum(sqz[...], axis=0) * (1.0 / total_b) + epsilon)
    w_b_ref[...] = weight_b
    hat_b_ref[...] = raw_b / weight_b
    for result in results[2:]:
        result.start()

    sent(0, bz.at[pl.ds(0, n_z - 1)])
    if n_x > 1:
        sent(1, call.at[pl.ds(0, n_x - 1)])
    sent(2, bfull.at[:, pl.ds(0, n_g - 1)])
    sent(3, pbc)
    sent(4, pby)
    sent(5, ra.at[pl.ds(0, n_s - 1)])
    sent(6, gb.at[0])
    sent(7, pa.at[pl.ds(0, n_q - 1)])
    sent(8, gz.at[pl.ds(0, n_z - 1)])
    sent(9, ga.at[pl.ds(0, n_q - 1)])
    sent(10, rb1.at[pl.ds(0, n_g - 1)])
    sent(11, rb2.at[pl.ds(0, n_z - 1)])
    sent(12, sqp.at[pl.ds(0, n_q - 1)])
    sent(13, sqz.at[pl.ds(0, n_z - 1)])
    for result in results:
        result.wait()


def finish(*refs):
    copies = [pltpu.make_async_copy(refs[i], refs[4 + i], refs[8].at[i]) for i in range(4)]
    for copy in copies:
        copy.start()
    for copy in copies:
        copy.wait()


def local(tensor, factor_b, factor_c):
    depth, height, width = tensor.shape
    rank = factor_c.shape[1]
    n_x, n_z = lax.axis_size("ka"), lax.axis_size("ia") // 2
    n_s, n_q, n_g = 4 * n_x, 8 * n_x, 2 * n_x
    part = rank // n_q
    n_chunk = 6
    v = pltpu.VMEM
    out = jax.ShapeDtypeStruct
    hbm = pl.BlockSpec(memory_space=pltpu.HBM)
    results = [out((8, rank), F32), out((1, rank), F32), out((8, rank), F32), out((1, rank), F32)]
    found = pl.pallas_call(
        functools.partial(kernel, n_x, n_z, height * lax.axis_size("ia"), width * lax.axis_size("ja")),
        out_shape=results,
        in_specs=[hbm] * 3,
        out_specs=[hbm] * 4,
        scratch_shapes=[
            v((8, rank), F32),
            v((1, rank), F32),
            v((8, rank), F32),
            v((1, rank), F32),
            v((8, rank), F32),
            v((depth, rank), F32),
            v((depth, height, width), F32),
            v((depth, height, width), BF16),
            v((depth, height, width), BF16),
            v((n_z, 8, rank), F32),
            v((n_z, n_g, 8, rank), F32),
            v((3 * width, rank), BF16),
            v((n_x, depth, rank), F32),
            v((2, rank // 2, rank), F32),
            v((rank // 2, rank), F32),
            v((rank // 2, rank), F32),
            v((rank // 2, rank), F32),
            v((2, rank // 2, rank), F32),
            v((rank, rank), F32),
            v((n_s, 8, rank), F32),
            v((n_s, 8, rank), F32),
            v((n_q, 8, rank), F32),
            v((n_q, part, rank), F32),
            v((n_z, part, rank), F32),
            v((part, rank), F32),
            v((n_q, part, rank), F32),
            v((rank, rank), F32),
            v((rank, 6 * NB), BF16),
            v((6 * NB, rank), BF16),
            v((NB, rank), F32),
            v((128, 8, 128), F32),
            v((1, rank), F32),
            v((1, rank), F32),
            v((rank, width), F32),
            v((n_z, n_g, 8, rank), F32),
            v((n_g, n_z, 8, rank), F32),
            v((n_z, 8, rank), F32),
            v((n_z, 8, rank), F32),
            v((1, rank), F32),
            v((n_q, 1, rank), F32),
            v((1, rank), F32),
            v((n_z, 1, rank), F32),
            pltpu.SemaphoreType.DMA((n_chunk + 2,)),
            pltpu.SemaphoreType.DMA((4,)),
            pltpu.SemaphoreType.DMA((14,)),
            pltpu.SemaphoreType.DMA((14,)),
        ],
        compiler_params=pltpu.CompilerParams(
            collective_id=0, has_side_effects=True, vmem_limit_bytes=VMEM_LIMIT
        ),
    )(tensor, factor_b, factor_c)
    hat_a, weight_a, hat_b, weight_b = pl.pallas_call(
        finish,
        out_shape=results,
        in_specs=[hbm] * 4,
        out_specs=[hbm] * 4,
        scratch_shapes=[pltpu.SemaphoreType.DMA((4,))],
        compiler_params=pltpu.CompilerParams(vmem_limit_bytes=VMEM_LIMIT),
    )(*found)
    return hat_a, weight_a.reshape(rank), hat_b, weight_b.reshape(rank)


def solution(mesh):
    return jax.shard_map(
        local,
        mesh=mesh,
        in_specs=(P("ka", "ia", "ja"), P(("ja", "ia", "ka"), None), P("ka", None)),
        out_specs=(P(("ia", "ja", "ka"), None), P(), P(("ja", "ia", "ka"), None), P()),
        check_vma=False,
    )
```

```python
import functools

import jax
import jax.numpy as jnp
from jax import lax
from jax.experimental import pallas as pl
from jax.experimental.pallas import tpu as pltpu
from jax.sharding import PartitionSpec as P

ridge_term = 0.01
epsilon = 1e-06

MESH = pl.DeviceIdType.MESH
HIGH = lax.Precision.HIGHEST
F32 = jnp.float32
BF16 = jnp.bfloat16
VMEM_LIMIT = 65000000
NB = 32
SUB = 16
TN = (((0,), (0,)), ((), ()))


def split2(x):
    hi = x.astype(BF16)
    return hi, (x - hi.astype(F32)).astype(BF16)


def split3(x):
    hi = x.astype(BF16)
    rest = x - hi.astype(F32)
    mid = rest.astype(BF16)
    return hi, mid, (rest - mid.astype(F32)).astype(BF16)


def sweep_half(a_ref, lt_ref, rt_ref, q_ref, tmp_ref, h):
    rank = a_ref.shape[0]
    parts = rank // 128
    row8 = lax.broadcasted_iota(jnp.int32, (8, 128), 0)
    lane8 = lax.broadcasted_iota(jnp.int32, (8, 128), 1)
    lane = lax.broadcasted_iota(jnp.int32, (NB, rank), 1)
    groups = NB // 8
    wide = SUB // 8
    for t in range(128 // NB):
        l0 = t * NB
        r0 = pl.multiple_of(h * 128 + l0, NB)
        before = (lane >= r0 - NB) & (lane < r0)
        r = jnp.where(before, 0.0, a_ref[pl.ds(r0, NB), :]) - jnp.dot(
            lt_ref[pl.ds(r0, NB), :], rt_ref[...], preferred_element_type=F32
        )
        catch_up(a_ref, lt_ref, rt_ref, q_ref, r0)
        r1, r2, r3 = split3(jnp.where((lane >= r0) & (lane < r0 + NB), 0.0, r))
        lt_ref[...] = jnp.concatenate([r1, r1, r2, r2, r1, r3], axis=0).T
        half = [r[:, 128 * v : 128 * v + 128] for v in range(parts)]
        own = half[0]
        for v in range(1, parts):
            own = jnp.where(h == v, half[v], own)
        half = [own] + [jnp.where(h == v, half[0], half[v]) for v in range(1, parts)]
        x = [[y[8 * m : 8 * m + 8] for y in half] for m in range(groups)]
        for u in range(NB // SUB):
            mine = range(u * wide, (u + 1) * wide)
            rest = [m for m in range(groups) if m not in mine]
            first = l0 + u * SUB
            spread = lambda m, j: jnp.broadcast_to(x[m][0][:, first + j : first + j + 1], (8, 128))
            cols = [{m: spread(m, j) for m in mine} for j in range(SUB)]
            left = {m: [spread(m, j) for j in range(SUB)] for m in rest}
            slot = 0

            def keep(y):
                nonlocal slot
                tmp_ref[slot] = y
                slot += 1
                return slot - 1

            def row_of(where, s):
                return jnp.broadcast_to(tmp_ref[where, s : s + 1, :], (8, 128))

            kept = [{mine[0]: keep(cols[j][mine[0]])} for j in range(SUB)]
            a, c, e = row_of(kept[0][mine[0]], 0), row_of(kept[0][mine[0]], 1), row_of(kept[1][mine[0]], 1)
            for p in range(0, SUB, 2):
                i, s = u * wide + p // 8, p % 8
                i2, s2 = u * wide + (p + 2) // 8, (p + 2) % 8
                det = a * e - c * c
                guess = pl.reciprocal(det, approx=True)
                off = 1.0 - det * guess
                inv = (guess + guess * off) * (1.0 + off * off)

                def combine(yp, yq):
                    return e * yp - c * yq, a * yq - c * yp

                def apply(y, np_, nq_):
                    done = {m: y[m] - (cols[p][m] * np_ + cols[p + 1][m] * nq_) * inv for m in mine}
                    plain = done[i]
                    done[i] = jnp.where(row8 == s, np_ * inv, jnp.where(row8 == s + 1, nq_ * inv, plain))
                    return done, plain

                mixed = {j: combine(row_of(kept[j][i], s), row_of(kept[j][i], s + 1)) for j in range(p + 2, SUB)}
                if p + 2 < SUB:
                    for j in range(p, p + 4):
                        if i2 not in kept[j]:
                            kept[j][i2] = keep(cols[j][i2])
                    (lp0, lp1), (lq0, lq1) = [[row_of(kept[j][i2], s2 + k) for k in (0, 1)] for j in (p, p + 1)]
                    a0, c0 = row_of(kept[p + 2][i2], s2), row_of(kept[p + 2][i2], s2 + 1)
                    e0 = row_of(kept[p + 3][i2], s2 + 1)
                    (np2, nq2), (np3, nq3) = mixed[p + 2], mixed[p + 3]
                    following = (
                        a0 - (lp0 * np2 + lq0 * nq2) * inv,
                        c0 - (lp1 * np2 + lq1 * nq2) * inv,
                        e0 - (lp1 * np3 + lq1 * nq3) * inv,
                    )
                for j in range(p + 2, SUB):
                    cols[j], plain = apply(cols[j], *mixed[j])
                    kept[j] = {i2: keep(plain if i2 == i else cols[j][i2])}
                here = (lane8 == first + p) | (lane8 == first + p + 1)
                unit = jnp.where(lane8 - first - p == row8 - s, -1.0, 0.0)
                for m in mine:
                    x[m][0] = jnp.where(here, unit if m == i else 0.0, x[m][0])
                for v in range(parts):
                    where = keep(x[i][v])
                    done, _ = apply({m: x[m][v] for m in mine}, *combine(row_of(where, s), row_of(where, s + 1)))
                    for m in mine:
                        x[m][v] = done[m]
                if p + 2 < SUB:
                    a, c, e = following
            ours = (lane8 >= first) & (lane8 < first + SUB)
            base = slot
            for m in mine:
                for v in range(parts):
                    tmp_ref[slot] = x[m][v]
                    slot += 1
            for m in rest:
                x[m][0] = jnp.where(ours, 0.0, x[m][0])
                for v in range(parts):
                    terms = [
                        left[m][j] * jnp.broadcast_to(tmp_ref[base + j // 8 * parts + v, j % 8 : j % 8 + 1, :], (8, 128))
                        for j in range(SUB)
                    ]
                    while len(terms) > 1:
                        terms = [terms[k] + terms[k + 1] for k in range(0, len(terms), 2)]
                    x[m][v] = x[m][v] - terms[0]
        half = [jnp.concatenate([x[m][v] for m in range(groups)], axis=0) for v in range(parts)]
        half = [jnp.where(h == 0, half[0], half[1]), jnp.where(h == 0, half[1], half[0])]
        q = jnp.concatenate(half, axis=1)
        q1, q2, q3 = split3(q)
        rt_ref[...] = jnp.concatenate([q1, q2, q1, q2, q3, q1], axis=0)
        q_ref[...] = q


def catch_up(a_ref, lt_ref, rt_ref, q_ref, r0):
    rank = a_ref.shape[0]
    lane = lax.broadcasted_iota(jnp.int32, (rank, rank), 1)
    update = jnp.dot(lt_ref[...], rt_ref[...], preferred_element_type=F32)
    a_ref[...] = jnp.where((lane >= r0 - NB) & (lane < r0), 0.0, a_ref[...]) - update
    a_ref[pl.ds(pl.multiple_of(jnp.maximum(r0 - NB, 0), NB), NB), :] = q_ref[...]


def sweep_begin(a_ref, lt_ref, rt_ref, q_ref, tmp_ref):
    lt_ref[...] = jnp.zeros_like(lt_ref)
    rt_ref[...] = jnp.zeros_like(rt_ref)
    q_ref[...] = a_ref[:NB, :]


def sweep_end(a_ref, lt_ref, rt_ref, q_ref, tmp_ref):
    catch_up(a_ref, lt_ref, rt_ref, q_ref, a_ref.shape[0])


def diagonal(matrix):
    rank = matrix.shape[0]
    eye = lax.broadcasted_iota(jnp.int32, (rank, rank), 0) == lax.broadcasted_iota(jnp.int32, (rank, rank), 1)
    kept = jnp.where(eye, matrix, 0.0)
    return jnp.sum(kept, axis=0, keepdims=True), jnp.sum(kept, axis=1, keepdims=True)


def set_system(a_ref, gram, along, down, gc, gc_along, gc_down):
    rank = gram.shape[0]
    eye = lax.broadcasted_iota(jnp.int32, (rank, rank), 0) == lax.broadcasted_iota(jnp.int32, (rank, rank), 1)
    (g_along, f_along), (g_down, f_down) = along, down
    s_along = lax.rsqrt(g_along * f_along * f_along * gc_along + ridge_term)
    s_down = lax.rsqrt(g_down * f_down * f_down * gc_down + ridge_term)
    scaled = gram * (f_down * s_down) * (f_along * s_along) * gc
    a_ref[...] = scaled + jnp.where(eye, ridge_term * s_along * s_along, 0.0)
    return s_along


def kernel(
    n_x, n_z, total_a, total_b,
    t_hbm, b_hbm, c_hbm,
    hat_a_hbm, w_a_hbm, hat_b_hbm, w_b_hbm,
    hat_a_ref, w_a_ref, hat_b_ref, w_b_ref, b_ref, c_ref, t_f32, t_hi, t_lo, bfull, bst, call, pb, pbc, hs, pby, gb, gc, gca, gcd, ma, ra, pa, pg, gz, gs, ga, sysm, lt, rt, qp, tmp, scl, iw,
    mbt, mb, rb1, mb1, rb2, sq, sqp, sqs, sqz,
    t_sem, out_sem, send_sem, recv_sem,
):
    depth, height, width = t_f32.shape
    rank = c_ref.shape[1]
    ia, ja, ka = lax.axis_index("ia"), lax.axis_index("ja"), lax.axis_index("ka")
    z, yl = lax.div(ia, 2), lax.rem(ia, 2)
    yh, core = lax.div(ja, 2), lax.rem(ja, 2)
    n_s = 4 * n_x
    n_q = 2 * n_s
    n_g = 2 * n_x
    s = ja * n_x + ka
    q = yl * n_s + s
    g = yl * n_x + ka

    yls = [lax.rem(yl + d, 2) for d in range(2)]
    jas = [lax.rem(ja + d, 4) for d in range(4)]
    kas = [lax.rem(ka + d, n_x) for d in range(n_x)]
    zs = [lax.rem(z + d, n_z) for d in range(n_z)]
    ias = [z * 2 + yl2 for yl2 in yls]

    def plane_peer(d):
        y, j, k = d // n_s, d // n_x % 4, d % n_x
        return yls[y] * n_s + jas[j] * n_x + kas[k], (ias[y], jas[j], kas[k])

    def group_peer(d):
        y, k = d // n_x, d % n_x
        return yls[y] * n_x + kas[k], (ias[y], ja, kas[k])

    def share_peer(d):
        j, k = d // n_x, d % n_x
        return jas[j] * n_x + kas[k], (ia, jas[j], kas[k])

    def z_peer(d):
        return zs[d], (zs[d] * 2 + yl, ja, ka)

    def x_peer(d):
        return kas[d], (ia, ja, kas[d])

    def send(stage, src, dst, device):
        pltpu.make_async_remote_copy(
            src_ref=src, dst_ref=dst, send_sem=send_sem.at[stage], recv_sem=recv_sem.at[stage],
            device_id=device, device_id_type=MESH,
        ).start()

    def fan(stage, count, peer, src, dst):
        for d in range(1, count):
            where, device = peer(d)
            send(stage, src(where), dst, device)

    def arrived(stage, ref):
        pltpu.make_async_copy(ref, ref, recv_sem.at[stage]).wait()

    def sent(stage, ref):
        pltpu.make_async_copy(ref, ref, send_sem.at[stage]).wait()

    n_chunk = t_sem.shape[0] - 2
    per = depth // n_chunk
    loads = [
        pltpu.make_async_copy(t_hbm.at[pl.ds(i * per, per)], t_f32.at[pl.ds(i * per, per)], t_sem.at[i])
        for i in range(n_chunk)
    ]
    small = [pltpu.make_async_copy(b_hbm, b_ref, t_sem.at[n_chunk]), pltpu.make_async_copy(c_hbm, c_ref, t_sem.at[n_chunk + 1])]
    for load in small + loads:
        load.start()

    barrier = pltpu.get_barrier_semaphore()

    for count, peer in ((n_z, z_peer), (n_q, plane_peer)):
        for d in range(1, count):
            pl.semaphore_signal(barrier, inc=1, device_id=peer(d)[1], device_id_type=MESH)
    pl.semaphore_wait(barrier, n_q + n_z - 2)

    for load in small:
        load.wait()
    for d in range(1, n_z):
        send(14 + d, b_ref, bfull.at[z, g], z_peer(d)[1])
    fan(2, n_g, group_peer, lambda _: b_ref, bfull.at[z, g])
    fan(1, n_x, x_peer, lambda _: c_ref, call.at[ka])
    bfull[z, g] = b_ref[...]
    call[ka] = c_ref[...]

    def cut(first, last):
        def body(k, carry):
            hi, lo = split2(t_f32[k])
            t_hi[k] = hi
            t_lo[k] = lo
            return carry

        lax.fori_loop(first, last, body, 0)

    for d in sorted(range(1, n_z), key=lambda d: min(d, n_z - d)):
        block = bfull.at[zs[n_z - d], g]
        arrived(14 + d, block)
        fan(2, n_g, group_peer, lambda _: block, block)
    for i in range(n_chunk):
        loads[i].wait()
        cut(i * per, (i + 1) * per)
    if n_x > 1:
        arrived(1, call.at[pl.ds(0, n_x - 1)])
    call_rows = call[...].reshape(n_x * depth, rank)
    gc[...] = lax.dot_general(call_rows, call_rows, TN, precision=HIGH, preferred_element_type=F32)
    gca[...], gcd[...] = diagonal(gc[...])

    arrived(2, bfull.at[:, pl.ds(0, n_g - 1)])
    rows_b = bfull[...].reshape(width, rank)
    pb[...] = lax.dot_general(rows_b, rows_b, TN, precision=HIGH, preferred_element_type=F32).reshape(pb.shape)
    sibling = (ia, ja + 1 - 2 * core, ka)
    across = (z * 2 + 1 - yl, ja + 2 - 4 * yh, ka)
    send(3, pb.at[1 - core], pbc, sibling)
    hi, lo = split2(rows_b)
    bst[...] = jnp.concatenate([hi, lo, hi], axis=0)
    ma[...] = jnp.zeros_like(ma)

    def first_mode(i, carry):
        k0 = i * per
        th = t_hi[pl.ds(k0, per)].reshape(per * height, width)
        tl = t_lo[pl.ds(k0, per)].reshape(per * height, width)
        along = jnp.dot(jnp.concatenate([th, th, tl], axis=1), bst[...], preferred_element_type=F32)
        total = ma[...].reshape(height, rank)
        for j in range(per):
            total = total + along[j * height : (j + 1) * height] * c_ref[pl.ds(k0 + j, 1), :]
        ma[...] = total.reshape(ma.shape)
        return carry

    lax.fori_loop(0, 1, first_mode, 0)
    arrived(3, pbc)
    hs[...] = pb[core] + pbc[...]
    send(4, hs, pby, across)
    lax.fori_loop(1, n_chunk - 1, first_mode, 0)
    arrived(4, pby)
    gb[core] = hs[...] + pby[...]
    send(6, gb.at[core], gb.at[core], sibling)
    lax.fori_loop(n_chunk - 1, n_chunk, first_mode, 0)
    fan(5, n_s, share_peer, lambda where: ma.at[where], ra.at[s])
    ra[s] = ma[s]
    arrived(6, gb.at[0])

    gram_b = gb[...].reshape(rank, rank)
    along, down = diagonal(gram_b)
    scl[...] = set_system(sysm, gram_b, (along, 1.0), (down, 1.0), gc[...], gca[...], gcd[...])
    sweep = (sysm, lt, rt, qp, tmp)

    def half_of(h, carry):
        sweep_half(*sweep, h)
        return carry

    sweep_begin(*sweep)
    lax.fori_loop(0, rank // 128, half_of, 0)
    sweep_end(*sweep)
    arrived(5, ra.at[pl.ds(0, n_s - 1)])
    share_a = jnp.sum(ra[...], axis=0)
    raw_a = -jnp.dot(share_a * scl[...], sysm[...], precision=HIGH, preferred_element_type=F32) * scl[...]

    pa[q] = raw_a
    fan(7, n_q, plane_peer, lambda _: pa.at[q], pa.at[q])
    arrived(7, pa.at[pl.ds(0, n_q - 1)])
    rows_a = pa[...].reshape(n_q * 8, rank)
    pg[...] = lax.dot_general(rows_a, rows_a, TN, precision=HIGH, preferred_element_type=F32).reshape(pg.shape)
    fan(8, n_z, z_peer, lambda _: pg.at[q], gz.at[z])
    gz[z] = pg[q]
    mbt[...] = jnp.zeros_like(mbt)

    def second_mode(i, carry):
        k0 = i * per
        rows = pa[pl.ds(yl * n_s, n_s)].reshape(height, rank)
        both = jnp.concatenate([rows * c_ref[pl.ds(k0 + j, 1), :] for j in range(per)], axis=0)
        hi, lo = split2(both)
        th = t_hi[pl.ds(k0, per)].reshape(per * height, width)
        tl = t_lo[pl.ds(k0, per)].reshape(per * height, width)
        mbt[...] += lax.dot_general(
            jnp.concatenate([hi, lo, hi], axis=0), jnp.concatenate([th, th, tl], axis=0), TN,
            preferred_element_type=F32,
        )
        return carry

    lax.fori_loop(0, 2, second_mode, 0)
    arrived(8, gz.at[pl.ds(0, n_z - 1)])
    gs[...] = jnp.sum(gz[...], axis=0)
    fan(9, n_q, plane_peer, lambda _: gs, ga.at[q])
    ga[q] = gs[...]
    lax.fori_loop(2, n_chunk, second_mode, 0)
    mb[...] = mbt[...].T.reshape(mb.shape)
    fan(10, n_g, group_peer, lambda where: mb.at[:, where], rb1.at[g])
    rb1[g] = mb[:, g]

    arrived(9, ga.at[pl.ds(0, n_q - 1)])
    gram = ga[...].reshape(rank, rank)
    along, down = diagonal(gram)
    weight_a = jnp.sqrt(along * (1.0 / total_a) + epsilon)
    iw[...] = 1.0 / weight_a
    w_a_ref[...] = weight_a
    hat_a_ref[...] = pa[q] / weight_a
    results = [
        pltpu.make_async_copy(have, want, out_sem.at[i])
        for i, (have, want) in enumerate(
            [(hat_a_ref, hat_a_hbm), (w_a_ref, w_a_hbm), (hat_b_ref, hat_b_hbm), (w_b_ref, w_b_hbm)]
        )
    ]
    for result in results[:2]:
        result.start()
    iw_down = 1.0 / jnp.sqrt(down * (1.0 / total_a) + epsilon)
    scl[...] = set_system(sysm, gram, (along, iw[...]), (down, iw_down), gc[...], gca[...], gcd[...])
    sweep_begin(*sweep)

    def half_with_sums(h, carry):
        sweep_half(*sweep, h)

        @pl.when(h == 0)
        def _():
            arrived(10, rb1.at[pl.ds(0, n_g - 1)])
            mb1[...] = jnp.sum(rb1[...], axis=0)
            fan(11, n_z, z_peer, lambda where: mb1.at[where], rb2.at[z])
            rb2[z] = mb1[z]

        return carry

    lax.fori_loop(0, rank // 128, half_with_sums, 0)
    sweep_end(*sweep)
    arrived(11, rb2.at[pl.ds(0, n_z - 1)])
    share_b = jnp.sum(rb2[...], axis=0)
    raw_b = -jnp.dot(share_b * iw[...] * scl[...], sysm[...], precision=HIGH, preferred_element_type=F32) * scl[...]

    sq[...] = jnp.sum(raw_b * raw_b, axis=0, keepdims=True)
    fan(12, n_q, plane_peer, lambda _: sq, sqp.at[q])
    sqp[q] = sq[...]
    arrived(12, sqp.at[pl.ds(0, n_q - 1)])
    sqs[...] = jnp.sum(sqp[...], axis=0)
    fan(13, n_z, z_peer, lambda _: sqs, sqz.at[z])
    sqz[z] = sqs[...]
    arrived(13, sqz.at[pl.ds(0, n_z - 1)])
    weight_b = jnp.sqrt(jnp.sum(sqz[...], axis=0) * (1.0 / total_b) + epsilon)
    w_b_ref[...] = weight_b
    hat_b_ref[...] = raw_b / weight_b
    for result in results[2:]:
        result.start()

    for d in range(1, n_z):
        sent(14 + d, bfull.at[z, g])
    if n_x > 1:
        sent(1, call.at[pl.ds(0, n_x - 1)])
    sent(2, bfull.at[:, pl.ds(0, n_g - 1)])
    sent(3, pbc)
    sent(4, pby)
    sent(5, ra.at[pl.ds(0, n_s - 1)])
    sent(6, gb.at[0])
    sent(7, pa.at[pl.ds(0, n_q - 1)])
    sent(8, gz.at[pl.ds(0, n_z - 1)])
    sent(9, ga.at[pl.ds(0, n_q - 1)])
    sent(10, rb1.at[pl.ds(0, n_g - 1)])
    sent(11, rb2.at[pl.ds(0, n_z - 1)])
    sent(12, sqp.at[pl.ds(0, n_q - 1)])
    sent(13, sqz.at[pl.ds(0, n_z - 1)])
    for result in results:
        result.wait()


def finish(*refs):
    copies = [pltpu.make_async_copy(refs[i], refs[4 + i], refs[8].at[i]) for i in range(4)]
    for copy in copies:
        copy.start()
    for copy in copies:
        copy.wait()


def local(tensor, factor_b, factor_c):
    depth, height, width = tensor.shape
    rank = factor_c.shape[1]
    n_x, n_z = lax.axis_size("ka"), lax.axis_size("ia") // 2
    n_s, n_q, n_g = 4 * n_x, 8 * n_x, 2 * n_x
    part = rank // n_q
    n_chunk = 6
    v = pltpu.VMEM
    out = jax.ShapeDtypeStruct
    hbm = pl.BlockSpec(memory_space=pltpu.HBM)
    results = [out((8, rank), F32), out((1, rank), F32), out((8, rank), F32), out((1, rank), F32)]
    found = pl.pallas_call(
        functools.partial(kernel, n_x, n_z, height * lax.axis_size("ia"), width * lax.axis_size("ja")),
        out_shape=results,
        in_specs=[hbm] * 3,
        out_specs=[hbm] * 4,
        scratch_shapes=[
            v((8, rank), F32),
            v((1, rank), F32),
            v((8, rank), F32),
            v((1, rank), F32),
            v((8, rank), F32),
            v((depth, rank), F32),
            v((depth, height, width), F32),
            v((depth, height, width), BF16),
            v((depth, height, width), BF16),
            v((n_z, n_g, 8, rank), F32),
            v((3 * width, rank), BF16),
            v((n_x, depth, rank), F32),
            v((2, rank // 2, rank), F32),
            v((rank // 2, rank), F32),
            v((rank // 2, rank), F32),
            v((rank // 2, rank), F32),
            v((2, rank // 2, rank), F32),
            v((rank, rank), F32),
            v((1, rank), F32),
            v((rank, 1), F32),
            v((n_s, 8, rank), F32),
            v((n_s, 8, rank), F32),
            v((n_q, 8, rank), F32),
            v((n_q, part, rank), F32),
            v((n_z, part, rank), F32),
            v((part, rank), F32),
            v((n_q, part, rank), F32),
            v((rank, rank), F32),
            v((rank, 6 * NB), BF16),
            v((6 * NB, rank), BF16),
            v((NB, rank), F32),
            v((160, 8, 128), F32),
            v((1, rank), F32),
            v((1, rank), F32),
            v((rank, width), F32),
            v((n_z, n_g, 8, rank), F32),
            v((n_g, n_z, 8, rank), F32),
            v((n_z, 8, rank), F32),
            v((n_z, 8, rank), F32),
            v((1, rank), F32),
            v((n_q, 1, rank), F32),
            v((1, rank), F32),
            v((n_z, 1, rank), F32),
            pltpu.SemaphoreType.DMA((n_chunk + 2,)),
            pltpu.SemaphoreType.DMA((4,)),
            pltpu.SemaphoreType.DMA((14 + n_z,)),
            pltpu.SemaphoreType.DMA((14 + n_z,)),
        ],
        compiler_params=pltpu.CompilerParams(
            collective_id=0, has_side_effects=True, vmem_limit_bytes=VMEM_LIMIT
        ),
    )(tensor, factor_b, factor_c)
    hat_a, weight_a, hat_b, weight_b = pl.pallas_call(
        finish,
        out_shape=results,
        in_specs=[hbm] * 4,
        out_specs=[hbm] * 4,
        scratch_shapes=[pltpu.SemaphoreType.DMA((4,))],
        compiler_params=pltpu.CompilerParams(vmem_limit_bytes=VMEM_LIMIT),
    )(*found)
    return hat_a, weight_a.reshape(rank), hat_b, weight_b.reshape(rank)


def solution(mesh):
    return jax.shard_map(
        local,
        mesh=mesh,
        in_specs=(P("ka", "ia", "ja"), P(("ja", "ia", "ka"), None), P("ka", None)),
        out_specs=(P(("ia", "ja", "ka"), None), P(), P(("ja", "ia", "ka"), None), P()),
        check_vma=False,
    )
```

```python
import functools

import jax
import jax.numpy as jnp
from jax import lax
from jax.experimental import pallas as pl
from jax.experimental.pallas import tpu as pltpu
from jax.sharding import PartitionSpec as P

ridge_term = 0.01
epsilon = 1e-06

MESH = pl.DeviceIdType.MESH
HIGH = lax.Precision.HIGHEST
F32 = jnp.float32
BF16 = jnp.bfloat16
VMEM_LIMIT = 65000000
NB = 32
SUB = 16
TN = (((0,), (0,)), ((), ()))


def split2(x):
    hi = x.astype(BF16)
    return hi, (x - hi.astype(F32)).astype(BF16)


def split3(x):
    hi = x.astype(BF16)
    rest = x - hi.astype(F32)
    mid = rest.astype(BF16)
    return hi, mid, (rest - mid.astype(F32)).astype(BF16)


def sweep_half(a_ref, lt_ref, rt_ref, q_ref, tmp_ref, h):
    rank = a_ref.shape[0]
    parts = rank // 128
    row8 = lax.broadcasted_iota(jnp.int32, (8, 128), 0)
    lane8 = lax.broadcasted_iota(jnp.int32, (8, 128), 1)
    lane = lax.broadcasted_iota(jnp.int32, (NB, rank), 1)
    groups = NB // 8
    wide = SUB // 8
    for t in range(128 // NB):
        l0 = t * NB
        r0 = pl.multiple_of(h * 128 + l0, NB)
        before = (lane >= r0 - NB) & (lane < r0)
        r = jnp.where(before, 0.0, a_ref[pl.ds(r0, NB), :]) - jnp.dot(
            lt_ref[pl.ds(r0, NB), :], rt_ref[...], preferred_element_type=F32
        )
        catch_up(a_ref, lt_ref, rt_ref, q_ref, r0)
        r1, r2, r3 = split3(jnp.where((lane >= r0) & (lane < r0 + NB), 0.0, r))
        half = [r[:, 128 * v : 128 * v + 128] for v in range(parts)]
        own = half[0]
        for v in range(1, parts):
            own = jnp.where(h == v, half[v], own)
        half = [own] + [jnp.where(h == v, half[0], half[v]) for v in range(1, parts)]
        x = [[y[8 * m : 8 * m + 8] for y in half] for m in range(groups)]
        for u in range(NB // SUB):
            mine = range(u * wide, (u + 1) * wide)
            rest = [m for m in range(groups) if m not in mine]
            first = l0 + u * SUB
            spread = lambda m, j: jnp.broadcast_to(x[m][0][:, first + j : first + j + 1], (8, 128))
            cols = [{m: spread(m, j) for m in mine} for j in range(SUB)]
            left = {m: [spread(m, j) for j in range(SUB)] for m in rest}
            slot = 0

            def keep(y):
                nonlocal slot
                tmp_ref[slot] = y
                slot += 1
                return slot - 1

            def row_of(where, s):
                return jnp.broadcast_to(tmp_ref[where, s : s + 1, :], (8, 128))

            kept = [{mine[0]: keep(cols[j][mine[0]])} for j in range(SUB)]
            a, c, e = row_of(kept[0][mine[0]], 0), row_of(kept[0][mine[0]], 1), row_of(kept[1][mine[0]], 1)
            for p in range(0, SUB, 2):
                i, s = u * wide + p // 8, p % 8
                i2, s2 = u * wide + (p + 2) // 8, (p + 2) % 8
                det = a * e - c * c
                guess = pl.reciprocal(det, approx=True)
                off = 1.0 - det * guess
                inv = (guess + guess * off) * (1.0 + off * off)

                def combine(yp, yq):
                    return e * yp - c * yq, a * yq - c * yp

                def apply(y, np_, nq_):
                    done = {m: y[m] - (cols[p][m] * np_ + cols[p + 1][m] * nq_) * inv for m in mine}
                    plain = done[i]
                    done[i] = jnp.where(row8 == s, np_ * inv, jnp.where(row8 == s + 1, nq_ * inv, plain))
                    return done, plain

                mixed = {j: combine(row_of(kept[j][i], s), row_of(kept[j][i], s + 1)) for j in range(p + 2, SUB)}
                if p + 2 < SUB:
                    for j in range(p, p + 4):
                        if i2 not in kept[j]:
                            kept[j][i2] = keep(cols[j][i2])
                    (lp0, lp1), (lq0, lq1) = [[row_of(kept[j][i2], s2 + k) for k in (0, 1)] for j in (p, p + 1)]
                    a0, c0 = row_of(kept[p + 2][i2], s2), row_of(kept[p + 2][i2], s2 + 1)
                    e0 = row_of(kept[p + 3][i2], s2 + 1)
                    (np2, nq2), (np3, nq3) = mixed[p + 2], mixed[p + 3]
                    following = (
                        a0 - (lp0 * np2 + lq0 * nq2) * inv,
                        c0 - (lp1 * np2 + lq1 * nq2) * inv,
                        e0 - (lp1 * np3 + lq1 * nq3) * inv,
                    )
                for j in range(p + 2, SUB):
                    cols[j], plain = apply(cols[j], *mixed[j])
                    kept[j] = {i2: keep(plain if i2 == i else cols[j][i2])}
                here = (lane8 == first + p) | (lane8 == first + p + 1)
                unit = jnp.where(lane8 - first - p == row8 - s, -1.0, 0.0)
                for m in mine:
                    x[m][0] = jnp.where(here, unit if m == i else 0.0, x[m][0])
                for v in range(parts):
                    where = keep(x[i][v])
                    done, _ = apply({m: x[m][v] for m in mine}, *combine(row_of(where, s), row_of(where, s + 1)))
                    for m in mine:
                        x[m][v] = done[m]
                if p + 2 < SUB:
                    a, c, e = following
            ours = (lane8 >= first) & (lane8 < first + SUB)
            base = slot
            for m in mine:
                for v in range(parts):
                    tmp_ref[slot] = x[m][v]
                    slot += 1
            if u == 0:
                lt_ref[...] = jnp.concatenate([r1, r1, r2, r2, r1, r3], axis=0).T
            for m in rest:
                x[m][0] = jnp.where(ours, 0.0, x[m][0])
                for v in range(parts):
                    terms = [
                        left[m][j] * jnp.broadcast_to(tmp_ref[base + j // 8 * parts + v, j % 8 : j % 8 + 1, :], (8, 128))
                        for j in range(SUB)
                    ]
                    while len(terms) > 1:
                        terms = [terms[k] + terms[k + 1] for k in range(0, len(terms), 2)]
                    x[m][v] = x[m][v] - terms[0]
        half = [jnp.concatenate([x[m][v] for m in range(groups)], axis=0) for v in range(parts)]
        half = [jnp.where(h == 0, half[0], half[1]), jnp.where(h == 0, half[1], half[0])]
        q = jnp.concatenate(half, axis=1)
        q1, q2, q3 = split3(q)
        rt_ref[...] = jnp.concatenate([q1, q2, q1, q2, q3, q1], axis=0)
        q_ref[...] = q


def catch_up(a_ref, lt_ref, rt_ref, q_ref, r0):
    rank = a_ref.shape[0]
    lane = lax.broadcasted_iota(jnp.int32, (8, rank), 1)
    done = (lane >= r0 - NB) & (lane < r0)
    update = jnp.dot(lt_ref[...], rt_ref[...], preferred_element_type=F32)
    rest = jnp.where(done[None], 0.0, a_ref[...].reshape(rank // 8, 8, rank))
    a_ref[...] = rest.reshape(rank, rank) - update
    a_ref[pl.ds(pl.multiple_of(jnp.maximum(r0 - NB, 0), NB), NB), :] = q_ref[...]


def sweep_begin(a_ref, lt_ref, rt_ref, q_ref, tmp_ref):
    lt_ref[...] = jnp.zeros_like(lt_ref)
    rt_ref[...] = jnp.zeros_like(rt_ref)
    q_ref[...] = a_ref[:NB, :]


def sweep_end(a_ref, lt_ref, rt_ref, q_ref, tmp_ref):
    catch_up(a_ref, lt_ref, rt_ref, q_ref, a_ref.shape[0])


def diagonal(matrix):
    rank = matrix.shape[0]
    eye = lax.broadcasted_iota(jnp.int32, (rank, rank), 0) == lax.broadcasted_iota(jnp.int32, (rank, rank), 1)
    kept = jnp.where(eye, matrix, 0.0)
    return jnp.sum(kept, axis=0, keepdims=True), jnp.sum(kept, axis=1, keepdims=True)


def set_system(a_ref, gram, along, down, gc, gc_along, gc_down):
    rank = gram.shape[0]
    eye = lax.broadcasted_iota(jnp.int32, (rank, rank), 0) == lax.broadcasted_iota(jnp.int32, (rank, rank), 1)
    (g_along, f_along), (g_down, f_down) = along, down
    s_along = lax.rsqrt(g_along * f_along * f_along * gc_along + ridge_term)
    s_down = lax.rsqrt(g_down * f_down * f_down * gc_down + ridge_term)
    scaled = gram * (f_down * s_down) * (f_along * s_along) * gc
    a_ref[...] = scaled + jnp.where(eye, ridge_term * s_along * s_along, 0.0)
    return s_along


def kernel(
    n_x, n_z, total_a, total_b,
    t_hbm, b_hbm, c_hbm,
    hat_a_hbm, w_a_hbm, hat_b_hbm, w_b_hbm,
    hat_a_ref, w_a_ref, hat_b_ref, w_b_ref, b_ref, c_ref, t_f32, t_hi, t_lo, bfull, bst, call, pb, pbc, hs, pby, gb, gc, gca, gcd, ma, ra, pa, pg, gz, gs, ga, sysm, lt, rt, qp, tmp, scl, iw,
    at, ctb, mbt, mb, rb1, mb1, rb2, sq, sqp, sqs, sqz,
    t_sem, out_sem, send_sem, recv_sem,
):
    depth, height, width = t_f32.shape
    rank = c_ref.shape[1]
    ia, ja, ka = lax.axis_index("ia"), lax.axis_index("ja"), lax.axis_index("ka")
    z, yl = lax.div(ia, 2), lax.rem(ia, 2)
    yh, core = lax.div(ja, 2), lax.rem(ja, 2)
    n_s = 4 * n_x
    n_q = 2 * n_s
    n_g = 2 * n_x
    s = ja * n_x + ka
    q = yl * n_s + s
    g = yl * n_x + ka

    yls = [lax.rem(yl + d, 2) for d in range(2)]
    jas = [lax.rem(ja + d, 4) for d in range(4)]
    kas = [lax.rem(ka + d, n_x) for d in range(n_x)]
    zs = [lax.rem(z + d, n_z) for d in range(n_z)]
    ias = [z * 2 + yl2 for yl2 in yls]

    def plane_peer(d):
        y, j, k = d // n_s, d // n_x % 4, d % n_x
        return yls[y] * n_s + jas[j] * n_x + kas[k], (ias[y], jas[j], kas[k])

    def group_peer(d):
        y, k = d // n_x, d % n_x
        return yls[y] * n_x + kas[k], (ias[y], ja, kas[k])

    def share_peer(d):
        j, k = d // n_x, d % n_x
        return jas[j] * n_x + kas[k], (ia, jas[j], kas[k])

    def z_peer(d):
        return zs[d], (zs[d] * 2 + yl, ja, ka)

    def x_peer(d):
        return kas[d], (ia, ja, kas[d])

    def send(stage, src, dst, device):
        pltpu.make_async_remote_copy(
            src_ref=src, dst_ref=dst, send_sem=send_sem.at[stage], recv_sem=recv_sem.at[stage],
            device_id=device, device_id_type=MESH,
        ).start()

    def fan(stage, count, peer, src, dst):
        for d in range(1, count):
            where, device = peer(d)
            send(stage, src(where), dst, device)

    def arrived(stage, ref):
        pltpu.make_async_copy(ref, ref, recv_sem.at[stage]).wait()

    def sent(stage, ref):
        pltpu.make_async_copy(ref, ref, send_sem.at[stage]).wait()

    n_chunk = t_sem.shape[0] - 2
    per = depth // n_chunk
    loads = [
        pltpu.make_async_copy(t_hbm.at[pl.ds(i * per, per)], t_f32.at[pl.ds(i * per, per)], t_sem.at[i])
        for i in range(n_chunk)
    ]
    small = [pltpu.make_async_copy(b_hbm, b_ref, t_sem.at[n_chunk]), pltpu.make_async_copy(c_hbm, c_ref, t_sem.at[n_chunk + 1])]
    for load in small + loads:
        load.start()

    barrier = pltpu.get_barrier_semaphore()

    for count, peer in ((n_z, z_peer), (n_q, plane_peer)):
        for d in range(1, count):
            pl.semaphore_signal(barrier, inc=1, device_id=peer(d)[1], device_id_type=MESH)
    pl.semaphore_wait(barrier, n_q + n_z - 2)

    for load in small:
        load.wait()
    for d in range(1, n_z):
        send(14 + d, b_ref, bfull.at[z, g], z_peer(d)[1])
    fan(2, n_g, group_peer, lambda _: b_ref, bfull.at[z, g])
    fan(1, n_x, x_peer, lambda _: c_ref, call.at[ka])
    bfull[z, g] = b_ref[...]
    call[ka] = c_ref[...]

    ct = jnp.concatenate([c_ref[...], jnp.zeros((128 - depth, rank), F32)], axis=0).T
    for k in range(depth):
        ctb[k] = jnp.broadcast_to(ct[:, k : k + 1], (rank, height))

    def cut(first, last):
        def body(k, carry):
            hi, lo = split2(t_f32[k])
            t_hi[k] = hi
            t_lo[k] = lo
            return carry

        lax.fori_loop(first, last, body, 0)

    for d in sorted(range(1, n_z), key=lambda d: min(d, n_z - d)):
        block = bfull.at[zs[n_z - d], g]
        arrived(14 + d, block)
        fan(2, n_g, group_peer, lambda _: block, block)
    for i in range(n_chunk):
        loads[i].wait()
        cut(i * per, (i + 1) * per)
    if n_x > 1:
        arrived(1, call.at[pl.ds(0, n_x - 1)])
    call_rows = call[...].reshape(n_x * depth, rank)
    gc[...] = lax.dot_general(call_rows, call_rows, TN, precision=HIGH, preferred_element_type=F32)
    gca[...], gcd[...] = diagonal(gc[...])

    arrived(2, bfull.at[:, pl.ds(0, n_g - 1)])
    rows_b = bfull[...].reshape(width, rank)
    side = rank // 2
    upper = lax.dot_general(rows_b[:, :side], rows_b, TN, precision=HIGH, preferred_element_type=F32)
    corner = lax.dot_general(rows_b[:, side:], rows_b[:, side:], TN, precision=HIGH, preferred_element_type=F32)
    pb[...] = jnp.concatenate([upper[:, :side], upper[:, side:], corner], axis=0).reshape(pb.shape)
    sibling = (ia, ja + 1 - 2 * core, ka)
    across = (z * 2 + 1 - yl, ja + 2 - 4 * yh, ka)
    send(3, pb.at[1 - core], pbc, sibling)
    hi, lo = split2(rows_b)
    bst[...] = jnp.concatenate([hi, lo, hi], axis=0)
    ma[...] = jnp.zeros_like(ma)

    def first_mode(i, carry):
        k0 = i * per
        th = t_hi[pl.ds(k0, per)].reshape(per * height, width)
        tl = t_lo[pl.ds(k0, per)].reshape(per * height, width)
        along = jnp.dot(jnp.concatenate([th, th, tl], axis=1), bst[...], preferred_element_type=F32)
        total = ma[...].reshape(height, rank)
        for j in range(per):
            total = total + along[j * height : (j + 1) * height] * c_ref[pl.ds(k0 + j, 1), :]
        ma[...] = total.reshape(ma.shape)
        return carry

    lax.fori_loop(0, 1, first_mode, 0)
    arrived(3, pbc)
    hs[...] = pb[core] + pbc[...]
    send(4, hs, pby, across)
    lax.fori_loop(1, n_chunk - 1, first_mode, 0)
    arrived(4, pby)
    gb[core] = hs[...] + pby[...]
    send(6, gb.at[core], gb.at[core], sibling)
    lax.fori_loop(n_chunk - 1, n_chunk, first_mode, 0)
    fan(5, n_s, share_peer, lambda where: ma.at[where], ra.at[s])
    ra[s] = ma[s]
    arrived(6, gb.at[0])

    blocks = gb[...].reshape(3 * side, side)
    gram_b = jnp.concatenate(
        [
            jnp.concatenate([blocks[:side], blocks[side : 2 * side]], axis=1),
            jnp.concatenate([blocks[side : 2 * side].T, blocks[2 * side :]], axis=1),
        ],
        axis=0,
    )
    along, down = diagonal(gram_b)
    scl[...] = set_system(sysm, gram_b, (along, 1.0), (down, 1.0), gc[...], gca[...], gcd[...])
    sweep = (sysm, lt, rt, qp, tmp)

    def half_of(h, carry):
        sweep_half(*sweep, h)
        return carry

    sweep_begin(*sweep)
    lax.fori_loop(0, rank // 128, half_of, 0)
    sweep_end(*sweep)
    arrived(5, ra.at[pl.ds(0, n_s - 1)])
    share_a = jnp.sum(ra[...], axis=0)
    raw_a = -jnp.dot(share_a * scl[...], sysm[...], precision=HIGH, preferred_element_type=F32) * scl[...]

    pa[q] = raw_a
    fan(7, n_q, plane_peer, lambda _: pa.at[q], pa.at[q])
    arrived(7, pa.at[pl.ds(0, n_q - 1)])
    rows_a = pa[...].reshape(n_q * 8, rank)
    pg[...] = lax.dot_general(rows_a, rows_a, TN, precision=HIGH, preferred_element_type=F32).reshape(pg.shape)
    fan(8, n_z, z_peer, lambda _: pg.at[q], gz.at[z])
    gz[z] = pg[q]
    mbt[...] = jnp.zeros_like(mbt)

    at[...] = pa[pl.ds(yl * n_s, n_s)].reshape(height, rank).T

    def second_mode(i, carry):
        k0 = i * per
        hi, lo = zip(*[split2(at[...] * ctb[k0 + j]) for j in range(per)])
        th = t_hi[pl.ds(k0, per)].reshape(per * height, width)
        tl = t_lo[pl.ds(k0, per)].reshape(per * height, width)
        mbt[...] += jnp.dot(
            jnp.concatenate(hi + lo + hi, axis=1), jnp.concatenate([th, th, tl], axis=0), preferred_element_type=F32
        )
        return carry

    lax.fori_loop(0, 2, second_mode, 0)
    arrived(8, gz.at[pl.ds(0, n_z - 1)])
    gs[...] = jnp.sum(gz[...], axis=0)
    fan(9, n_q, plane_peer, lambda _: gs, ga.at[q])
    ga[q] = gs[...]
    lax.fori_loop(2, n_chunk, second_mode, 0)
    mb[...] = mbt[...].T.reshape(mb.shape)
    fan(10, n_g, group_peer, lambda where: mb.at[:, where], rb1.at[g])
    rb1[g] = mb[:, g]

    arrived(9, ga.at[pl.ds(0, n_q - 1)])
    gram = ga[...].reshape(rank, rank)
    along, down = diagonal(gram)
    weight_a = jnp.sqrt(along * (1.0 / total_a) + epsilon)
    iw[...] = 1.0 / weight_a
    w_a_ref[...] = weight_a
    hat_a_ref[...] = pa[q] / weight_a
    results = [
        pltpu.make_async_copy(have, want, out_sem.at[i])
        for i, (have, want) in enumerate(
            [(hat_a_ref, hat_a_hbm), (w_a_ref, w_a_hbm), (hat_b_ref, hat_b_hbm), (w_b_ref, w_b_hbm)]
        )
    ]
    for result in results[:2]:
        result.start()
    iw_down = 1.0 / jnp.sqrt(down * (1.0 / total_a) + epsilon)
    scl[...] = set_system(sysm, gram, (along, iw[...]), (down, iw_down), gc[...], gca[...], gcd[...])
    sweep_begin(*sweep)

    def half_with_sums(h, carry):
        sweep_half(*sweep, h)

        @pl.when(h == 0)
        def _():
            arrived(10, rb1.at[pl.ds(0, n_g - 1)])
            mb1[...] = jnp.sum(rb1[...], axis=0)
            fan(11, n_z, z_peer, lambda where: mb1.at[where], rb2.at[z])
            rb2[z] = mb1[z]

        return carry

    lax.fori_loop(0, rank // 128, half_with_sums, 0)
    sweep_end(*sweep)
    arrived(11, rb2.at[pl.ds(0, n_z - 1)])
    share_b = jnp.sum(rb2[...], axis=0)
    raw_b = -jnp.dot(share_b * iw[...] * scl[...], sysm[...], precision=HIGH, preferred_element_type=F32) * scl[...]

    sq[...] = jnp.sum(raw_b * raw_b, axis=0, keepdims=True)
    fan(12, n_q, plane_peer, lambda _: sq, sqp.at[q])
    sqp[q] = sq[...]
    arrived(12, sqp.at[pl.ds(0, n_q - 1)])
    sqs[...] = jnp.sum(sqp[...], axis=0)
    fan(13, n_z, z_peer, lambda _: sqs, sqz.at[z])
    sqz[z] = sqs[...]
    arrived(13, sqz.at[pl.ds(0, n_z - 1)])
    weight_b = jnp.sqrt(jnp.sum(sqz[...], axis=0) * (1.0 / total_b) + epsilon)
    w_b_ref[...] = weight_b
    hat_b_ref[...] = raw_b / weight_b
    for result in results[2:]:
        result.start()

    for d in range(1, n_z):
        sent(14 + d, bfull.at[z, g])
    if n_x > 1:
        sent(1, call.at[pl.ds(0, n_x - 1)])
    sent(2, bfull.at[:, pl.ds(0, n_g - 1)])
    sent(3, pbc)
    sent(4, pby)
    sent(5, ra.at[pl.ds(0, n_s - 1)])
    sent(6, gb.at[0])
    sent(7, pa.at[pl.ds(0, n_q - 1)])
    sent(8, gz.at[pl.ds(0, n_z - 1)])
    sent(9, ga.at[pl.ds(0, n_q - 1)])
    sent(10, rb1.at[pl.ds(0, n_g - 1)])
    sent(11, rb2.at[pl.ds(0, n_z - 1)])
    sent(12, sqp.at[pl.ds(0, n_q - 1)])
    sent(13, sqz.at[pl.ds(0, n_z - 1)])
    for result in results:
        result.wait()


def finish(*refs):
    copies = [pltpu.make_async_copy(refs[i], refs[4 + i], refs[8].at[i]) for i in range(4)]
    for copy in copies:
        copy.start()
    for copy in copies:
        copy.wait()


def local(tensor, factor_b, factor_c):
    depth, height, width = tensor.shape
    rank = factor_c.shape[1]
    n_x, n_z = lax.axis_size("ka"), lax.axis_size("ia") // 2
    n_s, n_q, n_g = 4 * n_x, 8 * n_x, 2 * n_x
    part = rank // n_q
    n_chunk = 6
    v = pltpu.VMEM
    out = jax.ShapeDtypeStruct
    hbm = pl.BlockSpec(memory_space=pltpu.HBM)
    results = [out((8, rank), F32), out((1, rank), F32), out((8, rank), F32), out((1, rank), F32)]
    found = pl.pallas_call(
        functools.partial(kernel, n_x, n_z, height * lax.axis_size("ia"), width * lax.axis_size("ja")),
        out_shape=results,
        in_specs=[hbm] * 3,
        out_specs=[hbm] * 4,
        scratch_shapes=[
            v((8, rank), F32),
            v((1, rank), F32),
            v((8, rank), F32),
            v((1, rank), F32),
            v((8, rank), F32),
            v((depth, rank), F32),
            v((depth, height, width), F32),
            v((depth, height, width), BF16),
            v((depth, height, width), BF16),
            v((n_z, n_g, 8, rank), F32),
            v((3 * width, rank), BF16),
            v((n_x, depth, rank), F32),
            v((2, 3 * rank // 4, rank // 2), F32),
            v((3 * rank // 4, rank // 2), F32),
            v((3 * rank // 4, rank // 2), F32),
            v((3 * rank // 4, rank // 2), F32),
            v((2, 3 * rank // 4, rank // 2), F32),
            v((rank, rank), F32),
            v((1, rank), F32),
            v((rank, 1), F32),
            v((n_s, 8, rank), F32),
            v((n_s, 8, rank), F32),
            v((n_q, 8, rank), F32),
            v((n_q, part, rank), F32),
            v((n_z, part, rank), F32),
            v((part, rank), F32),
            v((n_q, part, rank), F32),
            v((rank, rank), F32),
            v((rank, 6 * NB), BF16),
            v((6 * NB, rank), BF16),
            v((NB, rank), F32),
            v((160, 8, 128), F32),
            v((1, rank), F32),
            v((1, rank), F32),
            v((rank, height), F32),
            v((depth, rank, height), F32),
            v((rank, width), F32),
            v((n_z, n_g, 8, rank), F32),
            v((n_g, n_z, 8, rank), F32),
            v((n_z, 8, rank), F32),
            v((n_z, 8, rank), F32),
            v((1, rank), F32),
            v((n_q, 1, rank), F32),
            v((1, rank), F32),
            v((n_z, 1, rank), F32),
            pltpu.SemaphoreType.DMA((n_chunk + 2,)),
            pltpu.SemaphoreType.DMA((4,)),
            pltpu.SemaphoreType.DMA((14 + n_z,)),
            pltpu.SemaphoreType.DMA((14 + n_z,)),
        ],
        compiler_params=pltpu.CompilerParams(
            collective_id=0, has_side_effects=True, vmem_limit_bytes=VMEM_LIMIT
        ),
    )(tensor, factor_b, factor_c)
    hat_a, weight_a, hat_b, weight_b = pl.pallas_call(
        finish,
        out_shape=results,
        in_specs=[hbm] * 4,
        out_specs=[hbm] * 4,
        scratch_shapes=[pltpu.SemaphoreType.DMA((4,))],
        compiler_params=pltpu.CompilerParams(vmem_limit_bytes=VMEM_LIMIT),
    )(*found)
    return hat_a, weight_a.reshape(rank), hat_b, weight_b.reshape(rank)


def solution(mesh):
    return jax.shard_map(
        local,
        mesh=mesh,
        in_specs=(P("ka", "ia", "ja"), P(("ja", "ia", "ka"), None), P("ka", None)),
        out_specs=(P(("ia", "ja", "ka"), None), P(), P(("ja", "ia", "ka"), None), P()),
        check_vma=False,
    )
```

```python
import functools

import jax
import jax.numpy as jnp
from jax import lax
from jax.experimental import pallas as pl
from jax.experimental.pallas import tpu as pltpu
from jax.sharding import PartitionSpec as P

ridge_term = 0.01
epsilon = 1e-06

MESH = pl.DeviceIdType.MESH
HIGH = lax.Precision.HIGHEST
F32 = jnp.float32
BF16 = jnp.bfloat16
VMEM_LIMIT = 65000000
NB = 32
SUB = 16
TN = (((0,), (0,)), ((), ()))


def split2(x):
    hi = x.astype(BF16)
    return hi, (x - hi.astype(F32)).astype(BF16)


def split3(x):
    hi = x.astype(BF16)
    rest = x - hi.astype(F32)
    mid = rest.astype(BF16)
    return hi, mid, (rest - mid.astype(F32)).astype(BF16)


def sweep_half(a_ref, lt_ref, rt_ref, q_ref, tmp_ref, h):
    rank = a_ref.shape[0]
    parts = rank // 128
    row8 = lax.broadcasted_iota(jnp.int32, (8, 128), 0)
    lane8 = lax.broadcasted_iota(jnp.int32, (8, 128), 1)
    lane = lax.broadcasted_iota(jnp.int32, (NB, rank), 1)
    groups = NB // 8
    wide = SUB // 8
    for t in range(128 // NB):
        l0 = t * NB
        r0 = pl.multiple_of(h * 128 + l0, NB)
        before = (lane >= r0 - NB) & (lane < r0)
        r = jnp.where(before, 0.0, a_ref[pl.ds(r0, NB), :]) - jnp.dot(
            lt_ref[pl.ds(r0, NB), :], rt_ref[...], preferred_element_type=F32
        )
        catch_up(a_ref, lt_ref, rt_ref, q_ref, r0)
        r1, r2, r3 = split3(jnp.where((lane >= r0) & (lane < r0 + NB), 0.0, r))
        half = [r[:, 128 * v : 128 * v + 128] for v in range(parts)]
        own = half[0]
        for v in range(1, parts):
            own = jnp.where(h == v, half[v], own)
        half = [own] + [jnp.where(h == v, half[0], half[v]) for v in range(1, parts)]
        x = [[y[8 * m : 8 * m + 8] for y in half] for m in range(groups)]
        for u in range(NB // SUB):
            mine = range(u * wide, (u + 1) * wide)
            rest = [m for m in range(groups) if m not in mine]
            first = l0 + u * SUB
            spread = lambda m, j: jnp.broadcast_to(x[m][0][:, first + j : first + j + 1], (8, 128))
            cols = [{m: spread(m, j) for m in mine} for j in range(SUB)]
            left = {m: [spread(m, j) for j in range(SUB)] for m in rest}
            slot = 0

            def keep(y):
                nonlocal slot
                tmp_ref[slot] = y
                slot += 1
                return slot - 1

            def row_of(where, s):
                return jnp.broadcast_to(tmp_ref[where, s : s + 1, :], (8, 128))

            kept = [{mine[0]: keep(cols[j][mine[0]])} for j in range(SUB)]
            a, c, e = row_of(kept[0][mine[0]], 0), row_of(kept[0][mine[0]], 1), row_of(kept[1][mine[0]], 1)
            for p in range(0, SUB, 2):
                i, s = u * wide + p // 8, p % 8
                i2, s2 = u * wide + (p + 2) // 8, (p + 2) % 8
                det = a * e - c * c
                guess = pl.reciprocal(det, approx=True)
                off = 1.0 - det * guess
                inv = (guess + guess * off) * (1.0 + off * off)

                def combine(yp, yq):
                    return e * yp - c * yq, a * yq - c * yp

                def apply(y, np_, nq_):
                    done = {m: y[m] - (cols[p][m] * np_ + cols[p + 1][m] * nq_) * inv for m in mine}
                    plain = done[i]
                    done[i] = jnp.where(row8 == s, np_ * inv, jnp.where(row8 == s + 1, nq_ * inv, plain))
                    return done, plain

                mixed = {j: combine(row_of(kept[j][i], s), row_of(kept[j][i], s + 1)) for j in range(p + 2, SUB)}
                if p + 2 < SUB:
                    for j in range(p, p + 4):
                        if i2 not in kept[j]:
                            kept[j][i2] = keep(cols[j][i2])
                    (lp0, lp1), (lq0, lq1) = [[row_of(kept[j][i2], s2 + k) for k in (0, 1)] for j in (p, p + 1)]
                    a0, c0 = row_of(kept[p + 2][i2], s2), row_of(kept[p + 2][i2], s2 + 1)
                    e0 = row_of(kept[p + 3][i2], s2 + 1)
                    (np2, nq2), (np3, nq3) = mixed[p + 2], mixed[p + 3]
                    following = (
                        a0 - (lp0 * np2 + lq0 * nq2) * inv,
                        c0 - (lp1 * np2 + lq1 * nq2) * inv,
                        e0 - (lp1 * np3 + lq1 * nq3) * inv,
                    )
                for j in range(p + 2, SUB):
                    cols[j], plain = apply(cols[j], *mixed[j])
                    kept[j] = {i2: keep(plain if i2 == i else cols[j][i2])}
                here = (lane8 == first + p) | (lane8 == first + p + 1)
                unit = jnp.where(lane8 - first - p == row8 - s, -1.0, 0.0)
                for m in mine:
                    x[m][0] = jnp.where(here, unit if m == i else 0.0, x[m][0])
                for v in range(parts):
                    where = keep(x[i][v])
                    done, _ = apply({m: x[m][v] for m in mine}, *combine(row_of(where, s), row_of(where, s + 1)))
                    for m in mine:
                        x[m][v] = done[m]
                if p + 2 < SUB:
                    a, c, e = following
            ours = (lane8 >= first) & (lane8 < first + SUB)
            base = slot
            for m in mine:
                for v in range(parts):
                    tmp_ref[slot] = x[m][v]
                    slot += 1
            if u == 0:
                lt_ref[...] = jnp.concatenate([r1, r1, r2, r2, r1, r3], axis=0).T
            for m in rest:
                x[m][0] = jnp.where(ours, 0.0, x[m][0])
                for v in range(parts):
                    terms = [
                        left[m][j] * jnp.broadcast_to(tmp_ref[base + j // 8 * parts + v, j % 8 : j % 8 + 1, :], (8, 128))
                        for j in range(SUB)
                    ]
                    while len(terms) > 1:
                        terms = [terms[k] + terms[k + 1] for k in range(0, len(terms), 2)]
                    x[m][v] = x[m][v] - terms[0]
        half = [jnp.concatenate([x[m][v] for m in range(groups)], axis=0) for v in range(parts)]
        half = [jnp.where(h == 0, half[0], half[1]), jnp.where(h == 0, half[1], half[0])]
        q = jnp.concatenate(half, axis=1)
        q1, q2, q3 = split3(q)
        rt_ref[...] = jnp.concatenate([q1, q2, q1, q2, q3, q1], axis=0)
        q_ref[...] = q


def catch_up(a_ref, lt_ref, rt_ref, q_ref, r0):
    rank = a_ref.shape[0]
    lane = lax.broadcasted_iota(jnp.int32, (8, rank), 1)
    done = (lane >= r0 - NB) & (lane < r0)
    update = jnp.dot(lt_ref[...], rt_ref[...], preferred_element_type=F32)
    rest = jnp.where(done[None], 0.0, a_ref[...].reshape(rank // 8, 8, rank))
    a_ref[...] = rest.reshape(rank, rank) - update
    a_ref[pl.ds(pl.multiple_of(jnp.maximum(r0 - NB, 0), NB), NB), :] = q_ref[...]


def sweep_begin(a_ref, lt_ref, rt_ref, q_ref, tmp_ref):
    lt_ref[...] = jnp.zeros_like(lt_ref)
    rt_ref[...] = jnp.zeros_like(rt_ref)
    q_ref[...] = a_ref[:NB, :]


def sweep_end(a_ref, lt_ref, rt_ref, q_ref, tmp_ref):
    catch_up(a_ref, lt_ref, rt_ref, q_ref, a_ref.shape[0])


def diagonal(matrix):
    rank = matrix.shape[0]
    eye = lax.broadcasted_iota(jnp.int32, (rank, rank), 0) == lax.broadcasted_iota(jnp.int32, (rank, rank), 1)
    kept = jnp.where(eye, matrix, 0.0)
    return jnp.sum(kept, axis=0, keepdims=True), jnp.sum(kept, axis=1, keepdims=True)


def set_system(a_ref, gram, along, down, gc, gc_along, gc_down):
    rank = gram.shape[0]
    eye = lax.broadcasted_iota(jnp.int32, (rank, rank), 0) == lax.broadcasted_iota(jnp.int32, (rank, rank), 1)
    (g_along, f_along), (g_down, f_down) = along, down
    s_along = lax.rsqrt(g_along * f_along * f_along * gc_along + ridge_term)
    s_down = lax.rsqrt(g_down * f_down * f_down * gc_down + ridge_term)
    scaled = gram * (f_down * s_down) * (f_along * s_along) * gc
    a_ref[...] = scaled + jnp.where(eye, ridge_term * s_along * s_along, 0.0)
    return s_along


def kernel(
    n_x, n_z, total_a, total_b,
    t_hbm, b_hbm, c_hbm,
    hat_a_hbm, w_a_hbm, hat_b_hbm, w_b_hbm,
    hat_a_ref, w_a_ref, hat_b_ref, w_b_ref, b_ref, c_ref, t_f32, t_hi, t_lo, bfull, bst, call, pb, pbc, hs, pby, gb, gc, gca, gcd, ma, ra, pa, pg, gz, ga, sysm, lt, rt, qp, tmp, scl, iw,
    at, ctb, mbt, mb, rb1, mb1, rb2, sqp, sqz,
    t_sem, out_sem, send_sem, recv_sem,
):
    depth, height, width = t_f32.shape
    rank = c_ref.shape[1]
    ia, ja, ka = lax.axis_index("ia"), lax.axis_index("ja"), lax.axis_index("ka")
    z, yl = lax.div(ia, 2), lax.rem(ia, 2)
    yh, core = lax.div(ja, 2), lax.rem(ja, 2)
    n_s = 4 * n_x
    n_q = 2 * n_s
    n_p = n_s
    n_g = 2 * n_x
    s = ja * n_x + ka
    q = core * n_p + (yl * 2 + yh) * n_x + ka
    g = yl * n_x + ka

    yls = [lax.rem(yl + d, 2) for d in range(2)]
    jas = [lax.rem(ja + d, 4) for d in range(4)]
    kas = [lax.rem(ka + d, n_x) for d in range(n_x)]
    zs = [lax.rem(z + d, n_z) for d in range(n_z)]
    ias = [z * 2 + yl2 for yl2 in yls]

    def plane_peer(d):
        y, j, k = d // (2 * n_x), d // n_x % 2, d % n_x
        return None, (ias[y], jas[2 * j], kas[k])

    def group_peer(d):
        y, k = d // n_x, d % n_x
        return yls[y] * n_x + kas[k], (ias[y], ja, kas[k])

    def share_peer(d):
        j, k = d // n_x, d % n_x
        return jas[j] * n_x + kas[k], (ia, jas[j], kas[k])

    def z_peer(d):
        return zs[d], (zs[d] * 2 + yl, ja, ka)

    def line_peer(d):
        c, k = d // n_z, d % n_z
        return None, (zs[k] * 2 + yl, ja + c * (1 - 2 * core), ka)

    def x_peer(d):
        return kas[d], (ia, ja, kas[d])

    def send(stage, src, dst, device):
        pltpu.make_async_remote_copy(
            src_ref=src, dst_ref=dst, send_sem=send_sem.at[stage], recv_sem=recv_sem.at[stage],
            device_id=device, device_id_type=MESH,
        ).start()

    def fan(stage, count, peer, src, dst):
        for d in range(1, count):
            where, device = peer(d)
            send(stage, src(where), dst, device)

    def arrived(stage, ref):
        pltpu.make_async_copy(ref, ref, recv_sem.at[stage]).wait()

    def sent(stage, ref):
        pltpu.make_async_copy(ref, ref, send_sem.at[stage]).wait()

    sibling = (ia, ja + 1 - 2 * core, ka)
    across = (z * 2 + 1 - yl, ja + 2 - 4 * yh, ka)

    def over_chips(stage, buf):
        fan(stage, n_p, plane_peer, lambda _: buf.at[q], buf.at[q])

    def over_cores(stage, forward, buf):
        arrived(stage, buf.at[pl.ds(0, n_p - 1)])
        ours = buf.at[pl.ds(core * n_p, n_p)]
        send(forward, ours, ours, sibling)

    n_chunk = t_sem.shape[0] - 2
    per = depth // n_chunk
    loads = [
        pltpu.make_async_copy(t_hbm.at[pl.ds(i * per, per)], t_f32.at[pl.ds(i * per, per)], t_sem.at[i])
        for i in range(n_chunk)
    ]
    small = [pltpu.make_async_copy(b_hbm, b_ref, t_sem.at[n_chunk]), pltpu.make_async_copy(c_hbm, c_ref, t_sem.at[n_chunk + 1])]
    for load in small + loads:
        load.start()

    barrier = pltpu.get_barrier_semaphore()

    greeted = [line_peer(d) for d in range(1, 2 * n_z) if d != n_z] + [plane_peer(d) for d in range(1, n_p)]
    greeted += [share_peer(d) for d in range(n_s) if d // n_x % 2]
    for _, device in greeted:
        pl.semaphore_signal(barrier, inc=1, device_id=device, device_id_type=MESH)
    pl.semaphore_wait(barrier, len(greeted))

    for load in small:
        load.wait()
    for d in range(1, n_z):
        send(14 + d, b_ref, bfull.at[z, g], z_peer(d)[1])
    fan(1, n_x, x_peer, lambda _: c_ref, call.at[ka])
    bfull[z, g] = b_ref[...]
    call[ka] = c_ref[...]

    ct = jnp.concatenate([c_ref[...], jnp.zeros((128 - depth, rank), F32)], axis=0).T
    for k in range(depth):
        ctb[k] = jnp.broadcast_to(ct[:, k : k + 1], (rank, height))

    def cut(first, last):
        def body(k, carry):
            hi, lo = split2(t_f32[k])
            t_hi[k] = hi
            t_lo[k] = lo
            return carry

        lax.fori_loop(first, last, body, 0)

    for d in range(1, n_z):
        arrived(14 + d, bfull.at[zs[n_z - d], g])
    fan(2, n_g, group_peer, lambda _: bfull.at[:, g], bfull.at[:, g])
    for i in range(n_chunk):
        loads[i].wait()
        cut(i * per, (i + 1) * per)
    if n_x > 1:
        arrived(1, call.at[pl.ds(0, n_x - 1)])
    call_rows = call[...].reshape(n_x * depth, rank)
    gc[...] = lax.dot_general(call_rows, call_rows, TN, precision=HIGH, preferred_element_type=F32)
    gca[...], gcd[...] = diagonal(gc[...])

    arrived(2, bfull.at[:, pl.ds(0, n_g - 1)])
    rows_b = bfull[...].reshape(width, rank)
    side = rank // 2
    upper = lax.dot_general(rows_b[:, :side], rows_b, TN, precision=HIGH, preferred_element_type=F32)
    corner = lax.dot_general(rows_b[:, side:], rows_b[:, side:], TN, precision=HIGH, preferred_element_type=F32)
    pb[...] = jnp.concatenate([upper[:, :side], upper[:, side:], corner], axis=0).reshape(pb.shape)
    send(3, pb.at[1 - core], pbc, sibling)
    hi, lo = split2(rows_b)
    bst[...] = jnp.concatenate([hi, lo, hi], axis=0)
    ma[...] = jnp.zeros_like(ma)

    def first_mode(i, carry):
        k0 = i * per
        th = t_hi[pl.ds(k0, per)].reshape(per * height, width)
        tl = t_lo[pl.ds(k0, per)].reshape(per * height, width)
        along = jnp.dot(jnp.concatenate([th, th, tl], axis=1), bst[...], preferred_element_type=F32)
        total = ma[...].reshape(height, rank)
        for j in range(per):
            total = total + along[j * height : (j + 1) * height] * c_ref[pl.ds(k0 + j, 1), :]
        ma[...] = total.reshape(ma.shape)
        return carry

    lax.fori_loop(0, 1, first_mode, 0)
    arrived(3, pbc)
    hs[...] = pb[core] + pbc[...]
    send(4, hs, pby, across)
    lax.fori_loop(1, n_chunk - 1, first_mode, 0)
    arrived(4, pby)
    gb[core] = hs[...] + pby[...]
    send(6, gb.at[core], gb.at[core], sibling)
    lax.fori_loop(n_chunk - 1, n_chunk, first_mode, 0)
    fan(5, n_s, share_peer, lambda where: ma.at[where], ra.at[s])
    ra[s] = ma[s]
    arrived(6, gb.at[0])

    blocks = gb[...].reshape(3 * side, side)
    gram_b = jnp.concatenate(
        [
            jnp.concatenate([blocks[:side], blocks[side : 2 * side]], axis=1),
            jnp.concatenate([blocks[side : 2 * side].T, blocks[2 * side :]], axis=1),
        ],
        axis=0,
    )
    along, down = diagonal(gram_b)
    scl[...] = set_system(sysm, gram_b, (along, 1.0), (down, 1.0), gc[...], gca[...], gcd[...])
    sweep = (sysm, lt, rt, qp, tmp)

    def half_of(h, carry):
        sweep_half(*sweep, h)
        return carry

    sweep_begin(*sweep)
    lax.fori_loop(0, rank // 128, half_of, 0)
    sweep_end(*sweep)
    arrived(5, ra.at[pl.ds(0, n_s - 1)])
    share_a = jnp.sum(ra[...], axis=0)
    raw_a = -jnp.dot(share_a * scl[...], sysm[...], precision=HIGH, preferred_element_type=F32) * scl[...]

    pa[q] = raw_a
    over_chips(7, pa)
    over_cores(7, 0, pa)
    arrived(0, pa.at[pl.ds(0, n_p)])
    rows_a = pa[...].reshape(n_q * 8, rank)
    pg[...] = lax.dot_general(rows_a, rows_a, TN, precision=HIGH, preferred_element_type=F32).reshape(pg.shape)
    fan(8, n_z, z_peer, lambda _: pg.at[q], gz.at[z])
    gz[z] = pg[q]
    mbt[...] = jnp.zeros_like(mbt)

    ours = [
        pa[pl.ds(c * n_p + (yl * 2 + y) * n_x, n_x)].reshape(n_x * 8, rank) for y in range(2) for c in range(2)
    ]
    at[...] = jnp.concatenate(ours, axis=0).T

    def second_mode(i, carry):
        k0 = i * per
        hi, lo = zip(*[split2(at[...] * ctb[k0 + j]) for j in range(per)])
        th = t_hi[pl.ds(k0, per)].reshape(per * height, width)
        tl = t_lo[pl.ds(k0, per)].reshape(per * height, width)
        mbt[...] += jnp.dot(
            jnp.concatenate(hi + lo + hi, axis=1), jnp.concatenate([th, th, tl], axis=0), preferred_element_type=F32
        )
        return carry

    lax.fori_loop(0, 2, second_mode, 0)
    arrived(8, gz.at[pl.ds(0, n_z - 1)])
    ga[q] = jnp.sum(gz[...], axis=0)
    over_chips(9, ga)
    lax.fori_loop(2, n_chunk - 1, second_mode, 0)
    over_cores(9, 14, ga)
    lax.fori_loop(n_chunk - 1, n_chunk, second_mode, 0)
    mb[...] = mbt[...].T.reshape(mb.shape)
    fan(10, n_g, group_peer, lambda where: mb.at[:, where], rb1.at[g])
    rb1[g] = mb[:, g]

    arrived(14, ga.at[pl.ds(0, n_p)])
    gram = ga[...].reshape(rank, rank)
    along, down = diagonal(gram)
    weight_a = jnp.sqrt(along * (1.0 / total_a) + epsilon)
    iw[...] = 1.0 / weight_a
    w_a_ref[...] = weight_a
    hat_a_ref[...] = pa[q] / weight_a
    results = [
        pltpu.make_async_copy(have, want, out_sem.at[i])
        for i, (have, want) in enumerate(
            [(hat_a_ref, hat_a_hbm), (w_a_ref, w_a_hbm), (hat_b_ref, hat_b_hbm), (w_b_ref, w_b_hbm)]
        )
    ]
    for result in results[:2]:
        result.start()
    iw_down = 1.0 / jnp.sqrt(down * (1.0 / total_a) + epsilon)
    scl[...] = set_system(sysm, gram, (along, iw[...]), (down, iw_down), gc[...], gca[...], gcd[...])
    sweep_begin(*sweep)

    def half_with_sums(h, carry):
        sweep_half(*sweep, h)

        @pl.when(h == 0)
        def _():
            arrived(10, rb1.at[pl.ds(0, n_g - 1)])
            mb1[...] = jnp.sum(rb1[...], axis=0)
            fan(11, n_z, z_peer, lambda where: mb1.at[where], rb2.at[z])
            rb2[z] = mb1[z]

        return carry

    lax.fori_loop(0, rank // 128, half_with_sums, 0)
    sweep_end(*sweep)
    arrived(11, rb2.at[pl.ds(0, n_z - 1)])
    share_b = jnp.sum(rb2[...], axis=0)
    raw_b = -jnp.dot(share_b * iw[...] * scl[...], sysm[...], precision=HIGH, preferred_element_type=F32) * scl[...]

    mine = yl * 2 * n_x + yh * n_x + ka
    sqp[mine] = jnp.sum(raw_b * raw_b, axis=0, keepdims=True)
    fan(12, n_p, plane_peer, lambda _: sqp.at[mine], sqp.at[mine])
    arrived(12, sqp.at[pl.ds(0, n_p - 1)])
    line = core * n_z + z
    sqz[line] = jnp.sum(sqp[...], axis=0)
    fan(13, 2 * n_z, line_peer, lambda _: sqz.at[line], sqz.at[line])
    arrived(13, sqz.at[pl.ds(0, 2 * n_z - 1)])
    weight_b = jnp.sqrt(jnp.sum(sqz[...], axis=0) * (1.0 / total_b) + epsilon)
    w_b_ref[...] = weight_b
    hat_b_ref[...] = raw_b / weight_b
    for result in results[2:]:
        result.start()

    for d in range(1, n_z):
        sent(14 + d, bfull.at[z, g])
    if n_x > 1:
        sent(1, call.at[pl.ds(0, n_x - 1)])
    sent(2, bfull.at[:, pl.ds(0, n_g - 1)])
    sent(3, pbc)
    sent(4, pby)
    sent(5, ra.at[pl.ds(0, n_s - 1)])
    sent(6, gb.at[0])
    sent(7, pa.at[pl.ds(0, n_p - 1)])
    sent(0, pa.at[pl.ds(0, n_p)])
    sent(8, gz.at[pl.ds(0, n_z - 1)])
    sent(9, ga.at[pl.ds(0, n_p - 1)])
    sent(14, ga.at[pl.ds(0, n_p)])
    sent(10, rb1.at[pl.ds(0, n_g - 1)])
    sent(11, rb2.at[pl.ds(0, n_z - 1)])
    sent(12, sqp.at[pl.ds(0, n_p - 1)])
    sent(13, sqz.at[pl.ds(0, 2 * n_z - 1)])
    for result in results:
        result.wait()


def finish(*refs):
    copies = [pltpu.make_async_copy(refs[i], refs[4 + i], refs[8].at[i]) for i in range(4)]
    for copy in copies:
        copy.start()
    for copy in copies:
        copy.wait()


def local(tensor, factor_b, factor_c):
    depth, height, width = tensor.shape
    rank = factor_c.shape[1]
    n_x, n_z = lax.axis_size("ka"), lax.axis_size("ia") // 2
    n_s, n_q, n_g = 4 * n_x, 8 * n_x, 2 * n_x
    part = rank // n_q
    n_chunk = 6
    v = pltpu.VMEM
    out = jax.ShapeDtypeStruct
    hbm = pl.BlockSpec(memory_space=pltpu.HBM)
    results = [out((8, rank), F32), out((1, rank), F32), out((8, rank), F32), out((1, rank), F32)]
    found = pl.pallas_call(
        functools.partial(kernel, n_x, n_z, height * lax.axis_size("ia"), width * lax.axis_size("ja")),
        out_shape=results,
        in_specs=[hbm] * 3,
        out_specs=[hbm] * 4,
        scratch_shapes=[
            v((8, rank), F32),
            v((1, rank), F32),
            v((8, rank), F32),
            v((1, rank), F32),
            v((8, rank), F32),
            v((depth, rank), F32),
            v((depth, height, width), F32),
            v((depth, height, width), BF16),
            v((depth, height, width), BF16),
            v((n_z, n_g, 8, rank), F32),
            v((3 * width, rank), BF16),
            v((n_x, depth, rank), F32),
            v((2, 3 * rank // 4, rank // 2), F32),
            v((3 * rank // 4, rank // 2), F32),
            v((3 * rank // 4, rank // 2), F32),
            v((3 * rank // 4, rank // 2), F32),
            v((2, 3 * rank // 4, rank // 2), F32),
            v((rank, rank), F32),
            v((1, rank), F32),
            v((rank, 1), F32),
            v((n_s, 8, rank), F32),
            v((n_s, 8, rank), F32),
            v((n_q, 8, rank), F32),
            v((n_q, part, rank), F32),
            v((n_z, part, rank), F32),
            v((n_q, part, rank), F32),
            v((rank, rank), F32),
            v((rank, 6 * NB), BF16),
            v((6 * NB, rank), BF16),
            v((NB, rank), F32),
            v((160, 8, 128), F32),
            v((1, rank), F32),
            v((1, rank), F32),
            v((rank, height), F32),
            v((depth, rank, height), F32),
            v((rank, width), F32),
            v((n_z, n_g, 8, rank), F32),
            v((n_g, n_z, 8, rank), F32),
            v((n_z, 8, rank), F32),
            v((n_z, 8, rank), F32),
            v((n_s, 1, rank), F32),
            v((2 * n_z, 1, rank), F32),
            pltpu.SemaphoreType.DMA((n_chunk + 2,)),
            pltpu.SemaphoreType.DMA((4,)),
            pltpu.SemaphoreType.DMA((14 + n_z,)),
            pltpu.SemaphoreType.DMA((14 + n_z,)),
        ],
        compiler_params=pltpu.CompilerParams(
            collective_id=0, has_side_effects=True, vmem_limit_bytes=VMEM_LIMIT
        ),
    )(tensor, factor_b, factor_c)
    hat_a, weight_a, hat_b, weight_b = pl.pallas_call(
        finish,
        out_shape=results,
        in_specs=[hbm] * 4,
        out_specs=[hbm] * 4,
        scratch_shapes=[pltpu.SemaphoreType.DMA((4,))],
        compiler_params=pltpu.CompilerParams(vmem_limit_bytes=VMEM_LIMIT),
    )(*found)
    return hat_a, weight_a.reshape(rank), hat_b, weight_b.reshape(rank)


def solution(mesh):
    return jax.shard_map(
        local,
        mesh=mesh,
        in_specs=(P("ka", "ia", "ja"), P(("ja", "ia", "ka"), None), P("ka", None)),
        out_specs=(P(("ia", "ja", "ka"), None), P(), P(("ja", "ia", "ka"), None), P()),
        check_vma=False,
    )
```

```python
import functools

import jax
import jax.numpy as jnp
from jax import lax
from jax.experimental import pallas as pl
from jax.experimental.pallas import tpu as pltpu
from jax.sharding import PartitionSpec as P

ridge_term = 0.01
epsilon = 1e-06

MESH = pl.DeviceIdType.MESH
HIGH = lax.Precision.HIGHEST
F32 = jnp.float32
BF16 = jnp.bfloat16
VMEM_LIMIT = 65000000
NB = 32
SUB = 16
TN = (((0,), (0,)), ((), ()))


def split2(x):
    hi = x.astype(BF16)
    return hi, (x - hi.astype(F32)).astype(BF16)


def split3(x):
    hi = x.astype(BF16)
    rest = x - hi.astype(F32)
    mid = rest.astype(BF16)
    return hi, mid, (rest - mid.astype(F32)).astype(BF16)


def sweep_half(a_ref, lt_ref, rt_ref, q_ref, tmp_ref, h, between=None):
    rank = a_ref.shape[0]
    parts = rank // 128
    row8 = lax.broadcasted_iota(jnp.int32, (8, 128), 0)
    lane8 = lax.broadcasted_iota(jnp.int32, (8, 128), 1)
    lane = lax.broadcasted_iota(jnp.int32, (NB, rank), 1)
    groups = NB // 8
    wide = SUB // 8
    for t in range(128 // NB):
        if between is not None and t == 2:
            pl.when(h == rank // 128 - 1)(between)
        l0 = t * NB
        r0 = pl.multiple_of(h * 128 + l0, NB)
        before = (lane >= r0 - NB) & (lane < r0)
        r = jnp.where(before, 0.0, a_ref[pl.ds(r0, NB), :]) - jnp.dot(
            lt_ref[pl.ds(r0, NB), :], rt_ref[...], preferred_element_type=F32
        )
        catch_up(a_ref, lt_ref, rt_ref, q_ref, r0)
        r1, r2, r3 = split3(jnp.where((lane >= r0) & (lane < r0 + NB), 0.0, r))
        half = [r[:, 128 * v : 128 * v + 128] for v in range(parts)]
        own = half[0]
        for v in range(1, parts):
            own = jnp.where(h == v, half[v], own)
        half = [own] + [jnp.where(h == v, half[0], half[v]) for v in range(1, parts)]
        x = [[y[8 * m : 8 * m + 8] for y in half] for m in range(groups)]
        for u in range(NB // SUB):
            mine = range(u * wide, (u + 1) * wide)
            rest = [m for m in range(groups) if m not in mine]
            first = l0 + u * SUB
            spread = lambda m, j: jnp.broadcast_to(x[m][0][:, first + j : first + j + 1], (8, 128))
            cols = [{m: spread(m, j) for m in mine} for j in range(SUB)]
            left = {m: [spread(m, j) for j in range(SUB)] for m in rest}
            slot = 0

            def keep(y):
                nonlocal slot
                tmp_ref[slot] = y
                slot += 1
                return slot - 1

            def row_of(where, s):
                return jnp.broadcast_to(tmp_ref[where, s : s + 1, :], (8, 128))

            kept = [{mine[0]: keep(cols[j][mine[0]])} for j in range(SUB)]
            a, c, e = row_of(kept[0][mine[0]], 0), row_of(kept[0][mine[0]], 1), row_of(kept[1][mine[0]], 1)
            for p in range(0, SUB, 2):
                i, s = u * wide + p // 8, p % 8
                i2, s2 = u * wide + (p + 2) // 8, (p + 2) % 8
                det = a * e - c * c
                guess = pl.reciprocal(det, approx=True)
                off = 1.0 - det * guess
                inv = (guess + guess * off) * (1.0 + off * off)

                def combine(yp, yq):
                    return e * yp - c * yq, a * yq - c * yp

                def apply(y, np_, nq_):
                    wp, wq = np_ * inv, nq_ * inv
                    done = {m: y[m] - cols[p][m] * wp - cols[p + 1][m] * wq for m in mine}
                    plain = done[i]
                    done[i] = jnp.where(row8 == s, wp, jnp.where(row8 == s + 1, wq, plain))
                    return done, plain

                mixed = {j: combine(row_of(kept[j][i], s), row_of(kept[j][i], s + 1)) for j in range(p + 2, SUB)}
                if p + 2 < SUB:
                    for j in range(p, p + 4):
                        if i2 not in kept[j]:
                            kept[j][i2] = keep(cols[j][i2])
                    (lp0, lp1), (lq0, lq1) = [[row_of(kept[j][i2], s2 + k) for k in (0, 1)] for j in (p, p + 1)]
                    a0, c0 = row_of(kept[p + 2][i2], s2), row_of(kept[p + 2][i2], s2 + 1)
                    e0 = row_of(kept[p + 3][i2], s2 + 1)
                    (np2, nq2), (np3, nq3) = mixed[p + 2], mixed[p + 3]
                    following = (
                        a0 - (lp0 * np2 + lq0 * nq2) * inv,
                        c0 - (lp1 * np2 + lq1 * nq2) * inv,
                        e0 - (lp1 * np3 + lq1 * nq3) * inv,
                    )
                for j in range(p + 2, SUB):
                    cols[j], plain = apply(cols[j], *mixed[j])
                    kept[j] = {i2: keep(plain if i2 == i else cols[j][i2])}
                here = (lane8 == first + p) | (lane8 == first + p + 1)
                unit = jnp.where(lane8 - first - p == row8 - s, -1.0, 0.0)
                for m in mine:
                    x[m][0] = jnp.where(here, unit if m == i else 0.0, x[m][0])
                for v in range(parts):
                    where = keep(x[i][v])
                    done, _ = apply({m: x[m][v] for m in mine}, *combine(row_of(where, s), row_of(where, s + 1)))
                    for m in mine:
                        x[m][v] = done[m]
                if p + 2 < SUB:
                    a, c, e = following
            ours = (lane8 >= first) & (lane8 < first + SUB)
            base = slot
            for m in mine:
                for v in range(parts):
                    tmp_ref[slot] = x[m][v]
                    slot += 1
            if u == 0:
                lt_ref[...] = jnp.concatenate([r1, r1, r2, r2, r1, r3], axis=0).T
            for m in rest:
                x[m][0] = jnp.where(ours, 0.0, x[m][0])
                for v in range(parts):
                    terms = [
                        left[m][j] * jnp.broadcast_to(tmp_ref[base + j // 8 * parts + v, j % 8 : j % 8 + 1, :], (8, 128))
                        for j in range(SUB)
                    ]
                    while len(terms) > 1:
                        terms = [terms[k] + terms[k + 1] for k in range(0, len(terms), 2)]
                    x[m][v] = x[m][v] - terms[0]
        half = [jnp.concatenate([x[m][v] for m in range(groups)], axis=0) for v in range(parts)]
        half = [jnp.where(h == 0, half[0], half[1]), jnp.where(h == 0, half[1], half[0])]
        q = jnp.concatenate(half, axis=1)
        q1, q2, q3 = split3(q)
        rt_ref[...] = jnp.concatenate([q1, q2, q1, q2, q3, q1], axis=0)
        q_ref[...] = q


def catch_up(a_ref, lt_ref, rt_ref, q_ref, r0):
    rank = a_ref.shape[0]
    lane = lax.broadcasted_iota(jnp.int32, (8, rank), 1)
    done = (lane >= r0 - NB) & (lane < r0)
    update = jnp.dot(lt_ref[...], rt_ref[...], preferred_element_type=F32)
    rest = jnp.where(done[None], 0.0, a_ref[...].reshape(rank // 8, 8, rank))
    a_ref[...] = rest.reshape(rank, rank) - update
    a_ref[pl.ds(pl.multiple_of(jnp.maximum(r0 - NB, 0), NB), NB), :] = q_ref[...]


def sweep_begin(a_ref, lt_ref, rt_ref, q_ref, tmp_ref):
    lt_ref[...] = jnp.zeros_like(lt_ref)
    rt_ref[...] = jnp.zeros_like(rt_ref)
    q_ref[...] = a_ref[:NB, :]


def sweep_end(a_ref, lt_ref, rt_ref, q_ref, tmp_ref):
    catch_up(a_ref, lt_ref, rt_ref, q_ref, a_ref.shape[0])


def diagonal(matrix):
    rank = matrix.shape[0]
    eye = lax.broadcasted_iota(jnp.int32, (rank, rank), 0) == lax.broadcasted_iota(jnp.int32, (rank, rank), 1)
    kept = jnp.where(eye, matrix, 0.0)
    return jnp.sum(kept, axis=0, keepdims=True), jnp.sum(kept, axis=1, keepdims=True)


def set_system(a_ref, gram, along, down, gc, gc_along, gc_down):
    rank = gram.shape[0]
    eye = lax.broadcasted_iota(jnp.int32, (rank, rank), 0) == lax.broadcasted_iota(jnp.int32, (rank, rank), 1)
    (g_along, f_along), (g_down, f_down) = along, down
    s_along = lax.rsqrt(g_along * f_along * f_along * gc_along + ridge_term)
    s_down = lax.rsqrt(g_down * f_down * f_down * gc_down + ridge_term)
    scaled = gram * (f_down * s_down) * (f_along * s_along) * gc
    a_ref[...] = scaled + jnp.where(eye, ridge_term * s_along * s_along, 0.0)
    return s_along


def kernel(
    n_x, n_z, total_a, total_b,
    t_hbm, b_hbm, c_hbm,
    hat_a_hbm, w_a_hbm, hat_b_hbm, w_b_hbm,
    hat_a_ref, w_a_ref, hat_b_ref, w_b_ref, b_ref, c_ref, t_f32, t_hi, t_lo, bfull, bst, call, pb, pbc, hs, pby, gb, gc, gca, gcd, ma, ra, pa, at2, gz, gs, ga, sysm, lt, rt, qp, tmp, scl, iw,
    at, ctb, mbt, mb, rb1, mb1, rb2, sq, sqp, sqs, sqz,
    t_sem, out_sem, send_sem, recv_sem,
):
    depth, height, width = t_f32.shape
    rank = c_ref.shape[1]
    ia, ja, ka = lax.axis_index("ia"), lax.axis_index("ja"), lax.axis_index("ka")
    z, yl = lax.div(ia, 2), lax.rem(ia, 2)
    yh, core = lax.div(ja, 2), lax.rem(ja, 2)
    n_s = 4 * n_x
    n_q = 2 * n_s
    n_g = 2 * n_x
    s = ja * n_x + ka
    q = yl * n_s + s
    g = yl * n_x + ka

    yls = [lax.rem(yl + d, 2) for d in range(2)]
    jas = [lax.rem(ja + d, 4) for d in range(4)]
    kas = [lax.rem(ka + d, n_x) for d in range(n_x)]
    zs = [lax.rem(z + d, n_z) for d in range(n_z)]
    ias = [z * 2 + yl2 for yl2 in yls]

    def plane_peer(d):
        y, j, k = d // n_s, d // n_x % 4, d % n_x
        return yls[y] * n_s + jas[j] * n_x + kas[k], (ias[y], jas[j], kas[k])

    def group_peer(d):
        y, k = d // n_x, d % n_x
        return yls[y] * n_x + kas[k], (ias[y], ja, kas[k])

    def share_peer(d):
        j, k = d // n_x, d % n_x
        return jas[j] * n_x + kas[k], (ia, jas[j], kas[k])

    def z_peer(d):
        return zs[d], (zs[d] * 2 + yl, ja, ka)

    def x_peer(d):
        return kas[d], (ia, ja, kas[d])

    def send(stage, src, dst, device):
        pltpu.make_async_remote_copy(
            src_ref=src, dst_ref=dst, send_sem=send_sem.at[stage], recv_sem=recv_sem.at[stage],
            device_id=device, device_id_type=MESH,
        ).start()

    def fan(stage, count, peer, src, dst):
        for d in range(1, count):
            where, device = peer(d)
            send(stage, src(where), dst, device)

    def arrived(stage, ref):
        pltpu.make_async_copy(ref, ref, recv_sem.at[stage]).wait()

    def sent(stage, ref):
        pltpu.make_async_copy(ref, ref, send_sem.at[stage]).wait()

    n_chunk = t_sem.shape[0] - 2
    per = depth // n_chunk
    loads = [
        pltpu.make_async_copy(t_hbm.at[pl.ds(i * per, per)], t_f32.at[pl.ds(i * per, per)], t_sem.at[i])
        for i in range(n_chunk)
    ]
    small = [pltpu.make_async_copy(b_hbm, b_ref, t_sem.at[n_chunk]), pltpu.make_async_copy(c_hbm, c_ref, t_sem.at[n_chunk + 1])]
    for load in small + loads:
        load.start()

    barrier = pltpu.get_barrier_semaphore()

    for count, peer in ((n_z, z_peer), (n_q, plane_peer)):
        for d in range(1, count):
            pl.semaphore_signal(barrier, inc=1, device_id=peer(d)[1], device_id_type=MESH)
    pl.semaphore_wait(barrier, n_q + n_z - 2)

    for load in small:
        load.wait()
    for d in range(1, n_z):
        send(14 + d, b_ref, bfull.at[z, g], z_peer(d)[1])
    fan(2, n_g, group_peer, lambda _: b_ref, bfull.at[z, g])
    fan(1, n_x, x_peer, lambda _: c_ref, call.at[ka])
    bfull[z, g] = b_ref[...]
    call[ka] = c_ref[...]

    ct = jnp.concatenate([c_ref[...], jnp.zeros((128 - depth, rank), F32)], axis=0).T
    for k in range(depth):
        ctb[k] = jnp.broadcast_to(ct[:, k : k + 1], (rank, height))

    def cut(first, last):
        def body(k, carry):
            hi, lo = split2(t_f32[k])
            t_hi[k] = hi
            t_lo[k] = lo
            return carry

        lax.fori_loop(first, last, body, 0)

    for d in sorted(range(1, n_z), key=lambda d: min(d, n_z - d)):
        block = bfull.at[zs[n_z - d], g]
        arrived(14 + d, block)
        fan(2, n_g, group_peer, lambda _: block, block)
    for i in range(n_chunk):
        loads[i].wait()
        cut(i * per, (i + 1) * per)
    if n_x > 1:
        arrived(1, call.at[pl.ds(0, n_x - 1)])
    call_rows = call[...].reshape(n_x * depth, rank)
    gc[...] = lax.dot_general(call_rows, call_rows, TN, precision=HIGH, preferred_element_type=F32)
    gca[...], gcd[...] = diagonal(gc[...])

    arrived(2, bfull.at[:, pl.ds(0, n_g - 1)])
    rows_b = bfull[...].reshape(width, rank)
    side = rank // 2
    upper = lax.dot_general(rows_b[:, :side], rows_b, TN, precision=HIGH, preferred_element_type=F32)
    corner = lax.dot_general(rows_b[:, side:], rows_b[:, side:], TN, precision=HIGH, preferred_element_type=F32)
    pb[...] = jnp.concatenate([upper[:, :side], upper[:, side:], corner], axis=0).reshape(pb.shape)
    sibling = (ia, ja + 1 - 2 * core, ka)
    across = (z * 2 + 1 - yl, ja + 2 - 4 * yh, ka)
    send(3, pb.at[1 - core], pbc, sibling)
    hi, lo = split2(rows_b)
    bst[...] = jnp.concatenate([hi, lo, hi], axis=0)
    ma[...] = jnp.zeros_like(ma)

    def first_mode(i, carry):
        k0 = i * per
        th = t_hi[pl.ds(k0, per)].reshape(per * height, width)
        tl = t_lo[pl.ds(k0, per)].reshape(per * height, width)
        along = jnp.dot(jnp.concatenate([th, th, tl], axis=1), bst[...], preferred_element_type=F32)
        total = ma[...].reshape(height, rank)
        for j in range(per):
            total = total + along[j * height : (j + 1) * height] * c_ref[pl.ds(k0 + j, 1), :]
        ma[...] = total.reshape(ma.shape)
        return carry

    lax.fori_loop(0, 1, first_mode, 0)
    arrived(3, pbc)
    hs[...] = pb[core] + pbc[...]
    send(4, hs, pby, across)
    lax.fori_loop(1, n_chunk - 1, first_mode, 0)
    arrived(4, pby)
    gb[core] = hs[...] + pby[...]
    send(6, gb.at[core], gb.at[core], sibling)
    lax.fori_loop(n_chunk - 1, n_chunk, first_mode, 0)
    fan(5, n_s, share_peer, lambda where: ma.at[where], ra.at[s])
    ra[s] = ma[s]
    arrived(6, gb.at[0])

    blocks = gb[...].reshape(3 * side, side)
    gram_b = jnp.concatenate(
        [
            jnp.concatenate([blocks[:side], blocks[side : 2 * side]], axis=1),
            jnp.concatenate([blocks[side : 2 * side].T, blocks[2 * side :]], axis=1),
        ],
        axis=0,
    )
    along, down = diagonal(gram_b)
    scl[...] = set_system(sysm, gram_b, (along, 1.0), (down, 1.0), gc[...], gca[...], gcd[...])
    sweep = (sysm, lt, rt, qp, tmp)

    def half_of(h, carry):
        sweep_half(*sweep, h)
        return carry

    sweep_begin(*sweep)
    lax.fori_loop(0, rank // 128, half_of, 0)
    sweep_end(*sweep)
    arrived(5, ra.at[pl.ds(0, n_s - 1)])
    share_a = jnp.sum(ra[...], axis=0)
    raw_a = -jnp.dot(share_a * scl[...], sysm[...], precision=HIGH, preferred_element_type=F32) * scl[...]

    pa[q] = raw_a
    fan(7, n_q, plane_peer, lambda _: pa.at[q], pa.at[q])
    arrived(7, pa.at[pl.ds(0, n_q - 1)])
    rows_a = pa[...].reshape(n_q * 8, rank)
    part = gz.shape[1]
    at2[...] = rows_a.T
    gz[z] = jnp.dot(at2[pl.ds(pl.multiple_of(q * part, part), part), :], rows_a, precision=HIGH, preferred_element_type=F32)
    fan(8, n_z, z_peer, lambda _: gz.at[z], gz.at[z])
    mbt[...] = jnp.zeros_like(mbt)

    at[...] = pa[pl.ds(yl * n_s, n_s)].reshape(height, rank).T

    def second_mode(i, carry):
        k0 = i * per
        hi, lo = zip(*[split2(at[...] * ctb[k0 + j]) for j in range(per)])
        th = t_hi[pl.ds(k0, per)].reshape(per * height, width)
        tl = t_lo[pl.ds(k0, per)].reshape(per * height, width)
        mbt[...] += jnp.dot(
            jnp.concatenate(hi + lo + hi, axis=1), jnp.concatenate([th, th, tl], axis=0), preferred_element_type=F32
        )
        return carry

    lax.fori_loop(0, n_chunk // 2, second_mode, 0)
    arrived(8, gz.at[pl.ds(0, n_z - 1)])
    gs[...] = jnp.sum(gz[...], axis=0)
    fan(9, n_q, plane_peer, lambda _: gs, ga.at[q])
    ga[q] = gs[...]
    lax.fori_loop(n_chunk // 2, n_chunk, second_mode, 0)
    mb[...] = mbt[...].T.reshape(mb.shape)
    fan(10, n_g, group_peer, lambda where: mb.at[:, where], rb1.at[g])
    rb1[g] = mb[:, g]

    arrived(9, ga.at[pl.ds(0, n_q - 1)])
    gram = ga[...].reshape(rank, rank)
    along, down = diagonal(gram)
    weight_a = jnp.sqrt(along * (1.0 / total_a) + epsilon)
    iw[...] = 1.0 / weight_a
    w_a_ref[...] = weight_a
    hat_a_ref[...] = pa[q] / weight_a
    results = [
        pltpu.make_async_copy(have, want, out_sem.at[i])
        for i, (have, want) in enumerate(
            [(hat_a_ref, hat_a_hbm), (w_a_ref, w_a_hbm), (hat_b_ref, hat_b_hbm), (w_b_ref, w_b_hbm)]
        )
    ]
    for result in results[:2]:
        result.start()
    iw_down = 1.0 / jnp.sqrt(down * (1.0 / total_a) + epsilon)
    scl[...] = set_system(sysm, gram, (along, iw[...]), (down, iw_down), gc[...], gca[...], gcd[...])
    sweep_begin(*sweep)

    def pass_sums():
        arrived(10, rb1.at[pl.ds(0, n_g - 1)])
        mb1[...] = jnp.sum(rb1[...], axis=0)
        fan(11, n_z, z_peer, lambda where: mb1.at[where], rb2.at[z])
        rb2[z] = mb1[z]

    def half_with_sums(h, carry):
        sweep_half(*sweep, h, pass_sums)
        return carry

    lax.fori_loop(0, rank // 128, half_with_sums, 0)
    sweep_end(*sweep)
    arrived(11, rb2.at[pl.ds(0, n_z - 1)])
    share_b = jnp.sum(rb2[...], axis=0)
    raw_b = -jnp.dot(share_b * iw[...] * scl[...], sysm[...], precision=HIGH, preferred_element_type=F32) * scl[...]

    sq[...] = jnp.sum(raw_b * raw_b, axis=0, keepdims=True)
    fan(12, n_q, plane_peer, lambda _: sq, sqp.at[q])
    sqp[q] = sq[...]
    arrived(12, sqp.at[pl.ds(0, n_q - 1)])
    sqs[...] = jnp.sum(sqp[...], axis=0)
    fan(13, n_z, z_peer, lambda _: sqs, sqz.at[z])
    sqz[z] = sqs[...]
    arrived(13, sqz.at[pl.ds(0, n_z - 1)])
    weight_b = jnp.sqrt(jnp.sum(sqz[...], axis=0) * (1.0 / total_b) + epsilon)
    w_b_ref[...] = weight_b
    hat_b_ref[...] = raw_b / weight_b
    for result in results[2:]:
        result.start()

    for d in range(1, n_z):
        sent(14 + d, bfull.at[z, g])
    if n_x > 1:
        sent(1, call.at[pl.ds(0, n_x - 1)])
    sent(2, bfull.at[:, pl.ds(0, n_g - 1)])
    sent(3, pbc)
    sent(4, pby)
    sent(5, ra.at[pl.ds(0, n_s - 1)])
    sent(6, gb.at[0])
    sent(7, pa.at[pl.ds(0, n_q - 1)])
    sent(8, gz.at[pl.ds(0, n_z - 1)])
    sent(9, ga.at[pl.ds(0, n_q - 1)])
    sent(10, rb1.at[pl.ds(0, n_g - 1)])
    sent(11, rb2.at[pl.ds(0, n_z - 1)])
    sent(12, sqp.at[pl.ds(0, n_q - 1)])
    sent(13, sqz.at[pl.ds(0, n_z - 1)])
    for result in results:
        result.wait()


def finish(*refs):
    copies = [pltpu.make_async_copy(refs[i], refs[4 + i], refs[8].at[i]) for i in range(4)]
    for copy in copies:
        copy.start()
    for copy in copies:
        copy.wait()


def local(tensor, factor_b, factor_c):
    depth, height, width = tensor.shape
    rank = factor_c.shape[1]
    n_x, n_z = lax.axis_size("ka"), lax.axis_size("ia") // 2
    n_s, n_q, n_g = 4 * n_x, 8 * n_x, 2 * n_x
    part = rank // n_q
    n_chunk = 6
    v = pltpu.VMEM
    out = jax.ShapeDtypeStruct
    hbm = pl.BlockSpec(memory_space=pltpu.HBM)
    results = [out((8, rank), F32), out((1, rank), F32), out((8, rank), F32), out((1, rank), F32)]
    found = pl.pallas_call(
        functools.partial(kernel, n_x, n_z, height * lax.axis_size("ia"), width * lax.axis_size("ja")),
        out_shape=results,
        in_specs=[hbm] * 3,
        out_specs=[hbm] * 4,
        scratch_shapes=[
            v((8, rank), F32),
            v((1, rank), F32),
            v((8, rank), F32),
            v((1, rank), F32),
            v((8, rank), F32),
            v((depth, rank), F32),
            v((depth, height, width), F32),
            v((depth, height, width), BF16),
            v((depth, height, width), BF16),
            v((n_z, n_g, 8, rank), F32),
            v((3 * width, rank), BF16),
            v((n_x, depth, rank), F32),
            v((2, 3 * rank // 4, rank // 2), F32),
            v((3 * rank // 4, rank // 2), F32),
            v((3 * rank // 4, rank // 2), F32),
            v((3 * rank // 4, rank // 2), F32),
            v((2, 3 * rank // 4, rank // 2), F32),
            v((rank, rank), F32),
            v((1, rank), F32),
            v((rank, 1), F32),
            v((n_s, 8, rank), F32),
            v((n_s, 8, rank), F32),
            v((n_q, 8, rank), F32),
            v((rank, n_q * 8), F32),
            v((n_z, part, rank), F32),
            v((part, rank), F32),
            v((n_q, part, rank), F32),
            v((rank, rank), F32),
            v((rank, 6 * NB), BF16),
            v((6 * NB, rank), BF16),
            v((NB, rank), F32),
            v((160, 8, 128), F32),
            v((1, rank), F32),
            v((1, rank), F32),
            v((rank, height), F32),
            v((depth, rank, height), F32),
            v((rank, width), F32),
            v((n_z, n_g, 8, rank), F32),
            v((n_g, n_z, 8, rank), F32),
            v((n_z, 8, rank), F32),
            v((n_z, 8, rank), F32),
            v((1, rank), F32),
            v((n_q, 1, rank), F32),
            v((1, rank), F32),
            v((n_z, 1, rank), F32),
            pltpu.SemaphoreType.DMA((n_chunk + 2,)),
            pltpu.SemaphoreType.DMA((4,)),
            pltpu.SemaphoreType.DMA((14 + n_z,)),
            pltpu.SemaphoreType.DMA((14 + n_z,)),
        ],
        compiler_params=pltpu.CompilerParams(
            collective_id=0, has_side_effects=True, vmem_limit_bytes=VMEM_LIMIT
        ),
    )(tensor, factor_b, factor_c)
    hat_a, weight_a, hat_b, weight_b = pl.pallas_call(
        finish,
        out_shape=results,
        in_specs=[hbm] * 4,
        out_specs=[hbm] * 4,
        scratch_shapes=[pltpu.SemaphoreType.DMA((4,))],
        compiler_params=pltpu.CompilerParams(vmem_limit_bytes=VMEM_LIMIT),
    )(*found)
    return hat_a, weight_a.reshape(rank), hat_b, weight_b.reshape(rank)


def solution(mesh):
    return jax.shard_map(
        local,
        mesh=mesh,
        in_specs=(P("ka", "ia", "ja"), P(("ja", "ia", "ka"), None), P("ka", None)),
        out_specs=(P(("ia", "ja", "ka"), None), P(), P(("ja", "ia", "ka"), None), P()),
        check_vma=False,
    )
```

```python
import functools

import jax
import jax.numpy as jnp
from jax import lax
from jax.experimental import pallas as pl
from jax.experimental.pallas import tpu as pltpu
from jax.sharding import PartitionSpec as P

ridge_term = 0.01
epsilon = 1e-06

MESH = pl.DeviceIdType.MESH
HIGH = lax.Precision.HIGHEST
F32 = jnp.float32
BF16 = jnp.bfloat16
VMEM_LIMIT = 65000000
NB = 32
SUB = 8
TN = (((0,), (0,)), ((), ()))


def split2(x):
    hi = x.astype(BF16)
    return hi, (x - hi.astype(F32)).astype(BF16)


def split3(x):
    hi = x.astype(BF16)
    rest = x - hi.astype(F32)
    mid = rest.astype(BF16)
    return hi, mid, (rest - mid.astype(F32)).astype(BF16)


def sweep_half(a_ref, lt_ref, rt_ref, q_ref, tmp_ref, h, between=None):
    rank = a_ref.shape[0]
    parts = rank // 128
    row8 = lax.broadcasted_iota(jnp.int32, (8, 128), 0)
    lane8 = lax.broadcasted_iota(jnp.int32, (8, 128), 1)
    lane = lax.broadcasted_iota(jnp.int32, (NB, rank), 1)
    groups = NB // 8
    wide = SUB // 8
    for t in range(128 // NB):
        if between is not None and t == 2:
            pl.when(h == rank // 128 - 1)(between)
        l0 = t * NB
        r0 = pl.multiple_of(h * 128 + l0, NB)
        before = (lane >= r0 - NB) & (lane < r0)
        r = jnp.where(before, 0.0, a_ref[pl.ds(r0, NB), :]) - jnp.dot(
            lt_ref[pl.ds(r0, NB), :], rt_ref[...], preferred_element_type=F32
        )
        catch_up(a_ref, lt_ref, rt_ref, q_ref, r0)
        r1, r2, r3 = split3(jnp.where((lane >= r0) & (lane < r0 + NB), 0.0, r))
        half = [r[:, 128 * v : 128 * v + 128] for v in range(parts)]
        own = half[0]
        for v in range(1, parts):
            own = jnp.where(h == v, half[v], own)
        half = [own] + [jnp.where(h == v, half[0], half[v]) for v in range(1, parts)]
        x = [[y[8 * m : 8 * m + 8] for y in half] for m in range(groups)]
        for u in range(NB // SUB):
            mine = range(u * wide, (u + 1) * wide)
            rest = [m for m in range(groups) if m not in mine]
            first = l0 + u * SUB
            spread = lambda m, j: jnp.broadcast_to(x[m][0][:, first + j : first + j + 1], (8, 128))
            cols = [{m: spread(m, j) for m in mine} for j in range(SUB)]
            left = {m: [spread(m, j) for j in range(SUB)] for m in rest}
            slot = 0

            def keep(y):
                nonlocal slot
                tmp_ref[slot] = y
                slot += 1
                return slot - 1

            def row_of(where, s):
                return jnp.broadcast_to(tmp_ref[where, s : s + 1, :], (8, 128))

            kept = [{mine[0]: keep(cols[j][mine[0]])} for j in range(SUB)]
            a, c, e = row_of(kept[0][mine[0]], 0), row_of(kept[0][mine[0]], 1), row_of(kept[1][mine[0]], 1)
            for p in range(0, SUB, 2):
                i, s = u * wide + p // 8, p % 8
                i2, s2 = u * wide + (p + 2) // 8, (p + 2) % 8
                det = a * e - c * c
                guess = pl.reciprocal(det, approx=True)
                off = 1.0 - det * guess
                inv = (guess + guess * off) * (1.0 + off * off)

                def combine(yp, yq):
                    return e * yp - c * yq, a * yq - c * yp

                def apply(y, np_, nq_):
                    wp, wq = np_ * inv, nq_ * inv
                    done = {m: y[m] - cols[p][m] * wp - cols[p + 1][m] * wq for m in mine}
                    plain = done[i]
                    done[i] = jnp.where(row8 == s, wp, jnp.where(row8 == s + 1, wq, plain))
                    return done, plain

                mixed = {j: combine(row_of(kept[j][i], s), row_of(kept[j][i], s + 1)) for j in range(p + 2, SUB)}
                if p + 2 < SUB:
                    for j in range(p, p + 4):
                        if i2 not in kept[j]:
                            kept[j][i2] = keep(cols[j][i2])
                    (lp0, lp1), (lq0, lq1) = [[row_of(kept[j][i2], s2 + k) for k in (0, 1)] for j in (p, p + 1)]
                    a0, c0 = row_of(kept[p + 2][i2], s2), row_of(kept[p + 2][i2], s2 + 1)
                    e0 = row_of(kept[p + 3][i2], s2 + 1)
                    (np2, nq2), (np3, nq3) = mixed[p + 2], mixed[p + 3]
                    following = (
                        a0 - (lp0 * np2 + lq0 * nq2) * inv,
                        c0 - (lp1 * np2 + lq1 * nq2) * inv,
                        e0 - (lp1 * np3 + lq1 * nq3) * inv,
                    )
                for j in range(p + 2, SUB):
                    cols[j], plain = apply(cols[j], *mixed[j])
                    kept[j] = {i2: keep(plain if i2 == i else cols[j][i2])}
                here = (lane8 == first + p) | (lane8 == first + p + 1)
                unit = jnp.where(lane8 - first - p == row8 - s, -1.0, 0.0)
                for m in mine:
                    x[m][0] = jnp.where(here, unit if m == i else 0.0, x[m][0])
                for v in range(parts):
                    where = keep(x[i][v])
                    done, _ = apply({m: x[m][v] for m in mine}, *combine(row_of(where, s), row_of(where, s + 1)))
                    for m in mine:
                        x[m][v] = done[m]
                if p + 2 < SUB:
                    a, c, e = following
            ours = (lane8 >= first) & (lane8 < first + SUB)
            base = slot
            for m in mine:
                for v in range(parts):
                    tmp_ref[slot] = x[m][v]
                    slot += 1
            if u == 0:
                lt_ref[...] = jnp.concatenate([r1, r1, r2, r2, r1, r3], axis=0).T
            for m in rest:
                x[m][0] = jnp.where(ours, 0.0, x[m][0])
                for v in range(parts):
                    terms = [
                        left[m][j] * jnp.broadcast_to(tmp_ref[base + j // 8 * parts + v, j % 8 : j % 8 + 1, :], (8, 128))
                        for j in range(SUB)
                    ]
                    while len(terms) > 1:
                        terms = [terms[k] + terms[k + 1] for k in range(0, len(terms), 2)]
                    x[m][v] = x[m][v] - terms[0]
        half = [jnp.concatenate([x[m][v] for m in range(groups)], axis=0) for v in range(parts)]
        half = [jnp.where(h == 0, half[0], half[1]), jnp.where(h == 0, half[1], half[0])]
        q = jnp.concatenate(half, axis=1)
        q1, q2, q3 = split3(q)
        rt_ref[...] = jnp.concatenate([q1, q2, q1, q2, q3, q1], axis=0)
        q_ref[...] = q


def catch_up(a_ref, lt_ref, rt_ref, q_ref, r0):
    rank = a_ref.shape[0]
    lane = lax.broadcasted_iota(jnp.int32, (8, rank), 1)
    done = (lane >= r0 - NB) & (lane < r0)
    update = jnp.dot(lt_ref[...], rt_ref[...], preferred_element_type=F32)
    rest = jnp.where(done[None], 0.0, a_ref[...].reshape(rank // 8, 8, rank))
    a_ref[...] = rest.reshape(rank, rank) - update
    a_ref[pl.ds(pl.multiple_of(jnp.maximum(r0 - NB, 0), NB), NB), :] = q_ref[...]


def sweep_begin(a_ref, lt_ref, rt_ref, q_ref, tmp_ref):
    lt_ref[...] = jnp.zeros_like(lt_ref)
    rt_ref[...] = jnp.zeros_like(rt_ref)
    q_ref[...] = a_ref[:NB, :]


def sweep_end(a_ref, lt_ref, rt_ref, q_ref, tmp_ref):
    catch_up(a_ref, lt_ref, rt_ref, q_ref, a_ref.shape[0])


def diagonal(matrix):
    rank = matrix.shape[0]
    eye = lax.broadcasted_iota(jnp.int32, (rank, rank), 0) == lax.broadcasted_iota(jnp.int32, (rank, rank), 1)
    kept = jnp.where(eye, matrix, 0.0)
    return jnp.sum(kept, axis=0, keepdims=True), jnp.sum(kept, axis=1, keepdims=True)


def set_system(a_ref, gram, along, down, gc, gc_along, gc_down):
    rank = gram.shape[0]
    eye = lax.broadcasted_iota(jnp.int32, (rank, rank), 0) == lax.broadcasted_iota(jnp.int32, (rank, rank), 1)
    (g_along, f_along), (g_down, f_down) = along, down
    s_along = lax.rsqrt(g_along * f_along * f_along * gc_along + ridge_term)
    s_down = lax.rsqrt(g_down * f_down * f_down * gc_down + ridge_term)
    scaled = gram * (f_down * s_down) * (f_along * s_along) * gc
    a_ref[...] = scaled + jnp.where(eye, ridge_term * s_along * s_along, 0.0)
    return s_along


def kernel(
    n_x, n_z, total_a, total_b,
    t_hbm, b_hbm, c_hbm,
    hat_a_hbm, w_a_hbm, hat_b_hbm, w_b_hbm,
    hat_a_ref, w_a_ref, hat_b_ref, w_b_ref, b_ref, c_ref, t_f32, t_hi, t_lo, bfull, bst, call, pb, pbc, hs, pby, gb, gc, gca, gcd, ma, ra, pa, at2, gz, gs, ga, sysm, lt, rt, qp, tmp, scl, iw,
    at, ctb, mbt, mb, rb1, mb1, rb2, sq, sqp, sqs, sqz,
    t_sem, out_sem, send_sem, recv_sem,
):
    depth, height, width = t_f32.shape
    rank = c_ref.shape[1]
    ia, ja, ka = lax.axis_index("ia"), lax.axis_index("ja"), lax.axis_index("ka")
    z, yl = lax.div(ia, 2), lax.rem(ia, 2)
    yh, core = lax.div(ja, 2), lax.rem(ja, 2)
    n_s = 4 * n_x
    n_q = 2 * n_s
    n_g = 2 * n_x
    s = ja * n_x + ka
    q = yl * n_s + s
    g = yl * n_x + ka

    yls = [lax.rem(yl + d, 2) for d in range(2)]
    jas = [lax.rem(ja + d, 4) for d in range(4)]
    kas = [lax.rem(ka + d, n_x) for d in range(n_x)]
    zs = [lax.rem(z + d, n_z) for d in range(n_z)]
    ias = [z * 2 + yl2 for yl2 in yls]

    def plane_peer(d):
        y, j, k = d // n_s, d // n_x % 4, d % n_x
        return yls[y] * n_s + jas[j] * n_x + kas[k], (ias[y], jas[j], kas[k])

    def group_peer(d):
        y, k = d // n_x, d % n_x
        return yls[y] * n_x + kas[k], (ias[y], ja, kas[k])

    def share_peer(d):
        j, k = d // n_x, d % n_x
        return jas[j] * n_x + kas[k], (ia, jas[j], kas[k])

    def z_peer(d):
        return zs[d], (zs[d] * 2 + yl, ja, ka)

    def x_peer(d):
        return kas[d], (ia, ja, kas[d])

    def send(stage, src, dst, device):
        pltpu.make_async_remote_copy(
            src_ref=src, dst_ref=dst, send_sem=send_sem.at[stage], recv_sem=recv_sem.at[stage],
            device_id=device, device_id_type=MESH,
        ).start()

    def fan(stage, count, peer, src, dst):
        for d in range(1, count):
            where, device = peer(d)
            send(stage, src(where), dst, device)

    def arrived(stage, ref):
        pltpu.make_async_copy(ref, ref, recv_sem.at[stage]).wait()

    def sent(stage, ref):
        pltpu.make_async_copy(ref, ref, send_sem.at[stage]).wait()

    n_chunk = t_sem.shape[0] - 2
    per = depth // n_chunk
    loads = [
        pltpu.make_async_copy(t_hbm.at[pl.ds(i * per, per)], t_f32.at[pl.ds(i * per, per)], t_sem.at[i])
        for i in range(n_chunk)
    ]
    small = [pltpu.make_async_copy(b_hbm, b_ref, t_sem.at[n_chunk]), pltpu.make_async_copy(c_hbm, c_ref, t_sem.at[n_chunk + 1])]
    for load in small + loads:
        load.start()

    barrier = pltpu.get_barrier_semaphore()

    for count, peer in ((n_z, z_peer), (n_q, plane_peer)):
        for d in range(1, count):
            pl.semaphore_signal(barrier, inc=1, device_id=peer(d)[1], device_id_type=MESH)
    pl.semaphore_wait(barrier, n_q + n_z - 2)

    for load in small:
        load.wait()
    for d in range(1, n_z):
        send(14 + d, b_ref, bfull.at[z, g], z_peer(d)[1])
    fan(2, n_g, group_peer, lambda _: b_ref, bfull.at[z, g])
    fan(1, n_x, x_peer, lambda _: c_ref, call.at[ka])
    bfull[z, g] = b_ref[...]
    call[ka] = c_ref[...]

    ct = jnp.concatenate([c_ref[...], jnp.zeros((128 - depth, rank), F32)], axis=0).T
    for k in range(depth):
        ctb[k] = jnp.broadcast_to(ct[:, k : k + 1], (rank, height))

    def cut(first, last):
        def body(k, carry):
            hi, lo = split2(t_f32[k])
            t_hi[k] = hi
            t_lo[k] = lo
            return carry

        lax.fori_loop(first, last, body, 0)

    for d in sorted(range(1, n_z), key=lambda d: min(d, n_z - d)):
        block = bfull.at[zs[n_z - d], g]
        arrived(14 + d, block)
        fan(2, n_g, group_peer, lambda _: block, block)
    for i in range(n_chunk):
        loads[i].wait()
        cut(i * per, (i + 1) * per)
    if n_x > 1:
        arrived(1, call.at[pl.ds(0, n_x - 1)])
    call_rows = call[...].reshape(n_x * depth, rank)
    gc[...] = lax.dot_general(call_rows, call_rows, TN, precision=HIGH, preferred_element_type=F32)
    gca[...], gcd[...] = diagonal(gc[...])

    arrived(2, bfull.at[:, pl.ds(0, n_g - 1)])
    rows_b = bfull[...].reshape(width, rank)
    side = rank // 2
    upper = lax.dot_general(rows_b[:, :side], rows_b, TN, precision=HIGH, preferred_element_type=F32)
    corner = lax.dot_general(rows_b[:, side:], rows_b[:, side:], TN, precision=HIGH, preferred_element_type=F32)
    pb[...] = jnp.concatenate([upper[:, :side], upper[:, side:], corner], axis=0).reshape(pb.shape)
    sibling = (ia, ja + 1 - 2 * core, ka)
    across = (z * 2 + 1 - yl, ja + 2 - 4 * yh, ka)
    send(3, pb.at[1 - core], pbc, sibling)
    hi, lo = split2(rows_b)
    bst[...] = jnp.concatenate([hi, lo, hi], axis=0)
    ma[...] = jnp.zeros_like(ma)

    def first_mode(i, carry):
        k0 = i * per
        th = t_hi[pl.ds(k0, per)].reshape(per * height, width)
        tl = t_lo[pl.ds(k0, per)].reshape(per * height, width)
        along = jnp.dot(jnp.concatenate([th, th, tl], axis=1), bst[...], preferred_element_type=F32)
        total = ma[...].reshape(height, rank)
        for j in range(per):
            total = total + along[j * height : (j + 1) * height] * c_ref[pl.ds(k0 + j, 1), :]
        ma[...] = total.reshape(ma.shape)
        return carry

    lax.fori_loop(0, 1, first_mode, 0)
    arrived(3, pbc)
    hs[...] = pb[core] + pbc[...]
    send(4, hs, pby, across)
    lax.fori_loop(1, n_chunk - 1, first_mode, 0)
    arrived(4, pby)
    gb[core] = hs[...] + pby[...]
    send(6, gb.at[core], gb.at[core], sibling)
    lax.fori_loop(n_chunk - 1, n_chunk, first_mode, 0)
    fan(5, n_s, share_peer, lambda where: ma.at[where], ra.at[s])
    ra[s] = ma[s]
    arrived(6, gb.at[0])

    blocks = gb[...].reshape(3 * side, side)
    gram_b = jnp.concatenate(
        [
            jnp.concatenate([blocks[:side], blocks[side : 2 * side]], axis=1),
            jnp.concatenate([blocks[side : 2 * side].T, blocks[2 * side :]], axis=1),
        ],
        axis=0,
    )
    along, down = diagonal(gram_b)
    scl[...] = set_system(sysm, gram_b, (along, 1.0), (down, 1.0), gc[...], gca[...], gcd[...])
    sweep = (sysm, lt, rt, qp, tmp)

    def half_of(h, carry):
        sweep_half(*sweep, h)
        return carry

    sweep_begin(*sweep)
    lax.fori_loop(0, rank // 128, half_of, 0)
    sweep_end(*sweep)
    arrived(5, ra.at[pl.ds(0, n_s - 1)])
    share_a = jnp.sum(ra[...], axis=0)
    raw_a = -jnp.dot(share_a * scl[...], sysm[...], precision=HIGH, preferred_element_type=F32) * scl[...]

    pa[q] = raw_a
    fan(7, n_q, plane_peer, lambda _: pa.at[q], pa.at[q])
    arrived(7, pa.at[pl.ds(0, n_q - 1)])
    rows_a = pa[...].reshape(n_q * 8, rank)
    part = gz.shape[1]
    at2[...] = rows_a.T
    gz[z] = jnp.dot(at2[pl.ds(pl.multiple_of(q * part, part), part), :], rows_a, precision=HIGH, preferred_element_type=F32)
    fan(8, n_z, z_peer, lambda _: gz.at[z], gz.at[z])
    mbt[...] = jnp.zeros_like(mbt)

    at[...] = pa[pl.ds(yl * n_s, n_s)].reshape(height, rank).T

    def second_mode(i, carry):
        k0 = i * per
        hi, lo = zip(*[split2(at[...] * ctb[k0 + j]) for j in range(per)])
        th = t_hi[pl.ds(k0, per)].reshape(per * height, width)
        tl = t_lo[pl.ds(k0, per)].reshape(per * height, width)
        mbt[...] += jnp.dot(
            jnp.concatenate(hi + lo + hi, axis=1), jnp.concatenate([th, th, tl], axis=0), preferred_element_type=F32
        )
        return carry

    lax.fori_loop(0, n_chunk // 2, second_mode, 0)
    arrived(8, gz.at[pl.ds(0, n_z - 1)])
    gs[...] = jnp.sum(gz[...], axis=0)
    fan(9, n_q, plane_peer, lambda _: gs, ga.at[q])
    ga[q] = gs[...]
    lax.fori_loop(n_chunk // 2, n_chunk, second_mode, 0)
    mb[...] = mbt[...].T.reshape(mb.shape)
    fan(10, n_g, group_peer, lambda where: mb.at[:, where], rb1.at[g])
    rb1[g] = mb[:, g]

    arrived(9, ga.at[pl.ds(0, n_q - 1)])
    gram = ga[...].reshape(rank, rank)
    along, down = diagonal(gram)
    weight_a = jnp.sqrt(along * (1.0 / total_a) + epsilon)
    iw[...] = 1.0 / weight_a
    w_a_ref[...] = weight_a
    hat_a_ref[...] = pa[q] / weight_a
    results = [
        pltpu.make_async_copy(have, want, out_sem.at[i])
        for i, (have, want) in enumerate(
            [(hat_a_ref, hat_a_hbm), (w_a_ref, w_a_hbm), (hat_b_ref, hat_b_hbm), (w_b_ref, w_b_hbm)]
        )
    ]
    for result in results[:2]:
        result.start()
    iw_down = 1.0 / jnp.sqrt(down * (1.0 / total_a) + epsilon)
    scl[...] = set_system(sysm, gram, (along, iw[...]), (down, iw_down), gc[...], gca[...], gcd[...])
    sweep_begin(*sweep)

    def pass_sums():
        arrived(10, rb1.at[pl.ds(0, n_g - 1)])
        mb1[...] = jnp.sum(rb1[...], axis=0)
        fan(11, n_z, z_peer, lambda where: mb1.at[where], rb2.at[z])
        rb2[z] = mb1[z]

    def half_with_sums(h, carry):
        sweep_half(*sweep, h, pass_sums)
        return carry

    lax.fori_loop(0, rank // 128, half_with_sums, 0)
    sweep_end(*sweep)
    arrived(11, rb2.at[pl.ds(0, n_z - 1)])
    share_b = jnp.sum(rb2[...], axis=0)
    raw_b = -jnp.dot(share_b * iw[...] * scl[...], sysm[...], precision=HIGH, preferred_element_type=F32) * scl[...]

    sq[...] = jnp.sum(raw_b * raw_b, axis=0, keepdims=True)
    fan(12, n_q, plane_peer, lambda _: sq, sqp.at[q])
    sqp[q] = sq[...]
    arrived(12, sqp.at[pl.ds(0, n_q - 1)])
    sqs[...] = jnp.sum(sqp[...], axis=0)
    fan(13, n_z, z_peer, lambda _: sqs, sqz.at[z])
    sqz[z] = sqs[...]
    arrived(13, sqz.at[pl.ds(0, n_z - 1)])
    weight_b = jnp.sqrt(jnp.sum(sqz[...], axis=0) * (1.0 / total_b) + epsilon)
    w_b_ref[...] = weight_b
    hat_b_ref[...] = raw_b / weight_b
    for result in results[2:]:
        result.start()

    for d in range(1, n_z):
        sent(14 + d, bfull.at[z, g])
    if n_x > 1:
        sent(1, call.at[pl.ds(0, n_x - 1)])
    sent(2, bfull.at[:, pl.ds(0, n_g - 1)])
    sent(3, pbc)
    sent(4, pby)
    sent(5, ra.at[pl.ds(0, n_s - 1)])
    sent(6, gb.at[0])
    sent(7, pa.at[pl.ds(0, n_q - 1)])
    sent(8, gz.at[pl.ds(0, n_z - 1)])
    sent(9, ga.at[pl.ds(0, n_q - 1)])
    sent(10, rb1.at[pl.ds(0, n_g - 1)])
    sent(11, rb2.at[pl.ds(0, n_z - 1)])
    sent(12, sqp.at[pl.ds(0, n_q - 1)])
    sent(13, sqz.at[pl.ds(0, n_z - 1)])
    for result in results:
        result.wait()


def finish(*refs):
    copies = [pltpu.make_async_copy(refs[i], refs[4 + i], refs[8].at[i]) for i in range(4)]
    for copy in copies:
        copy.start()
    for copy in copies:
        copy.wait()


def local(tensor, factor_b, factor_c):
    depth, height, width = tensor.shape
    rank = factor_c.shape[1]
    n_x, n_z = lax.axis_size("ka"), lax.axis_size("ia") // 2
    n_s, n_q, n_g = 4 * n_x, 8 * n_x, 2 * n_x
    part = rank // n_q
    n_chunk = 6
    v = pltpu.VMEM
    out = jax.ShapeDtypeStruct
    hbm = pl.BlockSpec(memory_space=pltpu.HBM)
    results = [out((8, rank), F32), out((1, rank), F32), out((8, rank), F32), out((1, rank), F32)]
    found = pl.pallas_call(
        functools.partial(kernel, n_x, n_z, height * lax.axis_size("ia"), width * lax.axis_size("ja")),
        out_shape=results,
        in_specs=[hbm] * 3,
        out_specs=[hbm] * 4,
        scratch_shapes=[
            v((8, rank), F32),
            v((1, rank), F32),
            v((8, rank), F32),
            v((1, rank), F32),
            v((8, rank), F32),
            v((depth, rank), F32),
            v((depth, height, width), F32),
            v((depth, height, width), BF16),
            v((depth, height, width), BF16),
            v((n_z, n_g, 8, rank), F32),
            v((3 * width, rank), BF16),
            v((n_x, depth, rank), F32),
            v((2, 3 * rank // 4, rank // 2), F32),
            v((3 * rank // 4, rank // 2), F32),
            v((3 * rank // 4, rank // 2), F32),
            v((3 * rank // 4, rank // 2), F32),
            v((2, 3 * rank // 4, rank // 2), F32),
            v((rank, rank), F32),
            v((1, rank), F32),
            v((rank, 1), F32),
            v((n_s, 8, rank), F32),
            v((n_s, 8, rank), F32),
            v((n_q, 8, rank), F32),
            v((rank, n_q * 8), F32),
            v((n_z, part, rank), F32),
            v((part, rank), F32),
            v((n_q, part, rank), F32),
            v((rank, rank), F32),
            v((rank, 6 * NB), BF16),
            v((6 * NB, rank), BF16),
            v((NB, rank), F32),
            v((160, 8, 128), F32),
            v((1, rank), F32),
            v((1, rank), F32),
            v((rank, height), F32),
            v((depth, rank, height), F32),
            v((rank, width), F32),
            v((n_z, n_g, 8, rank), F32),
            v((n_g, n_z, 8, rank), F32),
            v((n_z, 8, rank), F32),
            v((n_z, 8, rank), F32),
            v((1, rank), F32),
            v((n_q, 1, rank), F32),
            v((1, rank), F32),
            v((n_z, 1, rank), F32),
            pltpu.SemaphoreType.DMA((n_chunk + 2,)),
            pltpu.SemaphoreType.DMA((4,)),
            pltpu.SemaphoreType.DMA((14 + n_z,)),
            pltpu.SemaphoreType.DMA((14 + n_z,)),
        ],
        compiler_params=pltpu.CompilerParams(
            collective_id=0, has_side_effects=True, vmem_limit_bytes=VMEM_LIMIT
        ),
    )(tensor, factor_b, factor_c)
    hat_a, weight_a, hat_b, weight_b = pl.pallas_call(
        finish,
        out_shape=results,
        in_specs=[hbm] * 4,
        out_specs=[hbm] * 4,
        scratch_shapes=[pltpu.SemaphoreType.DMA((4,))],
        compiler_params=pltpu.CompilerParams(vmem_limit_bytes=VMEM_LIMIT),
    )(*found)
    return hat_a, weight_a.reshape(rank), hat_b, weight_b.reshape(rank)


def solution(mesh):
    return jax.shard_map(
        local,
        mesh=mesh,
        in_specs=(P("ka", "ia", "ja"), P(("ja", "ia", "ka"), None), P("ka", None)),
        out_specs=(P(("ia", "ja", "ka"), None), P(), P(("ja", "ia", "ka"), None), P()),
        check_vma=False,
    )
```
